512 devices in a mesh: tok: 128 (over z, y, core), head: 4 (over x).
Axes of the slice: x: 4, y: 8, z: 8, core: 2. Of those that a mesh axis runs over, the one named last changes fastest.
Arguments:
- queries: bfloat16 [32768, 3072], P(('tok', 'head')), may hold values from -9 to 9
- key_rows: bfloat16 [32768, 3072], P(('tok', 'head')), may hold values from -13.5 to 13.5
- values: bfloat16 [32768, 3072], P(('tok', 'head')), may hold values from -6 to 6
- cluster: int32 [32768], P('tok'), may hold values from 0 to 511, as said below
- owners: int32 [512], replicated, may hold values from 0 to 511, as said below
- pair_list: int32 [512, 8], P('tok'), may hold values from 0 to 511, as said below
Outputs:
- attended: bfloat16 [32768, 3072], P(('tok', 'head'))
The draws below stay inside these ranges and needn't reach their ends.
Inputs may be any that keep to these rules, and one draw needn't show every extreme that they name: Of the tokens of one tok index (aligned blocks of 256), at most 4 are in clusters whose slot lies on one owner (owners[c] // 4); at most 128 tokens share a cluster; both bounds are reached in every draw. A permutation: cluster c sits in slot owners[c], which is local cluster owners[c] % 4 of tok index owners[c] // 4. `pair_list`: row s starts with s; its other entries are distinct, differ from s, and are slots of tok indices s // 4 - 1 to s // 4 + 1.
All inputs are finite; a program needn't handle non-finite values.
Results may differ from the reference program's by a relative error of at most 0.0026.
Values may be sent and summed in bfloat16 or wider, within the bound.
A program may use at most 64 MiB of HBM per device.

```python
import jax
import jax.numpy as jnp
from jax import lax

HEADS = 24
HEAD_DIM = 128
CL_DEV = 4
PAIRS = 8
CAP = 128
D = 3072
TOK_DEV = 256
TOKENS = 32768
NCL = 512
SEND = 4


def route_plan(key):
    device_count = NCL // CL_DEV
    key_target, key_rotation, key_scores, key_order, key_owner = jax.random.split(key, 5)
    busiest = jax.random.randint(key_target, (), 0, device_count)
    rotation = jax.random.randint(key_rotation, (device_count,), 0, CL_DEV)
    spot_count = device_count * SEND
    spot_index = jnp.arange(spot_count, dtype=jnp.int32)
    noise_int = jax.random.randint(key_scores, (device_count, spot_count), 0, 2 ** 17)
    forced = (spot_index // SEND == busiest).astype(jnp.int32)
    scores = noise_int * spot_count + spot_index[None, :] + forced[None, :] * 2 ** 29
    chosen = lax.top_k(scores, TOK_DEV)[1].astype(jnp.int32)
    order_keys = jax.random.split(key_order, device_count)
    token_order = jax.vmap(lambda single: jax.random.permutation(single, TOK_DEV))(order_keys).astype(jnp.int32)
    spot_token = jnp.take_along_axis(chosen, token_order, axis=1)
    target = spot_token // SEND
    local_id = (spot_token % SEND + rotation[target]) % CL_DEV
    token_slot = (target * CL_DEV + local_id).reshape(-1).astype(jnp.int32)
    owners = jax.random.permutation(key_owner, NCL).astype(jnp.int32)
    inverse = jnp.argsort(owners).astype(jnp.int32)
    cluster = inverse[token_slot]
    return (token_slot, owners, cluster, busiest)


def draw_cluster(key, part):
    plan = route_plan(key)
    return plan[2]


def draw_owners(key, part):
    plan = route_plan(key)
    return plan[1]


def draw_pair_list(key, part):
    key = jax.random.fold_in(key, 3)
    slots = jnp.arange(NCL, dtype=jnp.int32)
    device_of = slots // CL_DEV
    offsets = jnp.arange(3 * CL_DEV, dtype=jnp.int32)
    candidate = (device_of[:, None] - 1) * CL_DEV + offsets[None, :]
    usable = (candidate >= 0) & (candidate < NCL) & (candidate != slots[:, None])
    noise_int = jax.random.randint(key, (NCL, 3 * CL_DEV), 0, 2 ** 20)
    scores = jnp.where(usable, noise_int * (3 * CL_DEV) + offsets[None, :], -1 - offsets[None, :])
    picked = lax.top_k(scores, PAIRS - 1)[1].astype(jnp.int32)
    others = jnp.take_along_axis(candidate, picked, axis=1)
    return jnp.concatenate([slots[:, None], others], axis=1).astype(jnp.int32)


def draw_queries(key, part):
    key = jax.random.fold_in(key, 5)
    base = jax.random.truncated_normal(key, -4.5, 4.5, (TOKENS, D), jnp.float32)
    return base.astype(jnp.bfloat16)


def draw_key_rows(key, part):
    key = jax.random.fold_in(key, 7)
    key_base, key_scale = jax.random.split(key)
    row_scale = jnp.exp(jax.random.uniform(key_scale, (TOKENS, 1), jnp.float32, jnp.log(0.3), jnp.log(3.0)))
    base = jax.random.truncated_normal(key_base, -4.5, 4.5, (TOKENS, D), jnp.float32) * row_scale
    return base.astype(jnp.bfloat16)


def level_of(stream_key, extent, cuts, smallest, high):
    gain, own = 1.0, jax.random.fold_in(stream_key, 6)
    for position, blocks in cuts:
        draws = jnp.exp(jax.random.uniform(jax.random.fold_in(own, position), (blocks,), jnp.float32, smallest / len(cuts), high / len(cuts)))
        gain = gain * jnp.repeat(draws, extent[position] // blocks).reshape([-1 if axis == position else 1 for axis in range(len(extent))])
    return gain


def bell_draw(key, shape, width, most, cuts=(), held_as=jnp.bfloat16):
    drawn = jax.random.normal(key, shape, jnp.float32) * width
    if len(cuts) > 0:
        drawn = level_of(key, shape, cuts, -0.22, 0.18) * drawn
    return jnp.clip(drawn, min=-most, max=most).astype(held_as)


def setup_inputs(seed: int = 0) -> dict:
    splits = jax.random.split(jax.random.key(seed), 7)
    queries = draw_queries(jax.random.fold_in(splits[6], 71), 0)
    key_rows = draw_key_rows(jax.random.fold_in(splits[6], 71), 0)
    values = bell_draw(splits[2], (TOKENS, D), 1.0, 6.0, ((0, 512),))
    cluster = draw_cluster(jax.random.fold_in(splits[6], 71), 0)
    owners = draw_owners(jax.random.fold_in(splits[6], 71), 0)
    pair_list = draw_pair_list(jax.random.fold_in(splits[6], 71), 0)
    return dict(queries=queries, key_rows=key_rows, values=values, cluster=cluster, owners=owners, pair_list=pair_list)


def reference(queries, key_rows, values, cluster, owners, pair_list):
    token_slot = owners[cluster].astype(jnp.int32)
    sort_order = jnp.argsort(token_slot, stable=True).astype(jnp.int32)
    filled = jnp.zeros((NCL,), jnp.int32).at[token_slot].add(1)
    starts = jnp.cumsum(filled) - filled
    sorted_slot = token_slot[sort_order]
    ranks_sorted = jnp.arange(TOKENS, dtype=jnp.int32) - starts[sorted_slot]
    slot_rank = jnp.zeros((TOKENS,), jnp.int32).at[sort_order].set(ranks_sorted)
    slot_row = token_slot * CAP + slot_rank
    slot_live = jnp.zeros((NCL * CAP,), jnp.int32).at[slot_row].set(1).reshape(NCL, CAP)
    score_scale = 1.0 / (HEAD_DIM ** 0.5)

    def one_head(head_index):
        first_col = head_index * HEAD_DIM
        query_head = lax.dynamic_slice_in_dim(queries, first_col, HEAD_DIM, 1)
        key_head = lax.dynamic_slice_in_dim(key_rows, first_col, HEAD_DIM, 1)
        value_head = lax.dynamic_slice_in_dim(values, first_col, HEAD_DIM, 1)
        query_blocks = jnp.zeros((NCL * CAP, HEAD_DIM), jnp.bfloat16).at[slot_row].set(query_head).reshape(NCL, CAP, HEAD_DIM)
        key_blocks = jnp.zeros((NCL * CAP, HEAD_DIM), jnp.bfloat16).at[slot_row].set(key_head).reshape(NCL, CAP, HEAD_DIM)
        value_blocks = jnp.zeros((NCL * CAP, HEAD_DIM), jnp.bfloat16).at[slot_row].set(value_head).reshape(NCL, CAP, HEAD_DIM)

        def one_owner(owner_index):
            first_slot = owner_index * CL_DEV
            query_part = lax.dynamic_slice_in_dim(query_blocks, first_slot, CL_DEV, 0)
            picked = lax.dynamic_slice_in_dim(pair_list, first_slot, CL_DEV, 0)
            key_part = key_blocks[picked].reshape(CL_DEV, PAIRS * CAP, HEAD_DIM)
            value_part = value_blocks[picked].reshape(CL_DEV, PAIRS * CAP, HEAD_DIM)
            key_live = slot_live[picked].reshape(CL_DEV, PAIRS * CAP) > 0
            scores = jnp.einsum("cqd,ckd->cqk", query_part.astype(jnp.float32), key_part.astype(jnp.float32)) * score_scale
            scores = jnp.where(key_live[:, None, :], scores, -1e30)
            row_max = jnp.max(scores, axis=-1, keepdims=True)
            weights = jnp.exp(scores - row_max)
            total = jnp.sum(weights, axis=-1, keepdims=True)
            rounded = weights.astype(jnp.bfloat16)
            mixed_out = jnp.einsum("cqk,ckd->cqd", rounded.astype(jnp.float32), value_part.astype(jnp.float32)) / total
            return mixed_out.astype(jnp.bfloat16)

        blocks = lax.map(one_owner, jnp.arange(NCL // CL_DEV, dtype=jnp.int32))
        flat_rows = blocks.reshape(NCL * CAP, HEAD_DIM)
        return flat_rows[slot_row]

    per_head = lax.map(one_head, jnp.arange(HEADS, dtype=jnp.int32))
    return jnp.transpose(per_head, (1, 0, 2)).reshape(TOKENS, HEADS * HEAD_DIM)
```

```python
import functools
import math

import jax
import jax.numpy as jnp
from jax import lax
from jax.experimental import pallas as pl
from jax.experimental.pallas import tpu as pltpu
from jax.sharding import PartitionSpec as P

HEAD_DIM = 128
CAP = 128
CORES = 2
SWAP = 1
LAG = 2
MASKED = -(2.0**100)
SCALE_LOG2 = math.log2(math.e) / math.sqrt(HEAD_DIM)
MESH = pl.DeviceIdType.MESH
F32 = jnp.float32
BF16 = jnp.bfloat16

X_OWN, X_SEND, X_RECV, A_SEND, A_RECV, B_SEND, B_RECV, H_SEND, H_RECV = range(9)
RB_SEND, RB_RECV, RA_SEND, RA_RECV, RX_SEND, RX_OWN = range(9, 15)
STAGES = 15


def matmul(left, right):
    return jnp.dot(left, right, preferred_element_type=F32)


def matmul_t(left, right):
    return lax.dot_general(left, right, (((1,), (1,)), ((), ())), preferred_element_type=F32)


def iota(shape, dim):
    return lax.broadcasted_iota(jnp.int32, shape, dim)


def one_hot(condition):
    return jnp.where(condition, 1.0, 0.0).astype(BF16)


def wait_bytes(ref, sem):
    pltpu.make_async_copy(ref, ref, sem).wait()


def kernel(
    dims, q_ref, k_ref, v_ref, cluster, owners, pair_list, out_ref,
    x_recv, a_send, a_recv, b_send, b_recv, halo, o_send, o_recv, t_send, t_recv, x_back,
    pick, pick_t, perm, perm_t,
    l_a_send, l_a_recv, l_b_send, l_b_recv, l_halo, mask_in, q_mask, k_mask, mask_tile,
    sem, label_sem, out_sem, mask_sem,
):
    nx, n_axis, per_pair, heads = dims
    tokens = nx * q_ref.shape[0]
    rows = q_ref.shape[0]
    slots = n_axis * n_axis * CORES * per_pair
    width = heads * HEAD_DIM
    line = n_axis * CORES
    a_rows = line * per_pair
    b_rows = n_axis * per_pair
    n_tok = n_axis * line
    pars = 1 + SWAP
    my_x = lax.axis_index("head")
    tok = lax.axis_index("tok")
    z, y, core = tok // line, (tok // CORES) % n_axis, tok % CORES

    def place(par):
        return z + par * (y - z), y + par * (z - y), core + par * (1 - 2 * core)

    def device(a, b, c, par):
        return (
            (a + par * (b - a)) * line + (b + par * (a - b)) * CORES + c + par * (1 - 2 * c),
            my_x,
        )

    def device_of(owner, par):
        return device(owner // line, (owner // CORES) % n_axis, owner % CORES, par)

    def neighbour(par, step):
        a, b, c = place(par)
        owner = (a * n_axis + b) * CORES + c
        return device_of(lax.rem(owner + step + n_tok, n_tok), par)

    def copy_to(src, dst, send, recv, target):
        return pltpu.make_async_remote_copy(
            src_ref=src, dst_ref=dst, send_sem=send, recv_sem=recv,
            device_id=target, device_id_type=MESH,
        )

    def lanes(start, size):
        return pl.ds(pl.multiple_of(start, HEAD_DIM), size)

    def block(index, size):
        return pl.ds(pl.multiple_of(index * size, size), size)

    barrier = pltpu.get_barrier_semaphore()

    def greet(target):
        pl.semaphore_signal(barrier, inc=1, device_id=target, device_id_type=MESH)

    @pl.loop(1, nx)
    def _(d):
        greet((tok, lax.rem(my_x + d, nx)))

    @pl.loop(1, line)
    def _(d):
        greet((z * line + lax.rem(y * CORES + core + d, line), my_x))

    @pl.loop(1, n_axis)
    def _(d):
        other = lax.rem(z + d, n_axis)
        for c in range(CORES):
            greet(((other * n_axis + y) * CORES + c, my_x))

    for par in range(pars):
        greet(neighbour(par, 1))
        greet(neighbour(par, -1))
    greeted = (nx - 1) + (line - 1) + (n_axis - 1) * CORES + 2 * pars
    if SWAP:
        partner = device(z, y, core, 1)
        greet(partner)
        greeted += 1

    def own_copy(ref, kind, h):
        return pltpu.make_async_copy(
            ref.at[:, lanes(my_x * width + h * HEAD_DIM, HEAD_DIM)],
            x_recv.at[h, block(my_x, rows), pl.ds(kind * HEAD_DIM, HEAD_DIM)],
            sem.at[X_OWN, h],
        )

    @pl.loop(0, heads)
    def _(h):
        for kind, ref in enumerate((q_ref, k_ref, v_ref)):
            own_copy(ref, kind, h).start()

    tile = mask_tile.shape[0]
    cl_dev, pairs = pair_list.shape
    pair_local = pair_list[...] - (tok - 1) * cl_dev
    lane = iota((cl_dev, HEAD_DIM), 1)
    allowed = lane > 3 * cl_dev
    for j in range(pairs):
        allowed = allowed | (pair_local[:, j : j + 1] == lane)
    pair_mask = jnp.where(allowed, 0.0, MASKED)
    mask_tile[...] = jnp.concatenate(
        [pair_mask, jnp.zeros((tile - cl_dev, HEAD_DIM), F32)], axis=0
    ).astype(BF16)
    pl.semaphore_wait(barrier, greeted)

    @pl.loop(0, heads)
    def _(h):
        for d in range(1, nx):
            other = lax.rem(my_x + d, nx)
            for kind, ref in enumerate((q_ref, k_ref, v_ref)):
                copy_to(
                    ref.at[:, lanes(other * width + h * HEAD_DIM, HEAD_DIM)],
                    x_recv.at[h, block(my_x, rows), pl.ds(kind * HEAD_DIM, HEAD_DIM)],
                    sem.at[X_SEND, h],
                    sem.at[X_RECV, h],
                    (tok, other),
                ).start()

    if SWAP:
        mask_copy = copy_to(mask_tile, mask_in, mask_sem.at[0], mask_sem.at[1], partner)
        mask_copy.start()

    clusters = owners.shape[1]
    cluster_hot = one_hot(iota((clusters, tokens), 0) == cluster[...])
    table = jnp.where(
        iota((tile, clusters), 0) == 0, owners[...] // cl_dev, owners[...] % cl_dev
    )
    found = matmul(table.astype(F32).astype(BF16), cluster_hot).astype(jnp.int32)
    target, local_id = found[0:1], found[1:2]
    target_hot = one_hot(iota((n_tok, tokens), 0) == target)
    earlier = one_hot(iota((tokens, tokens), 0) < iota((tokens, tokens), 1))
    rank = jnp.sum(matmul(target_hot, earlier) * target_hot.astype(F32), axis=0, keepdims=True)
    pos = target * per_pair + rank.astype(jnp.int32)
    pick[...] = one_hot(iota((slots, tokens), 0) == pos)
    same = one_hot(iota((tokens, tokens), 0) == iota((tokens, tokens), 1))
    pick_t[...] = matmul_t(same, pick[...]).astype(BF16)
    lane = iota((HEAD_DIM, tokens), 0)
    labels = matmul_t(pick[...], one_hot((lane == local_id) | (lane == cl_dev)))
    lane = iota((slots, HEAD_DIM), 1)
    l_a_send[...] = jnp.where(lane == cl_dev, 1.0 - labels, labels).astype(BF16)

    def first_hop(src, dst, send, recv, par):
        a, b, c = place(par)

        @pl.loop(1, n_axis)
        def _(d):
            other = lax.rem(a + d, n_axis)
            copy_to(
                src.at[block(other, a_rows)], dst.at[block(a, a_rows)], send, recv,
                device(other, b, c, par),
            ).start()

    def second_hop(src, dst, send, recv, par):
        a, b, c = place(par)
        here = b * CORES + c

        @pl.loop(1, line)
        def _(d):
            other = lax.rem(here + d, line)
            copy_to(
                src.at[block(other, b_rows)], dst.at[block(here, b_rows)], send, recv,
                device(a, other // CORES, other % CORES, par),
            ).start()

    others_a = pl.ds(0, slots - a_rows)
    others_b = pl.ds(0, slots - b_rows)

    def keep_a(src, dst, par):
        a, _, _ = place(par)
        dst[block(a, a_rows)] = src[block(a, a_rows)]

    def keep_b(src, dst, par):
        _, b, c = place(par)
        dst[block(b * CORES + c, b_rows)] = src[block(b * CORES + c, b_rows)]

    for par in range(pars):
        first_hop(
            l_a_send, l_a_recv.at[par], label_sem.at[0, par], label_sem.at[1, par], par
        )
        keep_a(l_a_send, l_a_recv.at[par], par)

    out_row, in_row = iota((slots, slots), 0), iota((slots, slots), 1)

    def source_of(row):
        r, a, bc = row % per_pair, (row // per_pair) % n_axis, row // b_rows
        return a * a_rows + bc * per_pair + r

    perm[...] = one_hot(source_of(out_row) == in_row)
    perm_t[...] = one_hot(source_of(in_row) == out_row)

    def pack(h):
        par = SWAP * (h % 2)
        for kind, ref in enumerate((q_ref, k_ref, v_ref)):
            own_copy(ref, kind, h).wait()
        wait_bytes(x_recv.at[h, pl.ds(0, tokens - rows)], sem.at[X_RECV, h])
        a_send[h] = matmul(pick[...], x_recv[h]).astype(BF16)
        first_hop(a_send.at[h], a_recv.at[h], sem.at[A_SEND, h], sem.at[A_RECV, h], par)
        keep_a(a_send.at[h], a_recv.at[h], par)

    def turn(h):
        par = SWAP * (h % 2)
        wait_bytes(a_recv.at[h, others_a], sem.at[A_RECV, h])
        b_send[h] = matmul(perm[...], a_recv[h]).astype(BF16)
        second_hop(b_send.at[h], b_recv.at[h], sem.at[B_SEND, h], sem.at[B_RECV, h], par)
        keep_b(b_send.at[h], b_recv.at[h], par)

    def share(h):
        par = SWAP * (h % 2)
        wait_bytes(b_recv.at[h, others_b], sem.at[B_RECV, h])
        for side, step in ((0, 1), (1, -1)):
            copy_to(
                b_recv.at[h, :, pl.ds(HEAD_DIM, 2 * HEAD_DIM)], halo.at[h, side],
                sem.at[H_SEND, h], sem.at[H_RECV, h], neighbour(par, step),
            ).start()

    query_rows = min(256, slots)

    def attend(h):
        par = SWAP * (h % 2)
        wait_bytes(halo.at[h], sem.at[H_RECV, h])

        @pl.loop(0, slots // query_rows)
        def _(step):
            here = block(step, query_rows)
            query = jnp.concatenate(
                [b_recv[h, here, 0:HEAD_DIM], q_mask[par, here]], axis=1
            )
            scores = []
            for part in range(3):
                if part == 1:
                    key = b_recv[h, :, HEAD_DIM : 2 * HEAD_DIM]
                else:
                    key = halo[h, part // 2, :, 0:HEAD_DIM]
                key = jnp.concatenate([key, k_mask[par, part]], axis=1)
                scores.append(matmul_t(query, key))
            row_max = functools.reduce(
                jnp.maximum, [jnp.max(s, axis=1, keepdims=True) for s in scores]
            )
            total, mixed = 0.0, 0.0
            for part in range(3):
                weights = jnp.exp2((scores[part] - row_max) * SCALE_LOG2)
                total = total + jnp.sum(weights, axis=1, keepdims=True)
                if part == 1:
                    value = b_recv[h, :, 2 * HEAD_DIM : 3 * HEAD_DIM]
                else:
                    value = halo[h, part // 2, :, HEAD_DIM : 2 * HEAD_DIM]
                mixed = mixed + matmul(weights.astype(BF16), value)
            o_send[h, here] = (mixed / total).astype(BF16)

        second_hop(o_send.at[h], o_recv.at[h], sem.at[RB_SEND, h], sem.at[RB_RECV, h], par)
        keep_b(o_send.at[h], o_recv.at[h], par)

    def turn_back(h):
        par = SWAP * (h % 2)
        wait_bytes(o_recv.at[h, others_b], sem.at[RB_RECV, h])
        t_send[h] = matmul(perm_t[...], o_recv[h]).astype(BF16)
        first_hop(t_send.at[h], t_recv.at[h], sem.at[RA_SEND, h], sem.at[RA_RECV, h], par)
        keep_a(t_send.at[h], t_recv.at[h], par)

    def finish(h):
        wait_bytes(t_recv.at[h, others_a], sem.at[RA_RECV, h])
        x_back[h] = matmul(pick_t[...], t_recv[h]).astype(BF16)
        column = lanes(my_x * width + h * HEAD_DIM, HEAD_DIM)
        pltpu.make_async_copy(
            x_back.at[h, block(my_x, rows)], out_ref.at[:, column], sem.at[RX_OWN, h]
        ).start()
        for d in range(1, nx):
            other = lax.rem(my_x + d, nx)
            copy_to(
                x_back.at[h, block(other, rows)], out_ref.at[:, column],
                sem.at[RX_SEND, h], out_sem, (tok, other),
            ).start()

    def turn_labels():
        for par in range(pars):
            wait_bytes(l_a_recv.at[par, others_a], label_sem.at[1, par])
            l_b_send[par] = matmul(perm[...], l_a_recv[par]).astype(BF16)
            second_hop(
                l_b_send.at[par], l_b_recv.at[par],
                label_sem.at[2, par], label_sem.at[3, par], par,
            )
            keep_b(l_b_send.at[par], l_b_recv.at[par], par)

    def share_labels():
        for par in range(pars):
            wait_bytes(l_b_recv.at[par, others_b], label_sem.at[3, par])
            for side, step in ((0, 1), (1, -1)):
                copy_to(
                    l_b_recv.at[par], l_halo.at[par, side],
                    label_sem.at[4, par], label_sem.at[5, par], neighbour(par, step),
                ).start()

    def make_masks():
        row, column = iota((HEAD_DIM, HEAD_DIM), 0), iota((HEAD_DIM, HEAD_DIM), 1)
        if SWAP:
            mask_copy.wait()
        for par in range(pars):
            wait_bytes(l_halo.at[par], label_sem.at[5, par])
            mask = (mask_in if par else mask_tile)[...]
            mask = jnp.concatenate([mask, jnp.zeros((HEAD_DIM - tile, HEAD_DIM), BF16)], axis=0)
            q_mask[par] = matmul(l_b_recv[par], mask).astype(BF16)
            for part in range(3):
                shift = one_hot(
                    ((row < cl_dev) & (column == row + cl_dev * part))
                    | ((row == cl_dev) & (column == 3 * cl_dev))
                )
                label = l_b_recv[par] if part == 1 else l_halo[par, part // 2]
                k_mask[par, part] = matmul(label, shift).astype(BF16)

    stages = (pack, turn, share, attend, turn_back, finish)

    @pl.loop(0, heads + LAG * (len(stages) - 1))
    def _(step):
        for number, stage in enumerate(stages):
            lag = LAG * number

            @pl.when((step >= lag) & (step < heads + lag))
            def _():
                stage(step - lag)

        for number, stage in enumerate((turn_labels, share_labels, make_masks)):

            @pl.when(step == number)
            def _():
                stage()

    everyone = out_ref.at[:, pl.ds(0, (nx - 1) * width)]
    wait_bytes(everyone, out_sem)

    @pl.loop(0, heads)
    def _(h):
        wait_bytes(x_recv.at[h, pl.ds(0, tokens - rows)], sem.at[X_SEND, h])
        wait_bytes(a_send.at[h, others_a], sem.at[A_SEND, h])
        wait_bytes(b_send.at[h, others_b], sem.at[B_SEND, h])
        wait_bytes(halo.at[h], sem.at[H_SEND, h])
        wait_bytes(o_send.at[h, others_b], sem.at[RB_SEND, h])
        wait_bytes(t_send.at[h, others_a], sem.at[RA_SEND, h])
        wait_bytes(x_back.at[h, pl.ds(0, tokens - rows)], sem.at[RX_SEND, h])
        wait_bytes(x_back.at[h, pl.ds(0, rows)], sem.at[RX_OWN, h])

    for par in range(pars):
        wait_bytes(l_a_send.at[others_a], label_sem.at[0, par])
        wait_bytes(l_b_send.at[par, others_b], label_sem.at[2, par])
        wait_bytes(l_halo.at[par], label_sem.at[4, par])


def per_device(queries, key_rows, values, cluster, owners, pair_list):
    nx, n_tok = lax.axis_size("head"), lax.axis_size("tok")
    n_axis = math.isqrt(n_tok // CORES)
    cl_dev = pair_list.shape[0]
    per_pair = CAP * cl_dev // n_tok
    rows, features = queries.shape
    heads = features // nx // HEAD_DIM
    tokens = rows * nx
    slots = n_tok * per_pair
    tile = 16

    pars = 1 + SWAP
    wide, thin = 3 * HEAD_DIM, HEAD_DIM

    def vmem(*shape):
        return pltpu.VMEM(shape, BF16)

    return pl.pallas_call(
        functools.partial(kernel, (nx, n_axis, per_pair, heads)),
        out_shape=jax.ShapeDtypeStruct((rows, features), BF16),
        in_specs=[pl.BlockSpec(memory_space=pltpu.HBM)] * 3
        + [pl.BlockSpec(memory_space=pltpu.VMEM)] * 3,
        out_specs=pl.BlockSpec(memory_space=pltpu.HBM),
        scratch_shapes=[
            vmem(heads, tokens, wide),
            vmem(heads, slots, wide),
            vmem(heads, slots, wide),
            vmem(heads, slots, wide),
            vmem(heads, slots, wide),
            vmem(heads, 2, slots, 2 * HEAD_DIM),
            vmem(heads, slots, thin),
            vmem(heads, slots, thin),
            vmem(heads, slots, thin),
            vmem(heads, slots, thin),
            vmem(heads, tokens, thin),
            vmem(slots, tokens),
            vmem(tokens, slots),
            vmem(slots, slots),
            vmem(slots, slots),
            vmem(slots, thin),
            vmem(pars, slots, thin),
            vmem(pars, slots, thin),
            vmem(pars, slots, thin),
            vmem(pars, 2, slots, thin),
            vmem(tile, thin),
            vmem(pars, slots, thin),
            vmem(pars, 3, slots, thin),
            vmem(tile, thin),
            pltpu.SemaphoreType.DMA((STAGES, heads)),
            pltpu.SemaphoreType.DMA((6, pars)),
            pltpu.SemaphoreType.DMA,
            pltpu.SemaphoreType.DMA((2,)),
        ],
        compiler_params=pltpu.CompilerParams(
            collective_id=0, has_side_effects=True, vmem_limit_bytes=60 * 2**20
        ),
    )(queries, key_rows, values, cluster[None, :], owners[None, :], pair_list)


def solution(mesh):
    return jax.shard_map(
        per_device,
        mesh=mesh,
        in_specs=(
            P(("tok", "head"), None),
            P(("tok", "head"), None),
            P(("tok", "head"), None),
            P("tok"),
            P(),
            P("tok", None),
        ),
        out_specs=P(("tok", "head"), None),
        check_vma=False,
    )
```

```python
import functools
import math

import jax
import jax.numpy as jnp
from jax import lax
from jax.experimental import pallas as pl
from jax.experimental.pallas import tpu as pltpu
from jax.sharding import PartitionSpec as P

HEAD_DIM = 128
CAP = 128
CORES = 2
SWAP = 1
MASKED = -(2.0**100)
SCALE_LOG2 = math.log2(math.e) / math.sqrt(HEAD_DIM)
MESH = pl.DeviceIdType.MESH
F32 = jnp.float32
BF16 = jnp.bfloat16

X_OWN, X_SEND, X_RECV, A_SEND, A_RECV, B_SEND, B_RECV, H_SEND, H_RECV = range(9)
RB_SEND, RB_RECV, RA_SEND, RA_RECV, RX_SEND, RX_OWN = range(9, 15)
A_VIA, B_VIA, RB_VIA, RA_VIA, A_ON, B_ON, RB_ON, RA_ON = range(15, 23)
STAGES = 23


def matmul(left, right):
    return jnp.dot(left, right, preferred_element_type=F32)


def matmul_t(left, right):
    return lax.dot_general(left, right, (((1,), (1,)), ((), ())), preferred_element_type=F32)


def iota(shape, dim):
    return lax.broadcasted_iota(jnp.int32, shape, dim)


def one_hot(condition):
    return jnp.where(condition, 1.0, 0.0).astype(BF16)


def wait_bytes(ref, sem):
    pltpu.make_async_copy(ref, ref, sem).wait()


def kernel(
    dims, q_ref, k_ref, v_ref, cluster, owners, pair_list, out_ref,
    x_recv, a_send, a_recv, b_send, b_recv, halo, o_send, o_recv, t_send, t_recv, x_back,
    a_via, b_via, rb_via, ra_via, pick, pick_t, perm, perm_t,
    l_a_send, l_a_recv, l_b_send, l_b_recv, l_halo, mask_in, q_mask, k_mask, mask_tile,
    sem, label_sem, out_sem, mask_sem,
):
    nx, n_axis, per_pair, heads = dims
    tokens = nx * q_ref.shape[0]
    rows = q_ref.shape[0]
    slots = n_axis * n_axis * CORES * per_pair
    width = heads * HEAD_DIM
    line = n_axis * CORES
    a_rows = line * per_pair
    b_rows = n_axis * per_pair
    n_tok = n_axis * line
    pars = 1 + SWAP
    my_x = lax.axis_index("head")
    tok = lax.axis_index("tok")
    z, y, core = tok // line, (tok // CORES) % n_axis, tok % CORES

    def place(par):
        return z + par * (y - z), y + par * (z - y), core + par * (1 - 2 * core)

    def device(a, b, c, par):
        return (
            (a + par * (b - a)) * line + (b + par * (a - b)) * CORES + c + par * (1 - 2 * c),
            my_x,
        )

    def device_of(owner, par):
        return device(owner // line, (owner // CORES) % n_axis, owner % CORES, par)

    def neighbour(par, step):
        a, b, c = place(par)
        owner = (a * n_axis + b) * CORES + c
        return device_of(lax.rem(owner + step + n_tok, n_tok), par)

    def copy_to(src, dst, send, recv, target):
        return pltpu.make_async_remote_copy(
            src_ref=src, dst_ref=dst, send_sem=send, recv_sem=recv,
            device_id=target, device_id_type=MESH,
        )

    def lanes(start, size):
        return pl.ds(pl.multiple_of(start, HEAD_DIM), size)

    def block(index, size):
        return pl.ds(pl.multiple_of(index * size, size), size)

    barrier = pltpu.get_barrier_semaphore()

    def greet(target):
        pl.semaphore_signal(barrier, inc=1, device_id=target, device_id_type=MESH)

    @pl.loop(1, nx)
    def _(d):
        greet((tok, lax.rem(my_x + d, nx)))

    @pl.loop(1, line)
    def _(d):
        greet((z * line + lax.rem(y * CORES + core + d, line), my_x))

    @pl.loop(1, n_axis)
    def _(d):
        other = lax.rem(z + d, n_axis)
        for c in range(CORES):
            greet(((other * n_axis + y) * CORES + c, my_x))

    for par in range(pars):
        greet(neighbour(par, 1))
        greet(neighbour(par, -1))
    greeted = (nx - 1) + (line - 1) + (n_axis - 1) * CORES + 2 * pars
    if SWAP:
        partner = device(z, y, core, 1)
        greet(partner)
        greeted += 1

    def own_copy(ref, kind, h):
        return pltpu.make_async_copy(
            ref.at[:, lanes(my_x * width + h * HEAD_DIM, HEAD_DIM)],
            x_recv.at[h, block(my_x, rows), pl.ds(kind * HEAD_DIM, HEAD_DIM)],
            sem.at[X_OWN, h],
        )

    @pl.loop(0, heads)
    def _(h):
        for kind, ref in enumerate((q_ref, k_ref, v_ref)):
            own_copy(ref, kind, h).start()

    tile = mask_tile.shape[0]
    cl_dev, pairs = pair_list.shape
    pair_local = pair_list[...] - (tok - 1) * cl_dev
    lane = iota((cl_dev, HEAD_DIM), 1)
    allowed = lane > 3 * cl_dev
    for j in range(pairs):
        allowed = allowed | (pair_local[:, j : j + 1] == lane)
    pair_mask = jnp.where(allowed, 0.0, MASKED)
    mask_tile[...] = jnp.concatenate(
        [pair_mask, jnp.zeros((tile - cl_dev, HEAD_DIM), F32)], axis=0
    ).astype(BF16)
    pl.semaphore_wait(barrier, greeted)

    @pl.loop(0, heads)
    def _(h):
        for d in range(1, nx):
            other = lax.rem(my_x + d, nx)
            for kind, ref in enumerate((q_ref, k_ref, v_ref)):
                copy_to(
                    ref.at[:, lanes(other * width + h * HEAD_DIM, HEAD_DIM)],
                    x_recv.at[h, block(my_x, rows), pl.ds(kind * HEAD_DIM, HEAD_DIM)],
                    sem.at[X_SEND, h],
                    sem.at[X_RECV, h],
                    (tok, other),
                ).start()

    if SWAP:
        mask_copy = copy_to(mask_tile, mask_in, mask_sem.at[0], mask_sem.at[1], partner)
        mask_copy.start()

    clusters = owners.shape[1]
    cluster_hot = one_hot(iota((clusters, tokens), 0) == cluster[...])
    table = jnp.where(
        iota((tile, clusters), 0) == 0, owners[...] // cl_dev, owners[...] % cl_dev
    )
    found = matmul(table.astype(F32).astype(BF16), cluster_hot).astype(jnp.int32)
    target, local_id = found[0:1], found[1:2]
    target_hot = one_hot(iota((n_tok, tokens), 0) == target)
    earlier = one_hot(iota((tokens, tokens), 0) < iota((tokens, tokens), 1))
    rank = jnp.sum(matmul(target_hot, earlier) * target_hot.astype(F32), axis=0, keepdims=True)
    pos = target * per_pair + rank.astype(jnp.int32)
    pick[...] = one_hot(iota((slots, tokens), 0) == pos)
    same = one_hot(iota((tokens, tokens), 0) == iota((tokens, tokens), 1))
    pick_t[...] = matmul_t(same, pick[...]).astype(BF16)
    lane = iota((HEAD_DIM, tokens), 0)
    labels = matmul_t(pick[...], one_hot((lane == local_id) | (lane == cl_dev)))
    lane = iota((slots, HEAD_DIM), 1)
    l_a_send[...] = jnp.where(lane == cl_dev, 1.0 - labels, labels).astype(BF16)

    half, quarter = n_axis // 2, n_axis // 4

    def first_hop(src, dst, send, recv, par, via=None, via_recv=None):
        a, b, c = place(par)

        def put(other, target, ref, rows, end):
            copy_to(
                src.at[block(other, a_rows)], ref.at[rows], send, end, device(target, b, c, par)
            ).start()

        opposite = lax.rem(a + half, n_axis)
        if via is None or not quarter:
            put(opposite, opposite, dst, block(a, a_rows), recv)
        else:
            between = lax.rem(a + n_axis + quarter * (1 - 2 * c), n_axis)
            put(opposite, between, via, pl.ds(0, a_rows), via_recv)

        @pl.loop(1, half)
        def _(d):
            for other in (lax.rem(a + d, n_axis), lax.rem(a + n_axis - d, n_axis)):
                put(other, other, dst, block(a, a_rows), recv)

    def first_on(dst, send, recv, par, via, via_recv):
        a, b, c = place(par)
        step = quarter * (1 - 2 * c)
        wait_bytes(via, via_recv)
        origin, target = lax.rem(a + n_axis - step, n_axis), lax.rem(a + n_axis + step, n_axis)
        copy_to(
            via, dst.at[block(origin, a_rows)], send, recv, device(target, b, c, par)
        ).start()

    def second_hop(src, dst, send, recv, par, via=None, via_recv=None):
        a, b, c = place(par)
        here = b * CORES + c

        def put(other, target, ref, rows, end):
            copy_to(
                src.at[block(other, b_rows)], ref.at[rows], send, end,
                device(a, target // CORES, target % CORES, par),
            ).start()

        opposite = lax.rem(b + half, n_axis)
        for end_c in range(CORES):
            other = opposite * CORES + end_c
            if via is None or not quarter:
                put(other, other, dst, block(here, b_rows), recv)
            else:
                between = lax.rem(b + n_axis + quarter * (1 - 2 * end_c), n_axis)
                put(other, between * CORES + end_c, via, block(c, b_rows), via_recv)

        @pl.loop(1, half)
        def _(d):
            for other in (lax.rem(b + d, n_axis), lax.rem(b + n_axis - d, n_axis)):
                for end_c in range(CORES):
                    other_bc = other * CORES + end_c
                    put(other_bc, other_bc, dst, block(here, b_rows), recv)

        near = b * CORES + 1 - c
        put(near, near, dst, block(here, b_rows), recv)

    def second_on(dst, send, recv, par, via, via_recv):
        a, b, c = place(par)
        step = quarter * (1 - 2 * c)
        wait_bytes(via, via_recv)
        origin, target = lax.rem(b + n_axis - step, n_axis), lax.rem(b + n_axis + step, n_axis)
        copy_to(
            via, dst.at[block(origin, CORES * b_rows)], send, recv, device(a, target, c, par)
        ).start()

    others_a = pl.ds(0, slots - a_rows)
    others_b = pl.ds(0, slots - b_rows)

    def keep_a(src, dst, par):
        a, _, _ = place(par)
        dst[block(a, a_rows)] = src[block(a, a_rows)]

    def keep_b(src, dst, par):
        _, b, c = place(par)
        dst[block(b * CORES + c, b_rows)] = src[block(b * CORES + c, b_rows)]

    for par in range(pars):
        first_hop(
            l_a_send, l_a_recv.at[par], label_sem.at[0, par], label_sem.at[1, par], par
        )
        keep_a(l_a_send, l_a_recv.at[par], par)

    out_row, in_row = iota((slots, slots), 0), iota((slots, slots), 1)

    def source_of(row):
        r, a, bc = row % per_pair, (row // per_pair) % n_axis, row // b_rows
        return a * a_rows + bc * per_pair + r

    perm[...] = one_hot(source_of(out_row) == in_row)
    perm_t[...] = one_hot(source_of(in_row) == out_row)

    def pack(h):
        par = SWAP * (h % 2)
        for kind, ref in enumerate((q_ref, k_ref, v_ref)):
            own_copy(ref, kind, h).wait()
        wait_bytes(x_recv.at[h, pl.ds(0, tokens - rows)], sem.at[X_RECV, h])
        a_send[h] = matmul(pick[...], x_recv[h]).astype(BF16)
        first_hop(
            a_send.at[h], a_recv.at[h], sem.at[A_SEND, h], sem.at[A_RECV, h], par,
            a_via.at[h], sem.at[A_VIA, h],
        )
        keep_a(a_send.at[h], a_recv.at[h], par)

    def turn(h):
        par = SWAP * (h % 2)
        wait_bytes(a_recv.at[h, others_a], sem.at[A_RECV, h])
        b_send[h] = matmul(perm[...], a_recv[h]).astype(BF16)
        second_hop(
            b_send.at[h], b_recv.at[h], sem.at[B_SEND, h], sem.at[B_RECV, h], par,
            b_via.at[h], sem.at[B_VIA, h],
        )
        keep_b(b_send.at[h], b_recv.at[h], par)

    def share(h):
        par = SWAP * (h % 2)
        wait_bytes(b_recv.at[h, others_b], sem.at[B_RECV, h])
        for side, step in ((0, 1), (1, -1)):
            copy_to(
                b_recv.at[h, :, pl.ds(HEAD_DIM, 2 * HEAD_DIM)], halo.at[h, side],
                sem.at[H_SEND, h], sem.at[H_RECV, h], neighbour(par, step),
            ).start()

    query_rows = min(256, slots)

    def attend(h):
        par = SWAP * (h % 2)
        wait_bytes(halo.at[h], sem.at[H_RECV, h])

        @pl.loop(0, slots // query_rows)
        def _(step):
            here = block(step, query_rows)
            query = jnp.concatenate(
                [b_recv[h, here, 0:HEAD_DIM], q_mask[par, here]], axis=1
            )
            scores = []
            for part in range(3):
                if part == 1:
                    key = b_recv[h, :, HEAD_DIM : 2 * HEAD_DIM]
                else:
                    key = halo[h, part // 2, :, 0:HEAD_DIM]
                key = jnp.concatenate([key, k_mask[par, part]], axis=1)
                scores.append(matmul_t(query, key))
            row_max = functools.reduce(
                jnp.maximum, [jnp.max(s, axis=1, keepdims=True) for s in scores]
            )
            total, mixed = 0.0, 0.0
            for part in range(3):
                weights = jnp.exp2((scores[part] - row_max) * SCALE_LOG2)
                total = total + jnp.sum(weights, axis=1, keepdims=True)
                if part == 1:
                    value = b_recv[h, :, 2 * HEAD_DIM : 3 * HEAD_DIM]
                else:
                    value = halo[h, part // 2, :, HEAD_DIM : 2 * HEAD_DIM]
                mixed = mixed + matmul(weights.astype(BF16), value)
            o_send[h, here] = (mixed / total).astype(BF16)

        second_hop(
            o_send.at[h], o_recv.at[h], sem.at[RB_SEND, h], sem.at[RB_RECV, h], par,
            rb_via.at[h], sem.at[RB_VIA, h],
        )
        keep_b(o_send.at[h], o_recv.at[h], par)

    def turn_back(h):
        par = SWAP * (h % 2)
        wait_bytes(o_recv.at[h, others_b], sem.at[RB_RECV, h])
        t_send[h] = matmul(perm_t[...], o_recv[h]).astype(BF16)
        first_hop(
            t_send.at[h], t_recv.at[h], sem.at[RA_SEND, h], sem.at[RA_RECV, h], par,
            ra_via.at[h], sem.at[RA_VIA, h],
        )
        keep_a(t_send.at[h], t_recv.at[h], par)

    def finish(h):
        wait_bytes(t_recv.at[h, others_a], sem.at[RA_RECV, h])
        x_back[h] = matmul(pick_t[...], t_recv[h]).astype(BF16)
        column = lanes(my_x * width + h * HEAD_DIM, HEAD_DIM)
        pltpu.make_async_copy(
            x_back.at[h, block(my_x, rows)], out_ref.at[:, column], sem.at[RX_OWN, h]
        ).start()
        for d in range(1, nx):
            other = lax.rem(my_x + d, nx)
            copy_to(
                x_back.at[h, block(other, rows)], out_ref.at[:, column],
                sem.at[RX_SEND, h], out_sem, (tok, other),
            ).start()

    def turn_labels():
        for par in range(pars):
            wait_bytes(l_a_recv.at[par, others_a], label_sem.at[1, par])
            l_b_send[par] = matmul(perm[...], l_a_recv[par]).astype(BF16)
            second_hop(
                l_b_send.at[par], l_b_recv.at[par],
                label_sem.at[2, par], label_sem.at[3, par], par,
            )
            keep_b(l_b_send.at[par], l_b_recv.at[par], par)

    def share_labels():
        for par in range(pars):
            wait_bytes(l_b_recv.at[par, others_b], label_sem.at[3, par])
            for side, step in ((0, 1), (1, -1)):
                copy_to(
                    l_b_recv.at[par], l_halo.at[par, side],
                    label_sem.at[4, par], label_sem.at[5, par], neighbour(par, step),
                ).start()

    def make_masks():
        row, column = iota((HEAD_DIM, HEAD_DIM), 0), iota((HEAD_DIM, HEAD_DIM), 1)
        if SWAP:
            mask_copy.wait()
        for par in range(pars):
            wait_bytes(l_halo.at[par], label_sem.at[5, par])
            mask = (mask_in if par else mask_tile)[...]
            mask = jnp.concatenate([mask, jnp.zeros((HEAD_DIM - tile, HEAD_DIM), BF16)], axis=0)
            q_mask[par] = matmul(l_b_recv[par], mask).astype(BF16)
            for part in range(3):
                shift = one_hot(
                    ((row < cl_dev) & (column == row + cl_dev * part))
                    | ((row == cl_dev) & (column == 3 * cl_dev))
                )
                label = l_b_recv[par] if part == 1 else l_halo[par, part // 2]
                k_mask[par, part] = matmul(label, shift).astype(BF16)

    def relay(on, dst, send, recv, via, via_recv):
        def stage(h):
            on(
                dst.at[h], sem.at[send, h], sem.at[recv, h], SWAP * (h % 2),
                via.at[h], sem.at[via_recv, h],
            )

        return stage

    relays = (
        (first_on, a_recv, A_ON, A_RECV, a_via, A_VIA),
        (second_on, b_recv, B_ON, B_RECV, b_via, B_VIA),
        (second_on, o_recv, RB_ON, RB_RECV, rb_via, RB_VIA),
        (first_on, t_recv, RA_ON, RA_RECV, ra_via, RA_VIA),
    )
    stages = [(0, pack), (2, turn), (4, share), (6, attend), (8, turn_back), (10, finish)]
    if quarter:
        stages += [(lag, relay(*r)) for lag, r in zip((1, 3, 7, 9), relays)]
    stages.sort(key=lambda entry: entry[0])

    @pl.loop(0, heads + 10)
    def _(step):
        for lag, stage in stages:

            @pl.when((step >= lag) & (step < heads + lag))
            def _():
                stage(step - lag)

        for number, stage in enumerate((turn_labels, share_labels, make_masks)):

            @pl.when(step == number)
            def _():
                stage()

    everyone = out_ref.at[:, pl.ds(0, (nx - 1) * width)]
    wait_bytes(everyone, out_sem)

    @pl.loop(0, heads)
    def _(h):
        wait_bytes(x_recv.at[h, pl.ds(0, tokens - rows)], sem.at[X_SEND, h])
        wait_bytes(a_send.at[h, others_a], sem.at[A_SEND, h])
        wait_bytes(b_send.at[h, others_b], sem.at[B_SEND, h])
        wait_bytes(halo.at[h], sem.at[H_SEND, h])
        wait_bytes(o_send.at[h, others_b], sem.at[RB_SEND, h])
        wait_bytes(t_send.at[h, others_a], sem.at[RA_SEND, h])
        wait_bytes(x_back.at[h, pl.ds(0, tokens - rows)], sem.at[RX_SEND, h])
        wait_bytes(x_back.at[h, pl.ds(0, rows)], sem.at[RX_OWN, h])
        if quarter:
            for _, _, on, _, via, _ in relays:
                wait_bytes(via.at[h], sem.at[on, h])

    for par in range(pars):
        wait_bytes(l_a_send.at[others_a], label_sem.at[0, par])
        wait_bytes(l_b_send.at[par, others_b], label_sem.at[2, par])
        wait_bytes(l_halo.at[par], label_sem.at[4, par])


def per_device(queries, key_rows, values, cluster, owners, pair_list):
    nx, n_tok = lax.axis_size("head"), lax.axis_size("tok")
    n_axis = math.isqrt(n_tok // CORES)
    cl_dev = pair_list.shape[0]
    per_pair = CAP * cl_dev // n_tok
    rows, features = queries.shape
    heads = features // nx // HEAD_DIM
    tokens = rows * nx
    slots, line = n_tok * per_pair, n_axis * CORES
    tile = 16

    pars = 1 + SWAP
    wide, thin = 3 * HEAD_DIM, HEAD_DIM

    def vmem(*shape):
        return pltpu.VMEM(shape, BF16)

    return pl.pallas_call(
        functools.partial(kernel, (nx, n_axis, per_pair, heads)),
        out_shape=jax.ShapeDtypeStruct((rows, features), BF16),
        in_specs=[pl.BlockSpec(memory_space=pltpu.HBM)] * 3
        + [pl.BlockSpec(memory_space=pltpu.VMEM)] * 3,
        out_specs=pl.BlockSpec(memory_space=pltpu.HBM),
        scratch_shapes=[
            vmem(heads, tokens, wide),
            vmem(heads, slots, wide),
            vmem(heads, slots, wide),
            vmem(heads, slots, wide),
            vmem(heads, slots, wide),
            vmem(heads, 2, slots, 2 * HEAD_DIM),
            vmem(heads, slots, thin),
            vmem(heads, slots, thin),
            vmem(heads, slots, thin),
            vmem(heads, slots, thin),
            vmem(heads, tokens, thin),
            vmem(heads, line * per_pair, wide),
            vmem(heads, line * per_pair, wide),
            vmem(heads, line * per_pair, thin),
            vmem(heads, line * per_pair, thin),
            vmem(slots, tokens),
            vmem(tokens, slots),
            vmem(slots, slots),
            vmem(slots, slots),
            vmem(slots, thin),
            vmem(pars, slots, thin),
            vmem(pars, slots, thin),
            vmem(pars, slots, thin),
            vmem(pars, 2, slots, thin),
            vmem(tile, thin),
            vmem(pars, slots, thin),
            vmem(pars, 3, slots, thin),
            vmem(tile, thin),
            pltpu.SemaphoreType.DMA((STAGES, heads)),
            pltpu.SemaphoreType.DMA((6, pars)),
            pltpu.SemaphoreType.DMA,
            pltpu.SemaphoreType.DMA((2,)),
        ],
        compiler_params=pltpu.CompilerParams(
            collective_id=0, has_side_effects=True, vmem_limit_bytes=60 * 2**20
        ),
    )(queries, key_rows, values, cluster[None, :], owners[None, :], pair_list)


def solution(mesh):
    return jax.shard_map(
        per_device,
        mesh=mesh,
        in_specs=(
            P(("tok", "head"), None),
            P(("tok", "head"), None),
            P(("tok", "head"), None),
            P("tok"),
            P(),
            P("tok", None),
        ),
        out_specs=P(("tok", "head"), None),
        check_vma=False,
    )
```

```python
import functools
import math

import jax
import jax.numpy as jnp
from jax import lax
from jax.experimental import pallas as pl
from jax.experimental.pallas import tpu as pltpu
from jax.sharding import PartitionSpec as P

HEAD_DIM = 128
CAP = 128
CORES = 2
SWAP = 1
STARTS = (0, 4, 7, 9, 11, 13)
AHEAD = 2
LANES = 8
MASKED = -(2.0**100)
SCALE_LOG2 = math.log2(math.e) / math.sqrt(HEAD_DIM)
MESH = pl.DeviceIdType.MESH
F32 = jnp.float32
BF16 = jnp.bfloat16

X_OWN, X_SEND, X_RECV, A_SEND, A_RECV, B_SEND, B_RECV, H_SEND, H_RECV = range(9)
RB_SEND, RB_RECV, RA_SEND, RA_RECV, RX_SEND, RX_OWN = range(9, 15)
STAGES = 15


def matmul(left, right):
    return jnp.dot(left, right, preferred_element_type=F32)


def matmul_t(left, right):
    return lax.dot_general(left, right, (((1,), (1,)), ((), ())), preferred_element_type=F32)


def iota(shape, dim):
    return lax.broadcasted_iota(jnp.int32, shape, dim)


def one_hot(condition):
    return jnp.where(condition, 1.0, 0.0).astype(BF16)


def wait_bytes(ref, sem):
    pltpu.make_async_copy(ref, ref, sem).wait()


def kernel(
    dims, q_ref, k_ref, v_ref, cluster, owners, pair_list, out_ref,
    x_recv, a_send, a_recv, b_send, b_recv, halo, o_send, o_recv, t_send, t_recv, x_back,
    pick, pick_t, perm, perm_t,
    l_a_send, l_a_recv, l_b_send, l_b_recv, l_own, l_halo, mask_in, q_mask, k_mask, mask_tile,
    sem, label_sem, out_sem, mask_sem,
):
    nx, n_axis, per_pair, heads = dims
    tokens = nx * q_ref.shape[0]
    rows = q_ref.shape[0]
    slots = n_axis * n_axis * CORES * per_pair
    width = heads * HEAD_DIM
    line = n_axis * CORES
    a_rows = line * per_pair
    b_rows = n_axis * per_pair
    n_tok = n_axis * line
    pars = 1 + SWAP
    my_x = lax.axis_index("head")
    tok = lax.axis_index("tok")
    z, y, core = tok // line, (tok // CORES) % n_axis, tok % CORES

    def place(par):
        return z + par * (y - z), y + par * (z - y), core + par * (1 - 2 * core)

    def device(a, b, c, par):
        return (
            (a + par * (b - a)) * line + (b + par * (a - b)) * CORES + c + par * (1 - 2 * c),
            my_x,
        )

    def device_of(owner, par):
        return device(owner // line, (owner // CORES) % n_axis, owner % CORES, par)

    def neighbour(par, step):
        a, b, c = place(par)
        owner = (a * n_axis + b) * CORES + c
        return device_of(lax.rem(owner + step + n_tok, n_tok), par)

    def copy_to(src, dst, send, recv, target):
        return pltpu.make_async_remote_copy(
            src_ref=src, dst_ref=dst, send_sem=send, recv_sem=recv,
            device_id=target, device_id_type=MESH,
        )

    def lanes(start, size):
        return pl.ds(pl.multiple_of(start, HEAD_DIM), size)

    def block(index, size):
        return pl.ds(pl.multiple_of(index * size, size), size)

    barrier = pltpu.get_barrier_semaphore()

    def greet(target):
        pl.semaphore_signal(barrier, inc=1, device_id=target, device_id_type=MESH)

    @pl.loop(1, nx)
    def _(d):
        greet((tok, lax.rem(my_x + d, nx)))

    @pl.loop(1, line)
    def _(d):
        greet((z * line + lax.rem(y * CORES + core + d, line), my_x))

    @pl.loop(1, n_axis)
    def _(d):
        other = lax.rem(z + d, n_axis)
        for c in range(CORES):
            greet(((other * n_axis + y) * CORES + c, my_x))

    for par in range(pars):
        greet(neighbour(par, 1))
        greet(neighbour(par, -1))
    greeted = (nx - 1) + (line - 1) + (n_axis - 1) * CORES + 2 * pars
    if SWAP:
        partner = device(z, y, core, 1)
        greet(partner)
        greeted += 1

    def own_copy(ref, kind, h):
        return pltpu.make_async_copy(
            ref.at[:, lanes(my_x * width + h * HEAD_DIM, HEAD_DIM)],
            x_recv.at[h, block(my_x, rows), pl.ds(kind * HEAD_DIM, HEAD_DIM)],
            sem.at[X_OWN, h],
        )

    @pl.loop(0, heads)
    def _(h):
        for kind, ref in enumerate((q_ref, k_ref, v_ref)):
            own_copy(ref, kind, h).start()

    tile = mask_tile.shape[0]
    cl_dev, pairs = pair_list.shape
    pair_local = pair_list[...] - (tok - 1) * cl_dev
    lane = iota((cl_dev, HEAD_DIM), 1)
    allowed = lane > 3 * cl_dev
    for j in range(pairs):
        allowed = allowed | (pair_local[:, j : j + 1] == lane)
    pair_mask = jnp.where(allowed, 0.0, MASKED)
    mask_tile[...] = jnp.concatenate(
        [pair_mask, jnp.zeros((tile - cl_dev, HEAD_DIM), F32)], axis=0
    ).astype(BF16)
    pl.semaphore_wait(barrier, greeted)

    def spread(h):
        for d in range(1, nx):
            other = lax.rem(my_x + d, nx)
            for kind, ref in enumerate((q_ref, k_ref, v_ref)):
                copy_to(
                    ref.at[:, lanes(other * width + h * HEAD_DIM, HEAD_DIM)],
                    x_recv.at[h, block(my_x, rows), pl.ds(kind * HEAD_DIM, HEAD_DIM)],
                    sem.at[X_SEND, h],
                    sem.at[X_RECV, h],
                    (tok, other),
                ).start()

    for h in range(min(AHEAD, heads)):
        spread(h)

    if SWAP:
        mask_copy = copy_to(mask_tile, mask_in, mask_sem.at[0], mask_sem.at[1], partner)
        mask_copy.start()

    clusters = owners.shape[1]
    cluster_hot = one_hot(iota((clusters, tokens), 0) == cluster[...])
    table = jnp.where(
        iota((tile, clusters), 0) == 0, owners[...] // cl_dev, owners[...] % cl_dev
    )
    found = matmul(table.astype(F32).astype(BF16), cluster_hot).astype(jnp.int32)
    target, local_id = found[0:1], found[1:2]
    target_hot = one_hot(iota((n_tok, tokens), 0) == target)
    earlier = one_hot(iota((tokens, tokens), 0) < iota((tokens, tokens), 1))
    rank = jnp.sum(matmul(target_hot, earlier) * target_hot.astype(F32), axis=0, keepdims=True)
    pos = target * per_pair + rank.astype(jnp.int32)
    pick[...] = one_hot(iota((slots, tokens), 0) == pos)
    same = one_hot(iota((tokens, tokens), 0) == iota((tokens, tokens), 1))
    pick_t[...] = matmul_t(same, pick[...]).astype(BF16)
    lane = iota((HEAD_DIM, tokens), 0) - rank.astype(jnp.int32) * LANES
    labels = matmul_t(target_hot, one_hot((lane == local_id) | (lane == cl_dev)))
    lane = iota((n_tok, HEAD_DIM), 1)
    l_a_send[...] = jnp.where(lane % LANES == cl_dev, 1.0 - labels, labels).astype(BF16)

    def first_hop(src, dst, send, recv, par, size):
        a, b, c = place(par)

        @pl.loop(1, n_axis)
        def _(d):
            other = lax.rem(a + d, n_axis)
            copy_to(
                src.at[block(other, size)], dst.at[block(a, size)], send, recv,
                device(other, b, c, par),
            ).start()

    def put(src, dst, send, recv, par, size, other):
        a, b, c = place(par)
        copy_to(
            src.at[block(other, size)], dst.at[block(b * CORES + c, size)], send, recv,
            device(a, other // CORES, other % CORES, par),
        ).start()

    def second_hop(src, dst, send, recv, par, size):
        _, b, c = place(par)

        @pl.loop(1, line)
        def _(d):
            put(src, dst, send, recv, par, size, lax.rem(b * CORES + c + d, line))

    def keep_a(src, dst, par, size):
        a, _, _ = place(par)
        dst[block(a, size)] = src[block(a, size)]

    def keep_b(src, dst, par, size):
        _, b, c = place(par)
        dst[block(b * CORES + c, size)] = src[block(b * CORES + c, size)]

    others_a = pl.ds(0, slots - a_rows)
    others_b = pl.ds(0, slots - b_rows)
    label_others_a = pl.ds(0, n_tok - line)
    label_others_b = pl.ds(0, (line - 1) * tile)

    for par in range(pars):
        first_hop(
            l_a_send, l_a_recv.at[par], label_sem.at[0, par], label_sem.at[1, par], par, line
        )
        keep_a(l_a_send, l_a_recv.at[par], par, line)

    out_row, in_row = iota((slots, slots), 0), iota((slots, slots), 1)

    def source_of(row):
        r, a, bc = row % per_pair, (row // per_pair) % n_axis, row // b_rows
        return a * a_rows + bc * per_pair + r

    perm[...] = one_hot(source_of(out_row) == in_row)
    perm_t[...] = one_hot(source_of(in_row) == out_row)

    def pack(h):
        par = SWAP * (h % 2)
        for kind, ref in enumerate((q_ref, k_ref, v_ref)):
            own_copy(ref, kind, h).wait()
        wait_bytes(x_recv.at[h, pl.ds(0, tokens - rows)], sem.at[X_RECV, h])

        @pl.when(h + AHEAD < heads)
        def _():
            spread(h + AHEAD)

        a_send[h] = matmul(pick[...], x_recv[h]).astype(BF16)
        first_hop(a_send.at[h], a_recv.at[h], sem.at[A_SEND, h], sem.at[A_RECV, h], par, a_rows)
        keep_a(a_send.at[h], a_recv.at[h], par, a_rows)

    def turn(h):
        par = SWAP * (h % 2)
        wait_bytes(a_recv.at[h, others_a], sem.at[A_RECV, h])
        b_send[h] = matmul(perm[...], a_recv[h]).astype(BF16)
        second_hop(
            b_send.at[h], b_recv.at[h], sem.at[B_SEND, h], sem.at[B_RECV, h], par, b_rows
        )
        keep_b(b_send.at[h], b_recv.at[h], par, b_rows)

    def share(h):
        par = SWAP * (h % 2)
        wait_bytes(b_recv.at[h, others_b], sem.at[B_RECV, h])
        for side, step in ((0, 1), (1, -1)):
            copy_to(
                b_recv.at[h, :, pl.ds(HEAD_DIM, 2 * HEAD_DIM)], halo.at[h, side],
                sem.at[H_SEND, h], sem.at[H_RECV, h], neighbour(par, step),
            ).start()

    query_rows = min(256, slots)

    def attend(h):
        par = SWAP * (h % 2)
        wait_bytes(halo.at[h], sem.at[H_RECV, h])

        _, b, c = place(par)
        mine = b * CORES + c
        parts, targets = slots // query_rows, query_rows // b_rows

        @pl.loop(0, parts)
        def _(step):
            step = lax.rem(step + mine // targets, parts)
            here = block(step, query_rows)
            query = jnp.concatenate(
                [b_recv[h, here, 0:HEAD_DIM], q_mask[par, here]], axis=1
            )
            scores = []
            for part in range(3):
                if part == 1:
                    key = b_recv[h, :, HEAD_DIM : 2 * HEAD_DIM]
                else:
                    key = halo[h, part // 2, :, 0:HEAD_DIM]
                key = jnp.concatenate([key, k_mask[par, part]], axis=1)
                scores.append(matmul_t(query, key))
            row_max = functools.reduce(
                jnp.maximum, [jnp.max(s, axis=1, keepdims=True) for s in scores]
            )
            total, mixed = 0.0, 0.0
            for part in range(3):
                weights = jnp.exp2((scores[part] - row_max) * SCALE_LOG2)
                total = total + jnp.sum(weights, axis=1, keepdims=True)
                if part == 1:
                    value = b_recv[h, :, 2 * HEAD_DIM : 3 * HEAD_DIM]
                else:
                    value = halo[h, part // 2, :, HEAD_DIM : 2 * HEAD_DIM]
                mixed = mixed + matmul(weights.astype(BF16), value)
            o_send[h, here] = (mixed / total).astype(BF16)

            @pl.loop(0, targets)
            def _(d):
                other = step * targets + lax.rem(mine + d, targets)

                @pl.when(other != mine)
                def _():
                    put(
                        o_send.at[h], o_recv.at[h], sem.at[RB_SEND, h], sem.at[RB_RECV, h],
                        par, b_rows, other,
                    )

        keep_b(o_send.at[h], o_recv.at[h], par, b_rows)

    def turn_back(h):
        par = SWAP * (h % 2)
        wait_bytes(o_recv.at[h, others_b], sem.at[RB_RECV, h])
        t_send[h] = matmul(perm_t[...], o_recv[h]).astype(BF16)
        first_hop(
            t_send.at[h], t_recv.at[h], sem.at[RA_SEND, h], sem.at[RA_RECV, h], par, a_rows
        )
        keep_a(t_send.at[h], t_recv.at[h], par, a_rows)

    def finish(h):
        wait_bytes(t_recv.at[h, others_a], sem.at[RA_RECV, h])
        x_back[h] = matmul(pick_t[...], t_recv[h]).astype(BF16)
        column = lanes(my_x * width + h * HEAD_DIM, HEAD_DIM)
        pltpu.make_async_copy(
            x_back.at[h, block(my_x, rows)], out_ref.at[:, column], sem.at[RX_OWN, h]
        ).start()
        for d in range(1, nx):
            other = lax.rem(my_x + d, nx)
            copy_to(
                x_back.at[h, block(other, rows)], out_ref.at[:, column],
                sem.at[RX_SEND, h], out_sem, (tok, other),
            ).start()

    def turn_labels():
        row, column = iota((line * tile, n_tok), 0), iota((line * tile, n_tok), 1)
        turned = one_hot((row % tile < n_axis) & (column == row % tile * line + row // tile))
        for par in range(pars):
            wait_bytes(l_a_recv.at[par, label_others_a], label_sem.at[1, par])
            l_b_send[par] = matmul(turned, l_a_recv[par]).astype(BF16)
            second_hop(
                l_b_send.at[par], l_b_recv.at[par],
                label_sem.at[2, par], label_sem.at[3, par], par, tile,
            )
            keep_b(l_b_send.at[par], l_b_recv.at[par], par, tile)

    def share_labels():
        row, column = iota((n_tok, line * tile), 0), iota((n_tok, line * tile), 1)
        dense = one_hot(column == row // n_axis * tile + row % n_axis)
        for par in range(pars):
            wait_bytes(l_b_recv.at[par, label_others_b], label_sem.at[3, par])
            l_own[par] = matmul(dense, l_b_recv[par]).astype(BF16)
            for side, step in ((0, 1), (1, -1)):
                copy_to(
                    l_own.at[par], l_halo.at[par, side],
                    label_sem.at[4, par], label_sem.at[5, par], neighbour(par, step),
                ).start()

    def make_masks():
        row, column = iota((HEAD_DIM, HEAD_DIM), 0), iota((HEAD_DIM, HEAD_DIM), 1)
        fold = one_hot((row % LANES == column) & (row < per_pair * LANES))
        owner_row = one_hot(iota((slots, n_tok), 0) // per_pair == iota((slots, n_tok), 1))
        slot_row, slot_lane = iota((slots, HEAD_DIM), 0), iota((slots, HEAD_DIM), 1)
        own_lanes = slot_lane // LANES == slot_row % per_pair

        def label_rows(label):
            spread_rows = jnp.where(own_lanes, matmul(owner_row, label), 0.0).astype(BF16)
            return matmul(spread_rows, fold).astype(BF16)

        if SWAP:
            mask_copy.wait()
        for par in range(pars):
            wait_bytes(l_halo.at[par], label_sem.at[5, par])
            mask = (mask_in if par else mask_tile)[...]
            mask = jnp.concatenate([mask, jnp.zeros((HEAD_DIM - tile, HEAD_DIM), BF16)], axis=0)
            for part in range(3):
                label = label_rows(l_own[par] if part == 1 else l_halo[par, part // 2])
                shift = one_hot(
                    ((row < cl_dev) & (column == row + cl_dev * part))
                    | ((row == cl_dev) & (column == 3 * cl_dev))
                )
                k_mask[par, part] = matmul(label, shift).astype(BF16)
                if part == 1:
                    q_mask[par] = matmul(label, mask).astype(BF16)

    stages = tuple(zip(STARTS, (pack, turn, share, attend, turn_back, finish)))

    @pl.loop(0, heads + STARTS[-1])
    def _(step):
        for lag, stage in stages:

            @pl.when((step >= lag) & (step < heads + lag))
            def _():
                stage(step - lag)

        for number, stage in enumerate((turn_labels, share_labels, make_masks)):

            @pl.when(step == number)
            def _():
                stage()

    everyone = out_ref.at[:, pl.ds(0, (nx - 1) * width)]
    wait_bytes(everyone, out_sem)

    @pl.loop(0, heads)
    def _(h):
        wait_bytes(x_recv.at[h, pl.ds(0, tokens - rows)], sem.at[X_SEND, h])
        wait_bytes(a_send.at[h, others_a], sem.at[A_SEND, h])
        wait_bytes(b_send.at[h, others_b], sem.at[B_SEND, h])
        wait_bytes(halo.at[h], sem.at[H_SEND, h])
        wait_bytes(o_send.at[h, others_b], sem.at[RB_SEND, h])
        wait_bytes(t_send.at[h, others_a], sem.at[RA_SEND, h])
        wait_bytes(x_back.at[h, pl.ds(0, tokens - rows)], sem.at[RX_SEND, h])
        wait_bytes(x_back.at[h, pl.ds(0, rows)], sem.at[RX_OWN, h])

    for par in range(pars):
        wait_bytes(l_a_send.at[label_others_a], label_sem.at[0, par])
        wait_bytes(l_b_send.at[par, label_others_b], label_sem.at[2, par])
        wait_bytes(l_halo.at[par], label_sem.at[4, par])


def per_device(queries, key_rows, values, cluster, owners, pair_list):
    nx, n_tok = lax.axis_size("head"), lax.axis_size("tok")
    n_axis = math.isqrt(n_tok // CORES)
    cl_dev = pair_list.shape[0]
    per_pair = CAP * cl_dev // n_tok
    rows, features = queries.shape
    heads = features // nx // HEAD_DIM
    tokens = rows * nx
    slots, line = n_tok * per_pair, n_axis * CORES
    tile = 16

    pars = 1 + SWAP
    wide, thin = 3 * HEAD_DIM, HEAD_DIM

    def vmem(*shape):
        return pltpu.VMEM(shape, BF16)

    return pl.pallas_call(
        functools.partial(kernel, (nx, n_axis, per_pair, heads)),
        out_shape=jax.ShapeDtypeStruct((rows, features), BF16),
        in_specs=[pl.BlockSpec(memory_space=pltpu.HBM)] * 3
        + [pl.BlockSpec(memory_space=pltpu.VMEM)] * 3,
        out_specs=pl.BlockSpec(memory_space=pltpu.HBM),
        scratch_shapes=[
            vmem(heads, tokens, wide),
            vmem(heads, slots, wide),
            vmem(heads, slots, wide),
            vmem(heads, slots, wide),
            vmem(heads, slots, wide),
            vmem(heads, 2, slots, 2 * HEAD_DIM),
            vmem(heads, slots, thin),
            vmem(heads, slots, thin),
            vmem(heads, slots, thin),
            vmem(heads, slots, thin),
            vmem(heads, tokens, thin),
            vmem(slots, tokens),
            vmem(tokens, slots),
            vmem(slots, slots),
            vmem(slots, slots),
            vmem(n_tok, thin),
            vmem(pars, n_tok, thin),
            vmem(pars, line * tile, thin),
            vmem(pars, line * tile, thin),
            vmem(pars, n_tok, thin),
            vmem(pars, 2, n_tok, thin),
            vmem(tile, thin),
            vmem(pars, slots, thin),
            vmem(pars, 3, slots, thin),
            vmem(tile, thin),
            pltpu.SemaphoreType.DMA((STAGES, heads)),
            pltpu.SemaphoreType.DMA((6, pars)),
            pltpu.SemaphoreType.DMA,
            pltpu.SemaphoreType.DMA((2,)),
        ],
        compiler_params=pltpu.CompilerParams(
            collective_id=0, has_side_effects=True, vmem_limit_bytes=60 * 2**20
        ),
    )(queries, key_rows, values, cluster[None, :], owners[None, :], pair_list)


def solution(mesh):
    return jax.shard_map(
        per_device,
        mesh=mesh,
        in_specs=(
            P(("tok", "head"), None),
            P(("tok", "head"), None),
            P(("tok", "head"), None),
            P("tok"),
            P(),
            P("tok", None),
        ),
        out_specs=P(("tok", "head"), None),
        check_vma=False,
    )
```

```python
import functools
import math

import jax
import jax.numpy as jnp
from jax import lax
from jax.experimental import pallas as pl
from jax.experimental.pallas import tpu as pltpu
from jax.sharding import PartitionSpec as P

HEAD_DIM = 128
CAP = 128
CORES = 2
SWAP = 1
STARTS = (0, 4, 7, 9, 11, 13)
AHEAD = 2
LANES = 8
MASKED = -(2.0**100)
SCALE_LOG2 = math.log2(math.e) / math.sqrt(HEAD_DIM)
MESH = pl.DeviceIdType.MESH
F32 = jnp.float32
BF16 = jnp.bfloat16

X_OWN, X_SEND, X_RECV, A_SEND, A_RECV, B_SEND, B_RECV, H_SEND, H_RECV = range(9)
RB_SEND, RB_RECV, RA_SEND, RA_RECV, RX_SEND, RX_OWN = range(9, 15)
STAGES = 15


def matmul(left, right):
    return jnp.dot(left, right, preferred_element_type=F32)


def matmul_t(left, right):
    return lax.dot_general(left, right, (((1,), (1,)), ((), ())), preferred_element_type=F32)


def iota(shape, dim):
    return lax.broadcasted_iota(jnp.int32, shape, dim)


def one_hot(condition):
    return jnp.where(condition, 1.0, 0.0).astype(BF16)


def wait_bytes(ref, sem):
    pltpu.make_async_copy(ref, ref, sem).wait()


def kernel(
    dims, q_ref, k_ref, v_ref, cluster, owners, pair_list, out_ref,
    x_recv, a_send, a_recv, b_send, b_recv, halo, o_send, o_recv, t_send, t_recv, x_back,
    pick, pick_t, perm, perm_t,
    l_a_send, l_a_recv, l_b_send, l_b_recv, l_own, l_halo, mask_in, q_mask, k_mask, mask_tile,
    sem, label_sem, out_sem, mask_sem,
):
    nx, n_axis, per_pair, heads = dims
    tokens = nx * q_ref.shape[0]
    rows = q_ref.shape[0]
    slots = n_axis * n_axis * CORES * per_pair
    width = heads * HEAD_DIM
    line = n_axis * CORES
    a_rows = line * per_pair
    b_rows = n_axis * per_pair
    n_tok = n_axis * line
    pars = 1 + SWAP
    my_x = lax.axis_index("head")
    tok = lax.axis_index("tok")
    z, y, core = tok // line, (tok // CORES) % n_axis, tok % CORES

    def place(par):
        return z + par * (y - z), y + par * (z - y), core + par * (1 - 2 * core)

    def device(a, b, c, par):
        return (
            (a + par * (b - a)) * line + (b + par * (a - b)) * CORES + c + par * (1 - 2 * c),
            my_x,
        )

    def device_of(owner, par):
        return device(owner // line, (owner // CORES) % n_axis, owner % CORES, par)

    def neighbour(par, step):
        a, b, c = place(par)
        owner = (a * n_axis + b) * CORES + c
        return device_of(lax.rem(owner + step + n_tok, n_tok), par)

    def copy_to(src, dst, send, recv, target):
        return pltpu.make_async_remote_copy(
            src_ref=src, dst_ref=dst, send_sem=send, recv_sem=recv,
            device_id=target, device_id_type=MESH,
        )

    def lanes(start, size):
        return pl.ds(pl.multiple_of(start, HEAD_DIM), size)

    def block(index, size):
        return pl.ds(pl.multiple_of(index * size, size), size)

    barrier = pltpu.get_barrier_semaphore()

    def greet(target):
        pl.semaphore_signal(barrier, inc=1, device_id=target, device_id_type=MESH)

    @pl.loop(1, nx)
    def _(d):
        greet((tok, lax.rem(my_x + d, nx)))

    @pl.loop(1, line)
    def _(d):
        greet((z * line + lax.rem(y * CORES + core + d, line), my_x))

    @pl.loop(1, n_axis)
    def _(d):
        other = lax.rem(z + d, n_axis)
        for c in range(CORES):
            greet(((other * n_axis + y) * CORES + c, my_x))

    for par in range(pars):
        greet(neighbour(par, 1))
        greet(neighbour(par, -1))
    greeted = (nx - 1) + (line - 1) + (n_axis - 1) * CORES + 2 * pars
    if SWAP:
        partner = device(z, y, core, 1)
        greet(partner)
        greeted += 1

    def own_copy(ref, kind, h):
        return pltpu.make_async_copy(
            ref.at[:, lanes(my_x * width + h * HEAD_DIM, HEAD_DIM)],
            x_recv.at[h, block(my_x, rows), pl.ds(kind * HEAD_DIM, HEAD_DIM)],
            sem.at[X_OWN, h],
        )

    @pl.loop(0, heads)
    def _(h):
        for kind, ref in enumerate((q_ref, k_ref, v_ref)):
            own_copy(ref, kind, h).start()

    tile = mask_tile.shape[0]
    cl_dev, pairs = pair_list.shape
    pair_local = pair_list[...] - (tok - 1) * cl_dev
    lane = iota((cl_dev, HEAD_DIM), 1)
    allowed = lane > 3 * cl_dev
    for j in range(pairs):
        allowed = allowed | (pair_local[:, j : j + 1] == lane)
    pair_mask = jnp.where(allowed, 0.0, MASKED)
    mask_tile[...] = jnp.concatenate(
        [pair_mask, jnp.zeros((tile - cl_dev, HEAD_DIM), F32)], axis=0
    ).astype(BF16)
    pl.semaphore_wait(barrier, greeted)

    def spread(h):
        for d in range(1, nx):
            other = lax.rem(my_x + d, nx)
            for kind, ref in enumerate((q_ref, k_ref, v_ref)):
                copy_to(
                    ref.at[:, lanes(other * width + h * HEAD_DIM, HEAD_DIM)],
                    x_recv.at[h, block(my_x, rows), pl.ds(kind * HEAD_DIM, HEAD_DIM)],
                    sem.at[X_SEND, h],
                    sem.at[X_RECV, h],
                    (tok, other),
                ).start()

    for h in range(min(AHEAD, heads)):
        spread(h)

    if SWAP:
        mask_copy = copy_to(mask_tile, mask_in, mask_sem.at[0], mask_sem.at[1], partner)
        mask_copy.start()

    clusters = owners.shape[1]
    cluster_hot = one_hot(iota((clusters, tokens), 0) == cluster[...])
    table = jnp.where(
        iota((tile, clusters), 0) == 0, owners[...] // cl_dev, owners[...] % cl_dev
    )
    found = matmul(table.astype(F32).astype(BF16), cluster_hot).astype(jnp.int32)
    target, local_id = found[0:1], found[1:2]
    target_hot = one_hot(iota((n_tok, tokens), 0) == target)
    earlier = one_hot(iota((tokens, tokens), 0) < iota((tokens, tokens), 1))
    rank = jnp.sum(matmul(target_hot, earlier) * target_hot.astype(F32), axis=0, keepdims=True)
    pos = target * per_pair + rank.astype(jnp.int32)
    pick[...] = one_hot(iota((slots, tokens), 0) == pos)
    same = one_hot(iota((tokens, tokens), 0) == iota((tokens, tokens), 1))
    pick_t[...] = matmul_t(same, pick[...]).astype(BF16)
    lane = iota((HEAD_DIM, tokens), 0) - rank.astype(jnp.int32) * LANES
    labels = matmul_t(target_hot, one_hot((lane == local_id) | (lane == cl_dev)))
    lane = iota((n_tok, HEAD_DIM), 1)
    l_a_send[...] = jnp.where(lane % LANES == cl_dev, 1.0 - labels, labels).astype(BF16)

    half = n_axis // 2

    def both_ways(here):
        far = [lax.rem(here + half, n_axis)]
        for d in range(half - 1, 0, -1):
            far += [lax.rem(here + d, n_axis), lax.rem(here + n_axis - d, n_axis)]
        return far

    def first_hop(src, dst, send, recv, par, size):
        a, b, c = place(par)
        for other in both_ways(a):
            copy_to(
                src.at[block(other, size)], dst.at[block(a, size)], send, recv,
                device(other, b, c, par),
            ).start()

    def put(src, dst, send, recv, par, size, other):
        a, b, c = place(par)
        copy_to(
            src.at[block(other, size)], dst.at[block(b * CORES + c, size)], send, recv,
            device(a, other // CORES, other % CORES, par),
        ).start()

    def second_hop(src, dst, send, recv, par, size):
        _, b, c = place(par)
        for other in both_ways(b):
            for end_c in range(CORES):
                put(src, dst, send, recv, par, size, other * CORES + end_c)
        put(src, dst, send, recv, par, size, b * CORES + 1 - c)

    def keep_a(src, dst, par, size):
        a, _, _ = place(par)
        dst[block(a, size)] = src[block(a, size)]

    def keep_b(src, dst, par, size):
        _, b, c = place(par)
        dst[block(b * CORES + c, size)] = src[block(b * CORES + c, size)]

    others_a = pl.ds(0, slots - a_rows)
    others_b = pl.ds(0, slots - b_rows)
    label_others_a = pl.ds(0, n_tok - line)
    label_others_b = pl.ds(0, (line - 1) * tile)

    for par in range(pars):
        first_hop(
            l_a_send, l_a_recv.at[par], label_sem.at[0, par], label_sem.at[1, par], par, line
        )
        keep_a(l_a_send, l_a_recv.at[par], par, line)

    out_row, in_row = iota((slots, slots), 0), iota((slots, slots), 1)

    def source_of(row):
        r, a, bc = row % per_pair, (row // per_pair) % n_axis, row // b_rows
        return a * a_rows + bc * per_pair + r

    perm[...] = one_hot(source_of(out_row) == in_row)
    perm_t[...] = one_hot(source_of(in_row) == out_row)

    def pack(h):
        par = SWAP * (h % 2)
        for kind, ref in enumerate((q_ref, k_ref, v_ref)):
            own_copy(ref, kind, h).wait()
        wait_bytes(x_recv.at[h, pl.ds(0, tokens - rows)], sem.at[X_RECV, h])

        @pl.when(h + AHEAD < heads)
        def _():
            spread(h + AHEAD)

        a_send[h] = matmul(pick[...], x_recv[h]).astype(BF16)
        first_hop(a_send.at[h], a_recv.at[h], sem.at[A_SEND, h], sem.at[A_RECV, h], par, a_rows)
        keep_a(a_send.at[h], a_recv.at[h], par, a_rows)

    def turn(h):
        par = SWAP * (h % 2)
        wait_bytes(a_recv.at[h, others_a], sem.at[A_RECV, h])
        b_send[h] = matmul(perm[...], a_recv[h]).astype(BF16)
        second_hop(
            b_send.at[h], b_recv.at[h], sem.at[B_SEND, h], sem.at[B_RECV, h], par, b_rows
        )
        keep_b(b_send.at[h], b_recv.at[h], par, b_rows)

    def share(h):
        par = SWAP * (h % 2)
        wait_bytes(b_recv.at[h, others_b], sem.at[B_RECV, h])
        for side, step in ((0, 1), (1, -1)):
            copy_to(
                b_recv.at[h, :, pl.ds(HEAD_DIM, 2 * HEAD_DIM)], halo.at[h, side],
                sem.at[H_SEND, h], sem.at[H_RECV, h], neighbour(par, step),
            ).start()

    query_rows = min(256, slots)

    def attend(h):
        par = SWAP * (h % 2)
        wait_bytes(halo.at[h], sem.at[H_RECV, h])

        @pl.loop(0, slots // query_rows)
        def _(step):
            here = block(step, query_rows)
            query = jnp.concatenate(
                [b_recv[h, here, 0:HEAD_DIM], q_mask[par, here]], axis=1
            )
            scores = []
            for part in range(3):
                if part == 1:
                    key = b_recv[h, :, HEAD_DIM : 2 * HEAD_DIM]
                else:
                    key = halo[h, part // 2, :, 0:HEAD_DIM]
                key = jnp.concatenate([key, k_mask[par, part]], axis=1)
                scores.append(matmul_t(query, key))
            row_max = functools.reduce(
                jnp.maximum, [jnp.max(s, axis=1, keepdims=True) for s in scores]
            )
            total, mixed = 0.0, 0.0
            for part in range(3):
                weights = jnp.exp2((scores[part] - row_max) * SCALE_LOG2)
                total = total + jnp.sum(weights, axis=1, keepdims=True)
                if part == 1:
                    value = b_recv[h, :, 2 * HEAD_DIM : 3 * HEAD_DIM]
                else:
                    value = halo[h, part // 2, :, HEAD_DIM : 2 * HEAD_DIM]
                mixed = mixed + matmul(weights.astype(BF16), value)
            o_send[h, here] = (mixed / total).astype(BF16)

        second_hop(o_send.at[h], o_recv.at[h], sem.at[RB_SEND, h], sem.at[RB_RECV, h], par, b_rows)
        keep_b(o_send.at[h], o_recv.at[h], par, b_rows)

    def turn_back(h):
        par = SWAP * (h % 2)
        wait_bytes(o_recv.at[h, others_b], sem.at[RB_RECV, h])
        t_send[h] = matmul(perm_t[...], o_recv[h]).astype(BF16)
        first_hop(
            t_send.at[h], t_recv.at[h], sem.at[RA_SEND, h], sem.at[RA_RECV, h], par, a_rows
        )
        keep_a(t_send.at[h], t_recv.at[h], par, a_rows)

    def finish(h):
        wait_bytes(t_recv.at[h, others_a], sem.at[RA_RECV, h])
        x_back[h] = matmul(pick_t[...], t_recv[h]).astype(BF16)
        column = lanes(my_x * width + h * HEAD_DIM, HEAD_DIM)
        pltpu.make_async_copy(
            x_back.at[h, block(my_x, rows)], out_ref.at[:, column], sem.at[RX_OWN, h]
        ).start()
        for d in range(1, nx):
            other = lax.rem(my_x + d, nx)
            copy_to(
                x_back.at[h, block(other, rows)], out_ref.at[:, column],
                sem.at[RX_SEND, h], out_sem, (tok, other),
            ).start()

    def turn_labels():
        row, column = iota((line * tile, n_tok), 0), iota((line * tile, n_tok), 1)
        turned = one_hot((row % tile < n_axis) & (column == row % tile * line + row // tile))
        for par in range(pars):
            wait_bytes(l_a_recv.at[par, label_others_a], label_sem.at[1, par])
            l_b_send[par] = matmul(turned, l_a_recv[par]).astype(BF16)
            second_hop(
                l_b_send.at[par], l_b_recv.at[par],
                label_sem.at[2, par], label_sem.at[3, par], par, tile,
            )
            keep_b(l_b_send.at[par], l_b_recv.at[par], par, tile)

    def share_labels():
        row, column = iota((n_tok, line * tile), 0), iota((n_tok, line * tile), 1)
        dense = one_hot(column == row // n_axis * tile + row % n_axis)
        for par in range(pars):
            wait_bytes(l_b_recv.at[par, label_others_b], label_sem.at[3, par])
            l_own[par] = matmul(dense, l_b_recv[par]).astype(BF16)
            for side, step in ((0, 1), (1, -1)):
                copy_to(
                    l_own.at[par], l_halo.at[par, side],
                    label_sem.at[4, par], label_sem.at[5, par], neighbour(par, step),
                ).start()

    def make_masks():
        row, column = iota((HEAD_DIM, HEAD_DIM), 0), iota((HEAD_DIM, HEAD_DIM), 1)
        fold = one_hot((row % LANES == column) & (row < per_pair * LANES))
        owner_row = one_hot(iota((slots, n_tok), 0) // per_pair == iota((slots, n_tok), 1))
        slot_row, slot_lane = iota((slots, HEAD_DIM), 0), iota((slots, HEAD_DIM), 1)
        own_lanes = slot_lane // LANES == slot_row % per_pair

        def label_rows(label):
            spread_rows = jnp.where(own_lanes, matmul(owner_row, label), 0.0).astype(BF16)
            return matmul(spread_rows, fold).astype(BF16)

        if SWAP:
            mask_copy.wait()
        for par in range(pars):
            wait_bytes(l_halo.at[par], label_sem.at[5, par])
            mask = (mask_in if par else mask_tile)[...]
            mask = jnp.concatenate([mask, jnp.zeros((HEAD_DIM - tile, HEAD_DIM), BF16)], axis=0)
            for part in range(3):
                label = label_rows(l_own[par] if part == 1 else l_halo[par, part // 2])
                shift = one_hot(
                    ((row < cl_dev) & (column == row + cl_dev * part))
                    | ((row == cl_dev) & (column == 3 * cl_dev))
                )
                k_mask[par, part] = matmul(label, shift).astype(BF16)
                if part == 1:
                    q_mask[par] = matmul(label, mask).astype(BF16)

    stages = tuple(zip(STARTS, (pack, turn, share, attend, turn_back, finish)))

    @pl.loop(0, heads + STARTS[-1])
    def _(step):
        for lag, stage in stages:

            @pl.when((step >= lag) & (step < heads + lag))
            def _():
                stage(step - lag)

        for number, stage in enumerate((turn_labels, share_labels, make_masks)):

            @pl.when(step == number)
            def _():
                stage()

    everyone = out_ref.at[:, pl.ds(0, (nx - 1) * width)]
    wait_bytes(everyone, out_sem)

    @pl.loop(0, heads)
    def _(h):
        wait_bytes(x_recv.at[h, pl.ds(0, tokens - rows)], sem.at[X_SEND, h])
        wait_bytes(a_send.at[h, others_a], sem.at[A_SEND, h])
        wait_bytes(b_send.at[h, others_b], sem.at[B_SEND, h])
        wait_bytes(halo.at[h], sem.at[H_SEND, h])
        wait_bytes(o_send.at[h, others_b], sem.at[RB_SEND, h])
        wait_bytes(t_send.at[h, others_a], sem.at[RA_SEND, h])
        wait_bytes(x_back.at[h, pl.ds(0, tokens - rows)], sem.at[RX_SEND, h])
        wait_bytes(x_back.at[h, pl.ds(0, rows)], sem.at[RX_OWN, h])

    for par in range(pars):
        wait_bytes(l_a_send.at[label_others_a], label_sem.at[0, par])
        wait_bytes(l_b_send.at[par, label_others_b], label_sem.at[2, par])
        wait_bytes(l_halo.at[par], label_sem.at[4, par])


def per_device(queries, key_rows, values, cluster, owners, pair_list):
    nx, n_tok = lax.axis_size("head"), lax.axis_size("tok")
    n_axis = math.isqrt(n_tok // CORES)
    cl_dev = pair_list.shape[0]
    per_pair = CAP * cl_dev // n_tok
    rows, features = queries.shape
    heads = features // nx // HEAD_DIM
    tokens = rows * nx
    slots, line = n_tok * per_pair, n_axis * CORES
    tile = 16

    pars = 1 + SWAP
    wide, thin = 3 * HEAD_DIM, HEAD_DIM

    def vmem(*shape):
        return pltpu.VMEM(shape, BF16)

    return pl.pallas_call(
        functools.partial(kernel, (nx, n_axis, per_pair, heads)),
        out_shape=jax.ShapeDtypeStruct((rows, features), BF16),
        in_specs=[pl.BlockSpec(memory_space=pltpu.HBM)] * 3
        + [pl.BlockSpec(memory_space=pltpu.VMEM)] * 3,
        out_specs=pl.BlockSpec(memory_space=pltpu.HBM),
        scratch_shapes=[
            vmem(heads, tokens, wide),
            vmem(heads, slots, wide),
            vmem(heads, slots, wide),
            vmem(heads, slots, wide),
            vmem(heads, slots, wide),
            vmem(heads, 2, slots, 2 * HEAD_DIM),
            vmem(heads, slots, thin),
            vmem(heads, slots, thin),
            vmem(heads, slots, thin),
            vmem(heads, slots, thin),
            vmem(heads, tokens, thin),
            vmem(slots, tokens),
            vmem(tokens, slots),
            vmem(slots, slots),
            vmem(slots, slots),
            vmem(n_tok, thin),
            vmem(pars, n_tok, thin),
            vmem(pars, line * tile, thin),
            vmem(pars, line * tile, thin),
            vmem(pars, n_tok, thin),
            vmem(pars, 2, n_tok, thin),
            vmem(tile, thin),
            vmem(pars, slots, thin),
            vmem(pars, 3, slots, thin),
            vmem(tile, thin),
            pltpu.SemaphoreType.DMA((STAGES, heads)),
            pltpu.SemaphoreType.DMA((6, pars)),
            pltpu.SemaphoreType.DMA,
            pltpu.SemaphoreType.DMA((2,)),
        ],
        compiler_params=pltpu.CompilerParams(
            collective_id=0, has_side_effects=True, vmem_limit_bytes=60 * 2**20
        ),
    )(queries, key_rows, values, cluster[None, :], owners[None, :], pair_list)


def solution(mesh):
    return jax.shard_map(
        per_device,
        mesh=mesh,
        in_specs=(
            P(("tok", "head"), None),
            P(("tok", "head"), None),
            P(("tok", "head"), None),
            P("tok"),
            P(),
            P("tok", None),
        ),
        out_specs=P(("tok", "head"), None),
        check_vma=False,
    )
```

```python
import functools
import math

import jax
import jax.numpy as jnp
from jax import lax
from jax.experimental import pallas as pl
from jax.experimental.pallas import tpu as pltpu
from jax.sharding import PartitionSpec as P

HEAD_DIM = 128
CAP = 128
CORES = 2
TILE = 16
LANES = 8
AHEAD = 2
STEP = 1
MASKED = -(2.0**100)
SCALE_LOG2 = math.log2(math.e) / math.sqrt(HEAD_DIM)
MESH = pl.DeviceIdType.MESH
F32 = jnp.float32
BF16 = jnp.bfloat16

X_OWN, X_SEND, X_RECV, A_SEND, A_RECV, B_SEND, B_NEAR, B_RECV, H_SEND, H_RECV = range(10)
RB_SEND, RB_RECV, RA_SEND, RA_RECV, RX_SEND, RX_OWN = range(10, 16)
STAGES = 16


def matmul(left, right):
    return jnp.dot(left, right, preferred_element_type=F32)


def matmul_t(left, right):
    return lax.dot_general(left, right, (((1,), (1,)), ((), ())), preferred_element_type=F32)


def iota(shape, dim):
    return lax.broadcasted_iota(jnp.int32, shape, dim)


def one_hot(condition):
    return jnp.where(condition, 1.0, 0.0).astype(BF16)


def wait_bytes(ref, sem):
    pltpu.make_async_copy(ref, ref, sem).wait()


def kernel(
    dims, q_ref, k_ref, v_ref, cluster, owners, pair_list, out_ref,
    x_recv, a_send, a_recv, b_send, work, o_send, o_recv, t_send, t_recv, x_back,
    pick, pick_t, perm, perm_t, scores, peak, total, mixed,
    l_a_send, l_a_recv, l_b_send, l_b_recv, labels, mask_tile, mask_in, q_mask, k_mask,
    sem, label_sem, mask_sem, out_sem,
):
    nx, n_axis, per_pair, heads = dims
    rows = q_ref.shape[0]
    tokens = nx * rows
    width = heads * HEAD_DIM
    line = n_axis * CORES
    n_tok = n_axis * line
    slots = n_tok * per_pair
    a_rows = line * per_pair
    b_rows = n_axis * per_pair
    mine = heads // CORES
    sides = CORES + 2
    cl_dev, pairs = pair_list.shape
    invalid = sides * cl_dev
    my_x = lax.axis_index("head")
    tok = lax.axis_index("tok")
    z, y, core = tok // line, (tok // CORES) % n_axis, tok % CORES

    def place(par):
        return z + par * (y - z), y + par * (z - y)

    def device(a, b, c, par):
        return ((a + par * (b - a)) * line + (b + par * (a - b)) * CORES + c, my_x)

    def next_chip(step):
        a, b = place(core)
        chip = lax.rem(a * n_axis + b + n_axis * n_axis + step, n_axis * n_axis)
        return device(chip // n_axis, chip % n_axis, core, core)

    def copy_to(src, dst, send, recv, target):
        pltpu.make_async_remote_copy(
            src_ref=src, dst_ref=dst, send_sem=send, recv_sem=recv,
            device_id=target, device_id_type=MESH,
        ).start()

    def lanes(start, size):
        return pl.ds(pl.multiple_of(start, HEAD_DIM), size)

    def block(index, size):
        return pl.ds(pl.multiple_of(index * size, size), size)

    barrier = pltpu.get_barrier_semaphore()

    def greet(target):
        pl.semaphore_signal(barrier, inc=1, device_id=target, device_id_type=MESH)

    @pl.loop(1, nx)
    def _(d):
        greet((tok, lax.rem(my_x + d, nx)))

    @pl.loop(1, line)
    def _(d):
        greet((z * line + lax.rem(y * CORES + core + d, line), my_x))

    @pl.loop(1, n_axis)
    def _(d):
        for c in range(CORES):
            greet(((lax.rem(z + d, n_axis) * n_axis + y) * CORES + c, my_x))

    greet(next_chip(1))
    greet(next_chip(-1))
    @pl.when(y != z)
    def _():
        for c in range(CORES):
            greet(((y * n_axis + z) * CORES + c, my_x))

    @pl.when(y == z)
    def _():
        for c in range(CORES):
            greet((tok + 1 - 2 * core, my_x))

    greeted = (nx - 1) + (line - 1) + (n_axis - 1) * CORES + 2 + CORES

    def own_copy(ref, kind, h):
        return pltpu.make_async_copy(
            ref.at[:, lanes(my_x * width + h * HEAD_DIM, HEAD_DIM)],
            x_recv.at[h, block(my_x, rows), pl.ds(kind * HEAD_DIM, HEAD_DIM)],
            sem.at[X_OWN, h],
        )

    @pl.loop(0, heads)
    def _(h):
        for kind, ref in enumerate((q_ref, k_ref, v_ref)):
            own_copy(ref, kind, h).start()

    pair_local = pair_list[...] - (tok - core - 1) * cl_dev
    lane = iota((cl_dev, HEAD_DIM), 1)
    allowed = lane > invalid
    for j in range(pairs):
        allowed = allowed | (pair_local[:, j : j + 1] == lane)
    mask_tile[...] = jnp.concatenate(
        [jnp.where(allowed, 0.0, MASKED), jnp.zeros((TILE - cl_dev, HEAD_DIM), F32)], axis=0
    ).astype(BF16)

    pl.semaphore_wait(barrier, greeted)

    def spread(h):
        @pl.loop(1, nx)
        def _(d):
            other = lax.rem(my_x + d, nx)
            for kind, ref in enumerate((q_ref, k_ref, v_ref)):
                copy_to(
                    ref.at[:, lanes(other * width + h * HEAD_DIM, HEAD_DIM)],
                    x_recv.at[h, block(my_x, rows), pl.ds(kind * HEAD_DIM, HEAD_DIM)],
                    sem.at[X_SEND, h],
                    sem.at[X_RECV, h],
                    (tok, other),
                )

    @pl.loop(0, min(AHEAD, heads))
    def _(h):
        spread(h)

    keepers = [(z * n_axis + y) * CORES, (y * n_axis + z) * CORES + 1]
    for end, keeper in enumerate(keepers):

        @pl.when(tok == keeper)
        def _():
            pltpu.make_async_copy(
                mask_tile, mask_in.at[core], mask_sem.at[CORES + core]
            ).start()

        @pl.when(tok != keeper)
        def _():
            copy_to(
                mask_tile, mask_in.at[core], mask_sem.at[end], mask_sem.at[CORES + core],
                (keeper, my_x),
            )

    clusters = owners.shape[1]
    cluster_hot = one_hot(iota((clusters, tokens), 0) == cluster[...])
    table = jnp.where(
        iota((TILE, clusters), 0) == 0, owners[...] // cl_dev, owners[...] % cl_dev
    )
    found = matmul(table.astype(F32).astype(BF16), cluster_hot).astype(jnp.int32)
    target, local_id = found[0:1], found[1:2]
    target_hot = one_hot(iota((n_tok, tokens), 0) == target)
    earlier = one_hot(iota((tokens, tokens), 0) < iota((tokens, tokens), 1))
    rank = jnp.sum(matmul(target_hot, earlier) * target_hot.astype(F32), axis=0, keepdims=True)
    rank = rank.astype(jnp.int32)
    send_row = target * per_pair + rank
    chunk = min(128, tokens)

    @pl.loop(0, slots // chunk)
    def _(i):
        pick[block(i, chunk)] = one_hot(iota((chunk, tokens), 0) + i * chunk == send_row)

    lane = iota((HEAD_DIM, tokens), 0) - rank * LANES
    filled = matmul_t(target_hot, one_hot((lane == local_id) | (lane == cl_dev)))
    lane = iota((n_tok, HEAD_DIM), 1)
    l_a_send[...] = jnp.where(lane % LANES == cl_dev, 1.0 - filled, filled).astype(BF16)

    def first_hop(src, dst, send, recv, par, size):
        a, b = place(par)
        pltpu.make_async_copy(src.at[block(a, size)], dst.at[block(a, size)], recv).start()

        @pl.loop(1, n_axis)
        def _(d):
            other = lax.rem(a + d, n_axis)
            copy_to(
                src.at[block(other, size)], dst.at[block(a, size)], send, recv,
                device(other, b, core, par),
            )

    def second_hop(src_at, dst, send, near, recv, par):
        a, b = place(par)

        @pl.when(core == par)
        def _():
            pltpu.make_async_copy(src_at(b), dst, recv).start()

        @pl.when(core != par)
        def _():
            copy_to(src_at(b), dst, near, recv, device(a, b, par, par))

        @pl.loop(1, n_axis)
        def _(d):
            other = lax.rem(b + d, n_axis)
            copy_to(src_at(other), dst, send, recv, device(a, other, par, par))

    def source(par):
        _, b = place(par)
        return b * CORES + core

    others_a = pl.ds(0, slots - a_rows)
    others_b = pl.ds(0, b_rows * (n_axis - 1))
    label_others = pl.ds(0, n_tok - line)

    for par in range(CORES):
        first_hop(
            l_a_send, l_a_recv.at[par], label_sem.at[0, par], label_sem.at[1, par], par, line
        )

    def pack(h):
        for kind, ref in enumerate((q_ref, k_ref, v_ref)):
            own_copy(ref, kind, h).wait()
        wait_bytes(x_recv.at[h, pl.ds(0, tokens - rows)], sem.at[X_RECV, h])

        @pl.when(h + AHEAD < heads)
        def _():
            spread(h + AHEAD)

        @pl.loop(0, 2)
        def _(i):
            part = block(i, slots // 2)
            a_send[h, part] = matmul(pick[part], x_recv[h]).astype(BF16)

        first_hop(a_send.at[h], a_recv.at[h], sem.at[A_SEND, h], sem.at[A_RECV, h], h % 2, a_rows)

    def turn(h):
        par = h % 2
        wait_bytes(a_recv.at[h], sem.at[A_RECV, h])

        @pl.loop(0, CORES)
        def _(i):
            b_send[h, i] = matmul(perm[i], a_recv[h]).astype(BF16)

        second_hop(
            lambda other: b_send.at[h, :, block(other, b_rows)],
            work.at[h // 2, pl.ds(1, CORES), block(source(par), b_rows)],
            sem.at[B_SEND, h], sem.at[B_NEAR, h], sem.at[B_RECV, h // 2], par,
        )

    def share(k):
        wait_bytes(work.at[k, pl.ds(1, CORES)], sem.at[B_RECV, k])
        for step, src, dst in ((-1, 1, CORES + 1), (1, CORES, 0)):
            copy_to(
                work.at[k, src, :, pl.ds(HEAD_DIM, 2 * HEAD_DIM)],
                work.at[k, dst, :, pl.ds(HEAD_DIM, 2 * HEAD_DIM)],
                sem.at[H_SEND, k], sem.at[H_RECV, k], next_chip(step),
            )

    two_sides = (pl.ds(0, 2), slice(None), pl.ds(HEAD_DIM, 2 * HEAD_DIM))
    tiles = slots // HEAD_DIM if slots >= HEAD_DIM else 1
    lane_step = min(slots, HEAD_DIM)

    def attend(k):
        wait_bytes(work.at[(k, *two_sides)], sem.at[H_RECV, k])

        @pl.loop(0, CORES)
        def _(i):
            peak[...] = jnp.full((slots, lane_step), -jnp.inf, F32)

            @pl.loop(0, 3)
            def _(part):
                query = jnp.concatenate([work[k, i + 1, :, 0:HEAD_DIM], q_mask[i]], axis=1)
                key = jnp.concatenate(
                    [work[k, i + part, :, HEAD_DIM : 2 * HEAD_DIM], k_mask[i + part]], axis=1
                )
                found = matmul_t(query, key)
                scores[part] = found
                peak[...] = functools.reduce(
                    jnp.maximum,
                    [found[:, t * lane_step : (t + 1) * lane_step] for t in range(tiles)],
                    peak[...],
                )

            row_max = jnp.max(peak[...], axis=1, keepdims=True)
            peak[...] = jnp.broadcast_to(row_max, (slots, lane_step))
            total[...] = jnp.zeros((slots, lane_step), F32)
            mixed[...] = jnp.zeros((slots, HEAD_DIM), F32)

            @pl.loop(0, 3)
            def _(part):
                row_max = peak[...]
                weights = [
                    jnp.exp2(
                        (scores[part, :, t * lane_step : (t + 1) * lane_step] - row_max)
                        * SCALE_LOG2
                    )
                    for t in range(tiles)
                ]
                total[...] += functools.reduce(jnp.add, weights)
                rounded = jnp.concatenate([w.astype(BF16) for w in weights], axis=1)
                mixed[...] += matmul(rounded, work[k, i + part, :, 2 * HEAD_DIM : 3 * HEAD_DIM])

            row_total = jnp.sum(total[...], axis=1, keepdims=True)
            o_send[k, i] = (mixed[...] / row_total).astype(BF16)

        h = CORES * k + core
        a, b = place(core)
        here = b * CORES + core
        dst = o_recv.at[h, :, block(b, b_rows)]

        def src(other):
            return o_send.at[k, :, block(other, b_rows)]

        pltpu.make_async_copy(src(here), dst, sem.at[RB_RECV, h]).start()

        @pl.loop(1, line)
        def _(d):
            other = lax.rem(here + d, line)
            copy_to(
                src(other), dst, sem.at[RB_SEND, k], sem.at[RB_RECV, h],
                device(a, other // CORES, other % CORES, core),
            )

    def turn_back(h):
        wait_bytes(o_recv.at[h], sem.at[RB_RECV, h])
        t_send[h] = matmul(perm_t[...], o_recv[h].reshape(slots, HEAD_DIM)).astype(BF16)
        first_hop(
            t_send.at[h], t_recv.at[h], sem.at[RA_SEND, h], sem.at[RA_RECV, h], h % 2, a_rows
        )

    def finish(h):
        wait_bytes(t_recv.at[h], sem.at[RA_RECV, h])
        x_back[h] = matmul(pick_t[...], t_recv[h]).astype(BF16)
        column = lanes(my_x * width + h * HEAD_DIM, HEAD_DIM)
        pltpu.make_async_copy(
            x_back.at[h, block(my_x, rows)], out_ref.at[:, column], sem.at[RX_OWN, h]
        ).start()

        @pl.loop(1, nx)
        def _(d):
            other = lax.rem(my_x + d, nx)
            copy_to(
                x_back.at[h, block(other, rows)], out_ref.at[:, column],
                sem.at[RX_SEND, h], out_sem, (tok, other),
            )

    def make_perms():
        half = slots // CORES

        def source_of(row, i):
            r, a, b = row % per_pair, (row // per_pair) % n_axis, row // b_rows
            return a * a_rows + b * (CORES * per_pair) + i * per_pair + r

        for i in range(CORES):
            perm[i] = one_hot(source_of(iota((half, slots), 0), i) == iota((half, slots), 1))

        @pl.loop(0, slots // chunk)
        def _(part):
            row, column = iota((chunk, slots), 0) + part * chunk, iota((chunk, slots), 1)
            perm_t[block(part, chunk)] = one_hot(
                source_of(column % half, column // half) == row
            )

        same = one_hot(iota((tokens, tokens), 0) == iota((tokens, tokens), 1))
        pick_t[...] = matmul_t(same, pick[...]).astype(BF16)

    def turn_labels():
        row, column = iota((n_tok, n_tok), 0), iota((n_tok, n_tok), 1)
        start = (row // CORES) % n_axis * line + row // line * CORES + row % CORES
        turned = one_hot(start == column)
        for par in range(CORES):
            wait_bytes(l_a_recv.at[par], label_sem.at[1, par])
            l_b_send[par] = matmul(turned, l_a_recv[par]).astype(BF16)
            second_hop(
                lambda other: l_b_send.at[par, block(other, line)],
                l_b_recv.at[block(source(par), line)],
                label_sem.at[2, par], label_sem.at[3, par], label_sem.at[4, 0], par,
            )

    def share_labels():
        wait_bytes(l_b_recv, label_sem.at[4, 0])
        shape = (n_tok, line * line)
        row, column = iota(shape, 0), iota(shape, 1)
        start = row // n_axis * line + row % n_axis * CORES
        for i in range(CORES):
            labels[i + 1] = matmul(one_hot(start + i == column), l_b_recv[...]).astype(BF16)
        for step, src, dst in ((-1, 1, CORES + 1), (1, CORES, 0)):
            copy_to(
                labels.at[src], labels.at[dst], label_sem.at[5, 0], label_sem.at[5, 1],
                next_chip(step),
            )

    def make_masks():
        wait_bytes(labels.at[pl.ds(0, 2)], label_sem.at[5, 1])
        for c in range(CORES):
            wait_bytes(mask_in.at[c], mask_sem.at[CORES + c])
        row, column = iota((HEAD_DIM, HEAD_DIM), 0), iota((HEAD_DIM, HEAD_DIM), 1)
        fold = one_hot((row % LANES == column) & (row < per_pair * LANES))
        owner_row = one_hot(iota((slots, n_tok), 0) // per_pair == iota((slots, n_tok), 1))
        shape = (slots, HEAD_DIM)
        own_lanes = iota(shape, 1) // LANES == iota(shape, 0) % per_pair
        rest = jnp.zeros((HEAD_DIM - TILE, HEAD_DIM), BF16)

        @pl.loop(0, sides)
        def _(side):
            spaced = jnp.where(own_lanes, matmul(owner_row, labels[side]), 0.0).astype(BF16)
            label = matmul(spaced, fold).astype(BF16)
            shift = one_hot(
                ((row < cl_dev) & (column == row + cl_dev * side))
                | ((row == cl_dev) & (column == invalid))
            )
            k_mask[side] = matmul(label, shift).astype(BF16)

            @pl.when((side >= 1) & (side <= CORES))
            def _():
                mask = jnp.concatenate([mask_in[side - 1], rest], axis=0)
                q_mask[side - 1] = matmul(label, mask).astype(BF16)

    def both(stage):
        def pair(k):
            @pl.loop(CORES * k, CORES * k + CORES)
            def _(h):
                stage(h)

        return pair

    stages = (both(pack), both(turn), share, attend, both(turn_back), both(finish))

    @pl.loop(0, mine + STEP * (len(stages) - 1))
    def _(step):
        for number, stage in enumerate(stages):
            lag = STEP * number

            @pl.when((step >= lag) & (step < mine + lag))
            def _():
                stage(step - lag)

            if number == 0:

                @pl.when(step == 0)
                def _():
                    make_perms()
                    turn_labels()

        @pl.when(step == 1)
        def _():
            share_labels()

        @pl.when(step == 2)
        def _():
            make_masks()

    wait_bytes(out_ref.at[:, pl.ds(0, (nx - 1) * width)], out_sem)

    @pl.loop(0, heads)
    def _(h):
        wait_bytes(x_recv.at[h, pl.ds(0, tokens - rows)], sem.at[X_SEND, h])
        wait_bytes(a_send.at[h, others_a], sem.at[A_SEND, h])
        wait_bytes(b_send.at[h, :, others_b], sem.at[B_SEND, h])
        wait_bytes(t_send.at[h, others_a], sem.at[RA_SEND, h])
        wait_bytes(x_back.at[h, pl.ds(0, tokens - rows)], sem.at[RX_SEND, h])
        wait_bytes(x_back.at[h, pl.ds(0, rows)], sem.at[RX_OWN, h])

        @pl.when(core != h % 2)
        def _():
            wait_bytes(b_send.at[h, :, pl.ds(0, b_rows)], sem.at[B_NEAR, h])

    @pl.loop(0, mine)
    def _(k):
        wait_bytes(work.at[(k, *two_sides)], sem.at[H_SEND, k])
        wait_bytes(o_send.at[k, :, pl.ds(0, (line - 1) * b_rows)], sem.at[RB_SEND, k])

    for par in range(CORES):
        wait_bytes(l_a_send.at[label_others], label_sem.at[0, par])
        wait_bytes(l_b_send.at[par, label_others], label_sem.at[2, par])

        @pl.when(core != par)
        def _():
            wait_bytes(l_b_send.at[par, pl.ds(0, line)], label_sem.at[3, par])

        @pl.when(tok != keepers[par])
        def _():
            wait_bytes(mask_tile, mask_sem.at[par])

    wait_bytes(labels.at[pl.ds(0, 2)], label_sem.at[5, 0])


def per_device(queries, key_rows, values, cluster, owners, pair_list):
    nx, n_tok = lax.axis_size("head"), lax.axis_size("tok")
    n_axis = math.isqrt(n_tok // CORES)
    cl_dev = pair_list.shape[0]
    per_pair = CAP * cl_dev // n_tok
    rows, features = queries.shape
    heads = features // nx // HEAD_DIM
    tokens = rows * nx
    slots, line = n_tok * per_pair, n_axis * CORES
    mine, sides, half = heads // CORES, CORES + 2, slots // CORES
    wide, thin = 3 * HEAD_DIM, HEAD_DIM
    lane_step = min(slots, HEAD_DIM)

    def vmem(*shape, dtype=BF16):
        return pltpu.VMEM(shape, dtype)

    return pl.pallas_call(
        functools.partial(kernel, (nx, n_axis, per_pair, heads)),
        out_shape=jax.ShapeDtypeStruct((rows, features), BF16),
        in_specs=[pl.BlockSpec(memory_space=pltpu.HBM)] * 3
        + [pl.BlockSpec(memory_space=pltpu.VMEM)] * 3,
        out_specs=pl.BlockSpec(memory_space=pltpu.HBM),
        scratch_shapes=[
            vmem(heads, tokens, wide),
            vmem(heads, slots, wide),
            vmem(heads, slots, wide),
            vmem(heads, CORES, half, wide),
            vmem(mine, sides, slots, wide),
            vmem(mine, CORES, slots, thin),
            vmem(heads, CORES, half, thin),
            vmem(heads, slots, thin),
            vmem(heads, slots, thin),
            vmem(heads, tokens, thin),
            vmem(slots, tokens),
            vmem(tokens, slots),
            vmem(CORES, half, slots),
            vmem(slots, slots),
            vmem(3, slots, slots, dtype=F32),
            vmem(slots, lane_step, dtype=F32),
            vmem(slots, lane_step, dtype=F32),
            vmem(slots, thin, dtype=F32),
            vmem(n_tok, thin),
            vmem(CORES, n_tok, thin),
            vmem(CORES, n_tok, thin),
            vmem(line * line, thin),
            vmem(sides, n_tok, thin),
            vmem(TILE, thin),
            vmem(CORES, TILE, thin),
            vmem(CORES, slots, thin),
            vmem(sides, slots, thin),
            pltpu.SemaphoreType.DMA((STAGES, heads)),
            pltpu.SemaphoreType.DMA((6, 2)),
            pltpu.SemaphoreType.DMA((2 * CORES,)),
            pltpu.SemaphoreType.DMA,
        ],
        compiler_params=pltpu.CompilerParams(
            collective_id=0, has_side_effects=True, vmem_limit_bytes=60 * 2**20
        ),
    )(queries, key_rows, values, cluster[None, :], owners[None, :], pair_list)


def solution(mesh):
    return jax.shard_map(
        per_device,
        mesh=mesh,
        in_specs=(
            P(("tok", "head"), None),
            P(("tok", "head"), None),
            P(("tok", "head"), None),
            P("tok"),
            P(),
            P("tok", None),
        ),
        out_specs=P(("tok", "head"), None),
        check_vma=False,
    )
```

```python
import functools
import math

import jax
import jax.numpy as jnp
from jax import lax
from jax.experimental import pallas as pl
from jax.experimental.pallas import tpu as pltpu
from jax.sharding import PartitionSpec as P

HEAD_DIM = 128
CAP = 128
CORES = 2
TILE = 16
LANES = 8
AHEAD = 2
STEP = 1
MASKED = -(2.0**100)
SCALE_LOG2 = math.log2(math.e) / math.sqrt(HEAD_DIM)
MESH = pl.DeviceIdType.MESH
F32 = jnp.float32
BF16 = jnp.bfloat16

X_OWN, X_SEND, X_RECV, A_SEND, A_RECV, B_SEND, B_NEAR, B_RECV, H_SEND, H_RECV = range(10)
RB_SEND, RB_RECV, RA_SEND, RA_RECV, RX_SEND, RX_OWN = range(10, 16)
STAGES = 16


def matmul(left, right):
    return jnp.dot(left, right, preferred_element_type=F32)


def matmul_t(left, right):
    return lax.dot_general(left, right, (((1,), (1,)), ((), ())), preferred_element_type=F32)


def iota(shape, dim):
    return lax.broadcasted_iota(jnp.int32, shape, dim)


def one_hot(condition):
    return jnp.where(condition, 1.0, 0.0).astype(BF16)


def wait_bytes(ref, sem):
    pltpu.make_async_copy(ref, ref, sem).wait()


def kernel(
    dims, q_ref, k_ref, v_ref, cluster, owners, pair_list, out_ref,
    x_recv, a_send, a_recv, b_send, work, o_send, o_recv, t_send, t_recv, x_back,
    pick, pick_t, perm, perm_t, scores, peak, total, mixed,
    l_a_send, l_a_recv, l_b_send, l_b_recv, labels, mask_tile, mask_in, q_mask, k_mask,
    sem, label_sem, mask_sem, out_sem,
):
    nx, n_axis, per_pair, heads = dims
    rows = q_ref.shape[0]
    tokens = nx * rows
    width = heads * HEAD_DIM
    line = n_axis * CORES
    n_tok = n_axis * line
    slots = n_tok * per_pair
    a_rows = line * per_pair
    b_rows = n_axis * per_pair
    mine = heads // CORES
    sides = CORES + 2
    cl_dev, pairs = pair_list.shape
    invalid = sides * cl_dev
    my_x = lax.axis_index("head")
    tok = lax.axis_index("tok")
    z, y, core = tok // line, (tok // CORES) % n_axis, tok % CORES

    def place(par):
        return z + par * (y - z), y + par * (z - y)

    def device(a, b, c, par):
        return ((a + par * (b - a)) * line + (b + par * (a - b)) * CORES + c, my_x)

    def next_chip(step):
        a, b = place(core)
        chip = lax.rem(a * n_axis + b + n_axis * n_axis + step, n_axis * n_axis)
        return device(chip // n_axis, chip % n_axis, core, core)

    def copy_to(src, dst, send, recv, target):
        pltpu.make_async_remote_copy(
            src_ref=src, dst_ref=dst, send_sem=send, recv_sem=recv,
            device_id=target, device_id_type=MESH,
        ).start()

    def lanes(start, size):
        return pl.ds(pl.multiple_of(start, HEAD_DIM), size)

    def block(index, size):
        return pl.ds(pl.multiple_of(index * size, size), size)

    barrier = pltpu.get_barrier_semaphore()

    def greet(target):
        pl.semaphore_signal(barrier, inc=1, device_id=target, device_id_type=MESH)

    @pl.loop(1, nx)
    def _(d):
        greet((tok, lax.rem(my_x + d, nx)))

    @pl.loop(1, line)
    def _(d):
        greet((z * line + lax.rem(y * CORES + core + d, line), my_x))

    @pl.loop(1, n_axis)
    def _(d):
        for c in range(CORES):
            greet(((lax.rem(z + d, n_axis) * n_axis + y) * CORES + c, my_x))

    greet(next_chip(1))
    greet(next_chip(-1))
    @pl.when(y != z)
    def _():
        for c in range(CORES):
            greet(((y * n_axis + z) * CORES + c, my_x))

    @pl.when(y == z)
    def _():
        for c in range(CORES):
            greet((tok + 1 - 2 * core, my_x))

    greeted = (nx - 1) + (line - 1) + (n_axis - 1) * CORES + 2 + CORES

    def own_copy(ref, kind, h):
        return pltpu.make_async_copy(
            ref.at[:, lanes(my_x * width + h * HEAD_DIM, HEAD_DIM)],
            x_recv.at[h, block(my_x, rows), pl.ds(kind * HEAD_DIM, HEAD_DIM)],
            sem.at[X_OWN, h],
        )

    pl.semaphore_wait(barrier, greeted)

    def spread(h):
        @pl.loop(1, nx)
        def _(d):
            other = lax.rem(my_x + d, nx)
            for kind, ref in enumerate((q_ref, k_ref, v_ref)):
                copy_to(
                    ref.at[:, lanes(other * width + h * HEAD_DIM, HEAD_DIM)],
                    x_recv.at[h, block(my_x, rows), pl.ds(kind * HEAD_DIM, HEAD_DIM)],
                    sem.at[X_SEND, h],
                    sem.at[X_RECV, h],
                    (tok, other),
                )

    @pl.loop(0, min(AHEAD, heads))
    def _(h):
        spread(h)

    @pl.loop(0, heads)
    def _(h):
        for kind, ref in enumerate((q_ref, k_ref, v_ref)):
            own_copy(ref, kind, h).start()

    pair_local = pair_list[...] - (tok - core - 1) * cl_dev
    lane = iota((cl_dev, HEAD_DIM), 1)
    allowed = lane > invalid
    for j in range(pairs):
        allowed = allowed | (pair_local[:, j : j + 1] == lane)
    mask_tile[...] = jnp.concatenate(
        [jnp.where(allowed, 0.0, MASKED), jnp.zeros((TILE - cl_dev, HEAD_DIM), F32)], axis=0
    ).astype(BF16)

    keepers = [(z * n_axis + y) * CORES, (y * n_axis + z) * CORES + 1]
    for end, keeper in enumerate(keepers):

        @pl.when(tok == keeper)
        def _():
            pltpu.make_async_copy(
                mask_tile, mask_in.at[core], mask_sem.at[CORES + core]
            ).start()

        @pl.when(tok != keeper)
        def _():
            copy_to(
                mask_tile, mask_in.at[core], mask_sem.at[end], mask_sem.at[CORES + core],
                (keeper, my_x),
            )

    clusters = owners.shape[1]
    cluster_hot = one_hot(iota((clusters, tokens), 0) == cluster[...])
    table = jnp.where(
        iota((TILE, clusters), 0) == 0, owners[...] // cl_dev, owners[...] % cl_dev
    )
    found = matmul(table.astype(F32).astype(BF16), cluster_hot).astype(jnp.int32)
    target, local_id = found[0:1], found[1:2]
    target_hot = one_hot(iota((n_tok, tokens), 0) == target)
    earlier = one_hot(iota((tokens, tokens), 0) < iota((tokens, tokens), 1))
    rank = jnp.sum(matmul(target_hot, earlier) * target_hot.astype(F32), axis=0, keepdims=True)
    rank = rank.astype(jnp.int32)
    send_row = target * per_pair + rank
    chunk = min(128, tokens)

    @pl.loop(0, slots // chunk)
    def _(i):
        pick[block(i, chunk)] = one_hot(iota((chunk, tokens), 0) + i * chunk == send_row)

    lane = iota((HEAD_DIM, tokens), 0) - rank * LANES
    filled = matmul_t(target_hot, one_hot((lane == local_id) | (lane == cl_dev)))
    lane = iota((n_tok, HEAD_DIM), 1)
    l_a_send[...] = jnp.where(lane % LANES == cl_dev, 1.0 - filled, filled).astype(BF16)

    def first_hop(src, dst, send, recv, par, size):
        a, b = place(par)
        pltpu.make_async_copy(src.at[block(a, size)], dst.at[block(a, size)], recv).start()

        @pl.loop(1, n_axis)
        def _(d):
            other = lax.rem(a + d, n_axis)
            copy_to(
                src.at[block(other, size)], dst.at[block(a, size)], send, recv,
                device(other, b, core, par),
            )

    def second_hop(src_at, dst, send, near, recv, par):
        a, b = place(par)

        @pl.when(core == par)
        def _():
            pltpu.make_async_copy(src_at(b), dst, recv).start()

        @pl.when(core != par)
        def _():
            copy_to(src_at(b), dst, near, recv, device(a, b, par, par))

        @pl.loop(1, n_axis)
        def _(d):
            other = lax.rem(b + d, n_axis)
            copy_to(src_at(other), dst, send, recv, device(a, other, par, par))

    def source(par):
        _, b = place(par)
        return b * CORES + core

    others_a = pl.ds(0, slots - a_rows)
    others_b = pl.ds(0, b_rows * (n_axis - 1))
    label_others = pl.ds(0, n_tok - line)

    for par in range(CORES):
        first_hop(
            l_a_send, l_a_recv.at[par], label_sem.at[0, par], label_sem.at[1, par], par, line
        )

    def pack(h):
        for kind, ref in enumerate((q_ref, k_ref, v_ref)):
            own_copy(ref, kind, h).wait()
        wait_bytes(x_recv.at[h, pl.ds(0, tokens - rows)], sem.at[X_RECV, h])

        @pl.when(h + AHEAD < heads)
        def _():
            spread(h + AHEAD)

        @pl.loop(0, 2)
        def _(i):
            part = block(i, slots // 2)
            a_send[h, part] = matmul(pick[part], x_recv[h]).astype(BF16)

        first_hop(a_send.at[h], a_recv.at[h], sem.at[A_SEND, h], sem.at[A_RECV, h], h % 2, a_rows)

    def turn(h):
        par = h % 2
        wait_bytes(a_recv.at[h], sem.at[A_RECV, h])

        @pl.loop(0, CORES)
        def _(i):
            b_send[h, i] = matmul(perm[i], a_recv[h]).astype(BF16)

        second_hop(
            lambda other: b_send.at[h, :, block(other, b_rows)],
            work.at[h // 2, pl.ds(1, CORES), block(source(par), b_rows)],
            sem.at[B_SEND, h], sem.at[B_NEAR, h], sem.at[B_RECV, h // 2], par,
        )

    def share(k):
        wait_bytes(work.at[k, pl.ds(1, CORES)], sem.at[B_RECV, k])
        for step, src, dst in ((-1, 1, CORES + 1), (1, CORES, 0)):
            copy_to(
                work.at[k, src, :, pl.ds(HEAD_DIM, 2 * HEAD_DIM)],
                work.at[k, dst, :, pl.ds(HEAD_DIM, 2 * HEAD_DIM)],
                sem.at[H_SEND, k], sem.at[H_RECV, k], next_chip(step),
            )

    two_sides = (pl.ds(0, 2), slice(None), pl.ds(HEAD_DIM, 2 * HEAD_DIM))
    tiles = slots // HEAD_DIM if slots >= HEAD_DIM else 1
    lane_step = min(slots, HEAD_DIM)

    def attend(k):
        peak[...] = jnp.full((CORES, slots, lane_step), -jnp.inf, F32)

        @pl.loop(0, 3 * CORES)
        def _(n):
            i = (n // 2) % 2 + n // 5
            part = 1 - i + n % 2 + (n // 4) * (2 * i - 1)

            @pl.when(n == 4)
            def _():
                wait_bytes(work.at[(k, *two_sides)], sem.at[H_RECV, k])

            query = jnp.concatenate([work[k, i + 1, :, 0:HEAD_DIM], q_mask[i]], axis=1)
            key = jnp.concatenate(
                [work[k, i + part, :, HEAD_DIM : 2 * HEAD_DIM], k_mask[i + part]], axis=1
            )
            found = matmul_t(query, key)
            scores[i, part] = found
            peak[i] = functools.reduce(
                jnp.maximum,
                [found[:, t * lane_step : (t + 1) * lane_step] for t in range(tiles)],
                peak[i],
            )

        @pl.loop(0, CORES)
        def _(i):
            row_max = jnp.max(peak[i], axis=1, keepdims=True)
            peak[i] = jnp.broadcast_to(row_max, (slots, lane_step))
            total[...] = jnp.zeros((slots, lane_step), F32)
            mixed[...] = jnp.zeros((slots, HEAD_DIM), F32)

            @pl.loop(0, 3)
            def _(part):
                row_max = peak[i]
                weights = [
                    jnp.exp2(
                        (scores[i, part, :, t * lane_step : (t + 1) * lane_step] - row_max)
                        * SCALE_LOG2
                    )
                    for t in range(tiles)
                ]
                total[...] += functools.reduce(jnp.add, weights)
                rounded = jnp.concatenate([w.astype(BF16) for w in weights], axis=1)
                mixed[...] += matmul(rounded, work[k, i + part, :, 2 * HEAD_DIM : 3 * HEAD_DIM])

            row_total = jnp.sum(total[...], axis=1, keepdims=True)
            o_send[k, i] = (mixed[...] / row_total).astype(BF16)

        h = CORES * k + core
        a, b = place(core)
        here = b * CORES + core
        dst = o_recv.at[h, :, block(b, b_rows)]

        def src(other):
            return o_send.at[k, :, block(other, b_rows)]

        pltpu.make_async_copy(src(here), dst, sem.at[RB_RECV, h]).start()

        @pl.loop(1, line)
        def _(d):
            other = lax.rem(here + d, line)
            copy_to(
                src(other), dst, sem.at[RB_SEND, k], sem.at[RB_RECV, h],
                device(a, other // CORES, other % CORES, core),
            )

    def turn_back(h):
        wait_bytes(o_recv.at[h], sem.at[RB_RECV, h])
        t_send[h] = matmul(perm_t[...], o_recv[h].reshape(slots, HEAD_DIM)).astype(BF16)
        first_hop(
            t_send.at[h], t_recv.at[h], sem.at[RA_SEND, h], sem.at[RA_RECV, h], h % 2, a_rows
        )

    def finish(h):
        wait_bytes(t_recv.at[h], sem.at[RA_RECV, h])
        x_back[h] = matmul(pick_t[...], t_recv[h]).astype(BF16)
        column = lanes(my_x * width + h * HEAD_DIM, HEAD_DIM)
        pltpu.make_async_copy(
            x_back.at[h, block(my_x, rows)], out_ref.at[:, column], sem.at[RX_OWN, h]
        ).start()

        @pl.loop(1, nx)
        def _(d):
            other = lax.rem(my_x + d, nx)
            copy_to(
                x_back.at[h, block(other, rows)], out_ref.at[:, column],
                sem.at[RX_SEND, h], out_sem, (tok, other),
            )

    def make_perms():
        half = slots // CORES

        def source_of(row, i):
            r, a, b = row % per_pair, (row // per_pair) % n_axis, row // b_rows
            return a * a_rows + b * (CORES * per_pair) + i * per_pair + r

        for i in range(CORES):
            perm[i] = one_hot(source_of(iota((half, slots), 0), i) == iota((half, slots), 1))

        @pl.loop(0, slots // chunk)
        def _(part):
            row, column = iota((chunk, slots), 0) + part * chunk, iota((chunk, slots), 1)
            perm_t[block(part, chunk)] = one_hot(
                source_of(column % half, column // half) == row
            )

        same = one_hot(iota((tokens, tokens), 0) == iota((tokens, tokens), 1))
        pick_t[...] = matmul_t(same, pick[...]).astype(BF16)

    def turn_labels():
        row, column = iota((n_tok, n_tok), 0), iota((n_tok, n_tok), 1)
        start = (row // CORES) % n_axis * line + row // line * CORES + row % CORES
        turned = one_hot(start == column)
        for par in range(CORES):
            wait_bytes(l_a_recv.at[par], label_sem.at[1, par])
            l_b_send[par] = matmul(turned, l_a_recv[par]).astype(BF16)
            second_hop(
                lambda other: l_b_send.at[par, block(other, line)],
                l_b_recv.at[block(source(par), line)],
                label_sem.at[2, par], label_sem.at[3, par], label_sem.at[4, 0], par,
            )

    def share_labels():
        wait_bytes(l_b_recv, label_sem.at[4, 0])
        shape = (n_tok, line * line)
        row, column = iota(shape, 0), iota(shape, 1)
        start = row // n_axis * line + row % n_axis * CORES
        for i in range(CORES):
            labels[i + 1] = matmul(one_hot(start + i == column), l_b_recv[...]).astype(BF16)
        for step, src, dst in ((-1, 1, CORES + 1), (1, CORES, 0)):
            copy_to(
                labels.at[src], labels.at[dst], label_sem.at[5, 0], label_sem.at[5, 1],
                next_chip(step),
            )

    def make_masks():
        wait_bytes(labels.at[pl.ds(0, 2)], label_sem.at[5, 1])
        for c in range(CORES):
            wait_bytes(mask_in.at[c], mask_sem.at[CORES + c])
        row, column = iota((HEAD_DIM, HEAD_DIM), 0), iota((HEAD_DIM, HEAD_DIM), 1)
        fold = one_hot((row % LANES == column) & (row < per_pair * LANES))
        owner_row = one_hot(iota((slots, n_tok), 0) // per_pair == iota((slots, n_tok), 1))
        shape = (slots, HEAD_DIM)
        own_lanes = iota(shape, 1) // LANES == iota(shape, 0) % per_pair
        rest = jnp.zeros((HEAD_DIM - TILE, HEAD_DIM), BF16)

        @pl.loop(0, sides)
        def _(side):
            spaced = jnp.where(own_lanes, matmul(owner_row, labels[side]), 0.0).astype(BF16)
            label = matmul(spaced, fold).astype(BF16)
            shift = one_hot(
                ((row < cl_dev) & (column == row + cl_dev * side))
                | ((row == cl_dev) & (column == invalid))
            )
            k_mask[side] = matmul(label, shift).astype(BF16)

            @pl.when((side >= 1) & (side <= CORES))
            def _():
                mask = jnp.concatenate([mask_in[side - 1], rest], axis=0)
                q_mask[side - 1] = matmul(label, mask).astype(BF16)

    def both(stage):
        def pair(k):
            @pl.loop(CORES * k, CORES * k + CORES)
            def _(h):
                stage(h)

        return pair

    stages = (both(pack), both(turn), share, attend, both(turn_back), both(finish))

    @pl.loop(0, mine + STEP * (len(stages) - 1))
    def _(step):
        for number, stage in enumerate(stages):
            lag = STEP * number

            @pl.when((step >= lag) & (step < mine + lag))
            def _():
                stage(step - lag)

            if number == 0:

                @pl.when(step == 0)
                def _():
                    make_perms()
                    turn_labels()

        @pl.when(step == 1)
        def _():
            share_labels()

        @pl.when(step == 2)
        def _():
            make_masks()

    wait_bytes(out_ref.at[:, pl.ds(0, (nx - 1) * width)], out_sem)

    @pl.loop(0, heads)
    def _(h):
        wait_bytes(x_recv.at[h, pl.ds(0, tokens - rows)], sem.at[X_SEND, h])
        wait_bytes(a_send.at[h, others_a], sem.at[A_SEND, h])
        wait_bytes(b_send.at[h, :, others_b], sem.at[B_SEND, h])
        wait_bytes(t_send.at[h, others_a], sem.at[RA_SEND, h])
        wait_bytes(x_back.at[h, pl.ds(0, tokens - rows)], sem.at[RX_SEND, h])
        wait_bytes(x_back.at[h, pl.ds(0, rows)], sem.at[RX_OWN, h])

        @pl.when(core != h % 2)
        def _():
            wait_bytes(b_send.at[h, :, pl.ds(0, b_rows)], sem.at[B_NEAR, h])

    @pl.loop(0, mine)
    def _(k):
        wait_bytes(work.at[(k, *two_sides)], sem.at[H_SEND, k])
        wait_bytes(o_send.at[k, :, pl.ds(0, (line - 1) * b_rows)], sem.at[RB_SEND, k])

    for par in range(CORES):
        wait_bytes(l_a_send.at[label_others], label_sem.at[0, par])
        wait_bytes(l_b_send.at[par, label_others], label_sem.at[2, par])

        @pl.when(core != par)
        def _():
            wait_bytes(l_b_send.at[par, pl.ds(0, line)], label_sem.at[3, par])

        @pl.when(tok != keepers[par])
        def _():
            wait_bytes(mask_tile, mask_sem.at[par])

    wait_bytes(labels.at[pl.ds(0, 2)], label_sem.at[5, 0])


def per_device(queries, key_rows, values, cluster, owners, pair_list):
    nx, n_tok = lax.axis_size("head"), lax.axis_size("tok")
    n_axis = math.isqrt(n_tok // CORES)
    cl_dev = pair_list.shape[0]
    per_pair = CAP * cl_dev // n_tok
    rows, features = queries.shape
    heads = features // nx // HEAD_DIM
    tokens = rows * nx
    slots, line = n_tok * per_pair, n_axis * CORES
    mine, sides, half = heads // CORES, CORES + 2, slots // CORES
    wide, thin = 3 * HEAD_DIM, HEAD_DIM
    lane_step = min(slots, HEAD_DIM)

    def vmem(*shape, dtype=BF16):
        return pltpu.VMEM(shape, dtype)

    return pl.pallas_call(
        functools.partial(kernel, (nx, n_axis, per_pair, heads)),
        out_shape=jax.ShapeDtypeStruct((rows, features), BF16),
        in_specs=[pl.BlockSpec(memory_space=pltpu.HBM)] * 3
        + [pl.BlockSpec(memory_space=pltpu.VMEM)] * 3,
        out_specs=pl.BlockSpec(memory_space=pltpu.HBM),
        scratch_shapes=[
            vmem(heads, tokens, wide),
            vmem(heads, slots, wide),
            vmem(heads, slots, wide),
            vmem(heads, CORES, half, wide),
            vmem(mine, sides, slots, wide),
            vmem(mine, CORES, slots, thin),
            vmem(heads, CORES, half, thin),
            vmem(heads, slots, thin),
            vmem(heads, slots, thin),
            vmem(heads, tokens, thin),
            vmem(slots, tokens),
            vmem(tokens, slots),
            vmem(CORES, half, slots),
            vmem(slots, slots),
            vmem(CORES, 3, slots, slots, dtype=F32),
            vmem(CORES, slots, lane_step, dtype=F32),
            vmem(slots, lane_step, dtype=F32),
            vmem(slots, thin, dtype=F32),
            vmem(n_tok, thin),
            vmem(CORES, n_tok, thin),
            vmem(CORES, n_tok, thin),
            vmem(line * line, thin),
            vmem(sides, n_tok, thin),
            vmem(TILE, thin),
            vmem(CORES, TILE, thin),
            vmem(CORES, slots, thin),
            vmem(sides, slots, thin),
            pltpu.SemaphoreType.DMA((STAGES, heads)),
            pltpu.SemaphoreType.DMA((6, 2)),
            pltpu.SemaphoreType.DMA((2 * CORES,)),
            pltpu.SemaphoreType.DMA,
        ],
        compiler_params=pltpu.CompilerParams(
            collective_id=0, has_side_effects=True, vmem_limit_bytes=60 * 2**20
        ),
    )(queries, key_rows, values, cluster[None, :], owners[None, :], pair_list)


def solution(mesh):
    return jax.shard_map(
        per_device,
        mesh=mesh,
        in_specs=(
            P(("tok", "head"), None),
            P(("tok", "head"), None),
            P(("tok", "head"), None),
            P("tok"),
            P(),
            P("tok", None),
        ),
        out_specs=P(("tok", "head"), None),
        check_vma=False,
    )
```

```python
import functools
import math

import jax
import jax.numpy as jnp
from jax import lax
from jax.experimental import pallas as pl
from jax.experimental.pallas import tpu as pltpu
from jax.sharding import PartitionSpec as P

HEAD_DIM = 128
CAP = 128
CORES = 2
TILE = 16
LANES = 8
AHEAD = 2
MASKED = -(2.0**100)
SCALE_LOG2 = math.log2(math.e) / math.sqrt(HEAD_DIM)
MESH = pl.DeviceIdType.MESH
F32 = jnp.float32
BF16 = jnp.bfloat16

X_OWN, X_SEND, X_RECV, A_SEND, A_RECV, B_SEND, B_NEAR, B_RECV, H_SEND, H_RECV = range(10)
RB_SEND, RB_RECV, RA_SEND, RA_RECV, RX_SEND, RX_OWN = range(10, 16)
A_VIA, A_ON, B_VIA, B_ON = range(16, 20)
STAGES = 20


def matmul(left, right):
    return jnp.dot(left, right, preferred_element_type=F32)


def matmul_t(left, right):
    return lax.dot_general(left, right, (((1,), (1,)), ((), ())), preferred_element_type=F32)


def iota(shape, dim):
    return lax.broadcasted_iota(jnp.int32, shape, dim)


def one_hot(condition):
    return jnp.where(condition, 1.0, 0.0).astype(BF16)


def wait_bytes(ref, sem):
    pltpu.make_async_copy(ref, ref, sem).wait()


def kernel(
    dims, q_ref, k_ref, v_ref, cluster, owners, pair_list, out_ref,
    x_recv, a_send, a_recv, a_via, b_send, b_via, work, o_send, o_recv, t_send, t_recv, x_back,
    pick, pick_t, perm, perm_t, scores, peak, total, mixed,
    l_a_send, l_a_recv, l_b_send, l_b_recv, labels, mask_tile, mask_in, q_mask, k_mask,
    sem, label_sem, mask_sem, out_sem,
):
    nx, n_axis, per_pair, heads = dims
    rows = q_ref.shape[0]
    tokens = nx * rows
    width = heads * HEAD_DIM
    line = n_axis * CORES
    n_tok = n_axis * line
    slots = n_tok * per_pair
    a_rows = line * per_pair
    b_rows = n_axis * per_pair
    mine = heads // CORES
    sides = CORES + 2
    cl_dev, pairs = pair_list.shape
    invalid = sides * cl_dev
    my_x = lax.axis_index("head")
    tok = lax.axis_index("tok")
    z, y, core = tok // line, (tok // CORES) % n_axis, tok % CORES

    def place(par):
        return z + par * (y - z), y + par * (z - y)

    def device(a, b, c, par):
        return ((a + par * (b - a)) * line + (b + par * (a - b)) * CORES + c, my_x)

    def next_chip(step):
        a, b = place(core)
        chip = lax.rem(a * n_axis + b + n_axis * n_axis + step, n_axis * n_axis)
        return device(chip // n_axis, chip % n_axis, core, core)

    def copy_to(src, dst, send, recv, target):
        pltpu.make_async_remote_copy(
            src_ref=src, dst_ref=dst, send_sem=send, recv_sem=recv,
            device_id=target, device_id_type=MESH,
        ).start()

    def lanes(start, size):
        return pl.ds(pl.multiple_of(start, HEAD_DIM), size)

    def block(index, size):
        return pl.ds(pl.multiple_of(index * size, size), size)

    barrier = pltpu.get_barrier_semaphore()

    def greet(target):
        pl.semaphore_signal(barrier, inc=1, device_id=target, device_id_type=MESH)

    @pl.loop(1, nx)
    def _(d):
        greet((tok, lax.rem(my_x + d, nx)))

    @pl.loop(1, line)
    def _(d):
        greet((z * line + lax.rem(y * CORES + core + d, line), my_x))

    @pl.loop(1, n_axis)
    def _(d):
        for c in range(CORES):
            greet(((lax.rem(z + d, n_axis) * n_axis + y) * CORES + c, my_x))

    greet(next_chip(1))
    greet(next_chip(-1))
    @pl.when(y != z)
    def _():
        for c in range(CORES):
            greet(((y * n_axis + z) * CORES + c, my_x))

    @pl.when(y == z)
    def _():
        for c in range(CORES):
            greet((tok + 1 - 2 * core, my_x))

    greeted = (nx - 1) + (line - 1) + (n_axis - 1) * CORES + 2 + CORES

    def own_copy(ref, kind, h):
        return pltpu.make_async_copy(
            ref.at[:, lanes(my_x * width + h * HEAD_DIM, HEAD_DIM)],
            x_recv.at[h, block(my_x, rows), pl.ds(kind * HEAD_DIM, HEAD_DIM)],
            sem.at[X_OWN, h],
        )

    pl.semaphore_wait(barrier, greeted)

    def spread(h):
        @pl.loop(1, nx)
        def _(d):
            other = lax.rem(my_x + d, nx)
            for kind, ref in enumerate((q_ref, k_ref, v_ref)):
                copy_to(
                    ref.at[:, lanes(other * width + h * HEAD_DIM, HEAD_DIM)],
                    x_recv.at[h, block(my_x, rows), pl.ds(kind * HEAD_DIM, HEAD_DIM)],
                    sem.at[X_SEND, h],
                    sem.at[X_RECV, h],
                    (tok, other),
                )

    @pl.loop(0, min(AHEAD, heads))
    def _(h):
        spread(h)

    @pl.loop(0, heads)
    def _(h):
        for kind, ref in enumerate((q_ref, k_ref, v_ref)):
            own_copy(ref, kind, h).start()

    pair_local = pair_list[...] - (tok - core - 1) * cl_dev
    lane = iota((cl_dev, HEAD_DIM), 1)
    allowed = lane > invalid
    for j in range(pairs):
        allowed = allowed | (pair_local[:, j : j + 1] == lane)
    mask_tile[...] = jnp.concatenate(
        [jnp.where(allowed, 0.0, MASKED), jnp.zeros((TILE - cl_dev, HEAD_DIM), F32)], axis=0
    ).astype(BF16)

    keepers = [(z * n_axis + y) * CORES, (y * n_axis + z) * CORES + 1]
    for end, keeper in enumerate(keepers):

        @pl.when(tok == keeper)
        def _():
            pltpu.make_async_copy(
                mask_tile, mask_in.at[core], mask_sem.at[CORES + core]
            ).start()

        @pl.when(tok != keeper)
        def _():
            copy_to(
                mask_tile, mask_in.at[core], mask_sem.at[end], mask_sem.at[CORES + core],
                (keeper, my_x),
            )

    clusters = owners.shape[1]
    cluster_hot = one_hot(iota((clusters, tokens), 0) == cluster[...])
    table = jnp.where(
        iota((TILE, clusters), 0) == 0, owners[...] // cl_dev, owners[...] % cl_dev
    )
    found = matmul(table.astype(F32).astype(BF16), cluster_hot).astype(jnp.int32)
    target, local_id = found[0:1], found[1:2]
    target_hot = one_hot(iota((n_tok, tokens), 0) == target)
    earlier = one_hot(iota((tokens, tokens), 0) < iota((tokens, tokens), 1))
    rank = jnp.sum(matmul(target_hot, earlier) * target_hot.astype(F32), axis=0, keepdims=True)
    rank = rank.astype(jnp.int32)
    send_row = target * per_pair + rank
    chunk = min(128, tokens)

    @pl.loop(0, slots // chunk)
    def _(i):
        pick[block(i, chunk)] = one_hot(iota((chunk, tokens), 0) + i * chunk == send_row)

    lane = iota((HEAD_DIM, tokens), 0) - rank * LANES
    filled = matmul_t(target_hot, one_hot((lane == local_id) | (lane == cl_dev)))
    lane = iota((n_tok, HEAD_DIM), 1)
    l_a_send[...] = jnp.where(lane % LANES == cl_dev, 1.0 - filled, filled).astype(BF16)

    half, half_way = n_axis // 2, n_axis // 4 * (1 - 2 * core)

    def round_ring(here, step):
        return lax.rem(here + n_axis + step, n_axis)

    def first_hop(src, dst, send, recv, par, size, via=None, via_recv=None):
        a, b = place(par)
        pltpu.make_async_copy(src.at[block(a, size)], dst.at[block(a, size)], recv).start()

        def put(other):
            copy_to(
                src.at[block(other, size)], dst.at[block(a, size)], send, recv,
                device(other, b, core, par),
            )

        if via is None:
            put(round_ring(a, half))
        else:
            copy_to(
                src.at[block(round_ring(a, half), size)], via, send, via_recv,
                device(round_ring(a, half_way), b, core, par),
            )

        @pl.loop(1, half)
        def _(d):
            put(round_ring(a, d))
            put(round_ring(a, -d))

    def second_hop(src_at, dst, send, near, recv, par, via=None, via_recv=None):
        a, b = place(par)

        def put(other):
            copy_to(src_at(other), dst, send, recv, device(a, other, par, par))

        if via is None:
            put(round_ring(b, half))
        else:
            copy_to(
                src_at(round_ring(b, half)), via, send, via_recv,
                device(a, round_ring(b, half_way), core, par),
            )

        @pl.loop(1, half)
        def _(d):
            put(round_ring(b, d))
            put(round_ring(b, -d))

        @pl.when(core == par)
        def _():
            pltpu.make_async_copy(src_at(b), dst, recv).start()

        @pl.when(core != par)
        def _():
            copy_to(src_at(b), dst, near, recv, device(a, b, par, par))

    relayed = n_axis >= 4

    def pass_first(h):
        par = h % 2
        a, b = place(par)
        wait_bytes(a_via.at[h], sem.at[A_VIA, h])
        copy_to(
            a_via.at[h], a_recv.at[h, block(round_ring(a, -half_way), a_rows)],
            sem.at[A_ON, h], sem.at[A_RECV, h],
            device(round_ring(a, half_way), b, core, par),
        )

    def pass_second(h):
        par = h % 2
        a, b = place(par)
        wait_bytes(b_via.at[h], sem.at[B_VIA, h])
        origin = round_ring(b, -half_way) * CORES + core
        copy_to(
            b_via.at[h], work.at[h // 2, pl.ds(1, CORES), block(origin, b_rows)],
            sem.at[B_ON, h], sem.at[B_RECV, h // 2],
            device(a, round_ring(b, half_way), par, par),
        )

    def source(par):
        _, b = place(par)
        return b * CORES + core

    others_a = pl.ds(0, slots - a_rows)
    others_b = pl.ds(0, b_rows * (n_axis - 1))
    label_others = pl.ds(0, n_tok - line)

    for par in range(CORES):
        first_hop(
            l_a_send, l_a_recv.at[par], label_sem.at[0, par], label_sem.at[1, par], par, line
        )

    def pack(h):
        for kind, ref in enumerate((q_ref, k_ref, v_ref)):
            own_copy(ref, kind, h).wait()
        wait_bytes(x_recv.at[h, pl.ds(0, tokens - rows)], sem.at[X_RECV, h])

        @pl.when(h + AHEAD < heads)
        def _():
            spread(h + AHEAD)

        @pl.loop(0, 2)
        def _(i):
            part = block(i, slots // 2)
            a_send[h, part] = matmul(pick[part], x_recv[h]).astype(BF16)

        via = (a_via.at[h], sem.at[A_VIA, h]) if relayed else ()
        first_hop(
            a_send.at[h], a_recv.at[h], sem.at[A_SEND, h], sem.at[A_RECV, h], h % 2, a_rows, *via
        )

    def turn(h):
        par = h % 2
        wait_bytes(a_recv.at[h], sem.at[A_RECV, h])

        @pl.loop(0, CORES)
        def _(i):
            b_send[h, i] = matmul(perm[i], a_recv[h]).astype(BF16)

        via = (b_via.at[h], sem.at[B_VIA, h]) if relayed else ()
        second_hop(
            lambda other: b_send.at[h, :, block(other, b_rows)],
            work.at[h // 2, pl.ds(1, CORES), block(source(par), b_rows)],
            sem.at[B_SEND, h], sem.at[B_NEAR, h], sem.at[B_RECV, h // 2], par, *via,
        )

    def share(k):
        wait_bytes(work.at[k, pl.ds(1, CORES)], sem.at[B_RECV, k])
        for step, src, dst in ((-1, 1, CORES + 1), (1, CORES, 0)):
            copy_to(
                work.at[k, src, :, pl.ds(HEAD_DIM, 2 * HEAD_DIM)],
                work.at[k, dst, :, pl.ds(HEAD_DIM, 2 * HEAD_DIM)],
                sem.at[H_SEND, k], sem.at[H_RECV, k], next_chip(step),
            )

    two_sides = (pl.ds(0, 2), slice(None), pl.ds(HEAD_DIM, 2 * HEAD_DIM))
    tiles = slots // HEAD_DIM if slots >= HEAD_DIM else 1
    lane_step = min(slots, HEAD_DIM)

    def attend(k):
        peak[...] = jnp.full((CORES, slots, lane_step), -jnp.inf, F32)

        @pl.loop(0, 3 * CORES)
        def _(n):
            i = (n // 2) % 2 + n // 5
            part = 1 - i + n % 2 + (n // 4) * (2 * i - 1)

            @pl.when(n == 4)
            def _():
                wait_bytes(work.at[(k, *two_sides)], sem.at[H_RECV, k])

            query = jnp.concatenate([work[k, i + 1, :, 0:HEAD_DIM], q_mask[i]], axis=1)
            key = jnp.concatenate(
                [work[k, i + part, :, HEAD_DIM : 2 * HEAD_DIM], k_mask[i + part]], axis=1
            )
            found = matmul_t(query, key)
            scores[i, part] = found
            peak[i] = functools.reduce(
                jnp.maximum,
                [found[:, t * lane_step : (t + 1) * lane_step] for t in range(tiles)],
                peak[i],
            )

        @pl.loop(0, CORES)
        def _(i):
            row_max = jnp.max(peak[i], axis=1, keepdims=True)
            peak[i] = jnp.broadcast_to(row_max, (slots, lane_step))
            total[...] = jnp.zeros((slots, lane_step), F32)
            mixed[...] = jnp.zeros((slots, HEAD_DIM), F32)

            @pl.loop(0, 3)
            def _(part):
                row_max = peak[i]
                weights = [
                    jnp.exp2(
                        (scores[i, part, :, t * lane_step : (t + 1) * lane_step] - row_max)
                        * SCALE_LOG2
                    )
                    for t in range(tiles)
                ]
                total[...] += functools.reduce(jnp.add, weights)
                rounded = jnp.concatenate([w.astype(BF16) for w in weights], axis=1)
                mixed[...] += matmul(rounded, work[k, i + part, :, 2 * HEAD_DIM : 3 * HEAD_DIM])

            row_total = jnp.sum(total[...], axis=1, keepdims=True)
            o_send[k, i] = (mixed[...] / row_total).astype(BF16)

        h = CORES * k + core
        a, b = place(core)
        here = b * CORES + core
        dst = o_recv.at[h, :, block(b, b_rows)]

        def src(other):
            return o_send.at[k, :, block(other, b_rows)]

        pltpu.make_async_copy(src(here), dst, sem.at[RB_RECV, h]).start()

        @pl.loop(1, line)
        def _(d):
            other = lax.rem(here + d, line)
            copy_to(
                src(other), dst, sem.at[RB_SEND, k], sem.at[RB_RECV, h],
                device(a, other // CORES, other % CORES, core),
            )

    def turn_back(h):
        wait_bytes(o_recv.at[h], sem.at[RB_RECV, h])
        t_send[h] = matmul(perm_t[...], o_recv[h].reshape(slots, HEAD_DIM)).astype(BF16)
        first_hop(
            t_send.at[h], t_recv.at[h], sem.at[RA_SEND, h], sem.at[RA_RECV, h], h % 2, a_rows
        )

    def finish(h):
        wait_bytes(t_recv.at[h], sem.at[RA_RECV, h])
        x_back[h] = matmul(pick_t[...], t_recv[h]).astype(BF16)
        column = lanes(my_x * width + h * HEAD_DIM, HEAD_DIM)
        pltpu.make_async_copy(
            x_back.at[h, block(my_x, rows)], out_ref.at[:, column], sem.at[RX_OWN, h]
        ).start()

        @pl.loop(1, nx)
        def _(d):
            other = lax.rem(my_x + d, nx)
            copy_to(
                x_back.at[h, block(other, rows)], out_ref.at[:, column],
                sem.at[RX_SEND, h], out_sem, (tok, other),
            )

    def make_perms():
        half = slots // CORES

        def source_of(row, i):
            r, a, b = row % per_pair, (row // per_pair) % n_axis, row // b_rows
            return a * a_rows + b * (CORES * per_pair) + i * per_pair + r

        for i in range(CORES):
            perm[i] = one_hot(source_of(iota((half, slots), 0), i) == iota((half, slots), 1))

        @pl.loop(0, slots // chunk)
        def _(part):
            row, column = iota((chunk, slots), 0) + part * chunk, iota((chunk, slots), 1)
            perm_t[block(part, chunk)] = one_hot(
                source_of(column % half, column // half) == row
            )

        same = one_hot(iota((tokens, tokens), 0) == iota((tokens, tokens), 1))
        pick_t[...] = matmul_t(same, pick[...]).astype(BF16)

    def turn_labels():
        row, column = iota((n_tok, n_tok), 0), iota((n_tok, n_tok), 1)
        start = (row // CORES) % n_axis * line + row // line * CORES + row % CORES
        turned = one_hot(start == column)
        for par in range(CORES):
            wait_bytes(l_a_recv.at[par], label_sem.at[1, par])
            l_b_send[par] = matmul(turned, l_a_recv[par]).astype(BF16)
            second_hop(
                lambda other: l_b_send.at[par, block(other, line)],
                l_b_recv.at[block(source(par), line)],
                label_sem.at[2, par], label_sem.at[3, par], label_sem.at[4, 0], par,
            )

    def share_labels():
        wait_bytes(l_b_recv, label_sem.at[4, 0])
        shape = (n_tok, line * line)
        row, column = iota(shape, 0), iota(shape, 1)
        start = row // n_axis * line + row % n_axis * CORES
        for i in range(CORES):
            labels[i + 1] = matmul(one_hot(start + i == column), l_b_recv[...]).astype(BF16)
        for step, src, dst in ((-1, 1, CORES + 1), (1, CORES, 0)):
            copy_to(
                labels.at[src], labels.at[dst], label_sem.at[5, 0], label_sem.at[5, 1],
                next_chip(step),
            )

    def make_masks():
        wait_bytes(labels.at[pl.ds(0, 2)], label_sem.at[5, 1])
        for c in range(CORES):
            wait_bytes(mask_in.at[c], mask_sem.at[CORES + c])
        row, column = iota((HEAD_DIM, HEAD_DIM), 0), iota((HEAD_DIM, HEAD_DIM), 1)
        fold = one_hot((row % LANES == column) & (row < per_pair * LANES))
        owner_row = one_hot(iota((slots, n_tok), 0) // per_pair == iota((slots, n_tok), 1))
        shape = (slots, HEAD_DIM)
        own_lanes = iota(shape, 1) // LANES == iota(shape, 0) % per_pair
        rest = jnp.zeros((HEAD_DIM - TILE, HEAD_DIM), BF16)

        @pl.loop(0, sides)
        def _(side):
            spaced = jnp.where(own_lanes, matmul(owner_row, labels[side]), 0.0).astype(BF16)
            label = matmul(spaced, fold).astype(BF16)
            shift = one_hot(
                ((row < cl_dev) & (column == row + cl_dev * side))
                | ((row == cl_dev) & (column == invalid))
            )
            k_mask[side] = matmul(label, shift).astype(BF16)

            @pl.when((side >= 1) & (side <= CORES))
            def _():
                mask = jnp.concatenate([mask_in[side - 1], rest], axis=0)
                q_mask[side - 1] = matmul(label, mask).astype(BF16)

    def both(stage):
        def pair(k):
            @pl.loop(CORES * k, CORES * k + CORES)
            def _(h):
                stage(h)

        return pair

    stages = [(0, both(pack)), (1, both(turn)), (2, share), (4, both(turn_back))]
    stages += [(5, both(finish)), (3, attend)]
    if relayed:
        stages.insert(3, (1, both(pass_second)))
        stages.insert(2, (0, both(pass_first)))

    @pl.loop(0, mine + 5)
    def _(step):
        for number, (lag, stage) in enumerate(stages):

            @pl.when((step >= lag) & (step < mine + lag))
            def _():
                stage(step - lag)

            if number == 0:

                @pl.when(step == 0)
                def _():
                    make_perms()
                    turn_labels()

        @pl.when(step == 1)
        def _():
            share_labels()

        @pl.when(step == 2)
        def _():
            make_masks()

    wait_bytes(out_ref.at[:, pl.ds(0, (nx - 1) * width)], out_sem)

    @pl.loop(0, heads)
    def _(h):
        wait_bytes(x_recv.at[h, pl.ds(0, tokens - rows)], sem.at[X_SEND, h])
        wait_bytes(a_send.at[h, others_a], sem.at[A_SEND, h])
        wait_bytes(b_send.at[h, :, others_b], sem.at[B_SEND, h])
        wait_bytes(t_send.at[h, others_a], sem.at[RA_SEND, h])
        wait_bytes(x_back.at[h, pl.ds(0, tokens - rows)], sem.at[RX_SEND, h])
        wait_bytes(x_back.at[h, pl.ds(0, rows)], sem.at[RX_OWN, h])

        if relayed:
            wait_bytes(a_via.at[h], sem.at[A_ON, h])
            wait_bytes(b_via.at[h], sem.at[B_ON, h])

        @pl.when(core != h % 2)
        def _():
            wait_bytes(b_send.at[h, :, pl.ds(0, b_rows)], sem.at[B_NEAR, h])

    @pl.loop(0, mine)
    def _(k):
        wait_bytes(work.at[(k, *two_sides)], sem.at[H_SEND, k])
        wait_bytes(o_send.at[k, :, pl.ds(0, (line - 1) * b_rows)], sem.at[RB_SEND, k])

    for par in range(CORES):
        wait_bytes(l_a_send.at[label_others], label_sem.at[0, par])
        wait_bytes(l_b_send.at[par, label_others], label_sem.at[2, par])

        @pl.when(core != par)
        def _():
            wait_bytes(l_b_send.at[par, pl.ds(0, line)], label_sem.at[3, par])

        @pl.when(tok != keepers[par])
        def _():
            wait_bytes(mask_tile, mask_sem.at[par])

    wait_bytes(labels.at[pl.ds(0, 2)], label_sem.at[5, 0])


def per_device(queries, key_rows, values, cluster, owners, pair_list):
    nx, n_tok = lax.axis_size("head"), lax.axis_size("tok")
    n_axis = math.isqrt(n_tok // CORES)
    cl_dev = pair_list.shape[0]
    per_pair = CAP * cl_dev // n_tok
    rows, features = queries.shape
    heads = features // nx // HEAD_DIM
    tokens = rows * nx
    slots, line = n_tok * per_pair, n_axis * CORES
    mine, sides, half = heads // CORES, CORES + 2, slots // CORES
    wide, thin = 3 * HEAD_DIM, HEAD_DIM
    lane_step = min(slots, HEAD_DIM)

    def vmem(*shape, dtype=BF16):
        return pltpu.VMEM(shape, dtype)

    return pl.pallas_call(
        functools.partial(kernel, (nx, n_axis, per_pair, heads)),
        out_shape=jax.ShapeDtypeStruct((rows, features), BF16),
        in_specs=[pl.BlockSpec(memory_space=pltpu.HBM)] * 3
        + [pl.BlockSpec(memory_space=pltpu.VMEM)] * 3,
        out_specs=pl.BlockSpec(memory_space=pltpu.HBM),
        scratch_shapes=[
            vmem(heads, tokens, wide),
            vmem(heads, slots, wide),
            vmem(heads, slots, wide),
            vmem(heads, line * per_pair, wide),
            vmem(heads, CORES, half, wide),
            vmem(heads, CORES, n_axis * per_pair, wide),
            vmem(mine, sides, slots, wide),
            vmem(mine, CORES, slots, thin),
            vmem(heads, CORES, half, thin),
            vmem(heads, slots, thin),
            vmem(heads, slots, thin),
            vmem(heads, tokens, thin),
            vmem(slots, tokens),
            vmem(tokens, slots),
            vmem(CORES, half, slots),
            vmem(slots, slots),
            vmem(CORES, 3, slots, slots, dtype=F32),
            vmem(CORES, slots, lane_step, dtype=F32),
            vmem(slots, lane_step, dtype=F32),
            vmem(slots, thin, dtype=F32),
            vmem(n_tok, thin),
            vmem(CORES, n_tok, thin),
            vmem(CORES, n_tok, thin),
            vmem(line * line, thin),
            vmem(sides, n_tok, thin),
            vmem(TILE, thin),
            vmem(CORES, TILE, thin),
            vmem(CORES, slots, thin),
            vmem(sides, slots, thin),
            pltpu.SemaphoreType.DMA((STAGES, heads)),
            pltpu.SemaphoreType.DMA((6, 2)),
            pltpu.SemaphoreType.DMA((2 * CORES,)),
            pltpu.SemaphoreType.DMA,
        ],
        compiler_params=pltpu.CompilerParams(
            collective_id=0, has_side_effects=True, vmem_limit_bytes=60 * 2**20
        ),
    )(queries, key_rows, values, cluster[None, :], owners[None, :], pair_list)


def solution(mesh):
    return jax.shard_map(
        per_device,
        mesh=mesh,
        in_specs=(
            P(("tok", "head"), None),
            P(("tok", "head"), None),
            P(("tok", "head"), None),
            P("tok"),
            P(),
            P("tok", None),
        ),
        out_specs=P(("tok", "head"), None),
        check_vma=False,
    )
```

```python
import functools
import math

import jax
import jax.numpy as jnp
from jax import lax
from jax.experimental import pallas as pl
from jax.experimental.pallas import tpu as pltpu
from jax.sharding import PartitionSpec as P

HEAD_DIM = 128
CAP = 128
CORES = 2
TILE = 16
LANES = 8
AHEAD = 2
MASKED = -(2.0**100)
SCALE_LOG2 = math.log2(math.e) / math.sqrt(HEAD_DIM)
MESH = pl.DeviceIdType.MESH
F32 = jnp.float32
BF16 = jnp.bfloat16

X_OWN, X_SEND, X_RECV, A_SEND, A_RECV, B_SEND, B_NEAR, B_RECV, H_SEND, H_RECV = range(10)
RB_SEND, RB_RECV, RA_SEND, RA_RECV, RX_SEND, RX_OWN = range(10, 16)
STAGES = 16


def matmul(left, right):
    return jnp.dot(left, right, preferred_element_type=F32)


def matmul_t(left, right):
    return lax.dot_general(left, right, (((1,), (1,)), ((), ())), preferred_element_type=F32)


def iota(shape, dim):
    return lax.broadcasted_iota(jnp.int32, shape, dim)


def one_hot(condition):
    return jnp.where(condition, 1.0, 0.0).astype(BF16)


def wait_bytes(ref, sem):
    pltpu.make_async_copy(ref, ref, sem).wait()


def kernel(
    dims, q_ref, k_ref, v_ref, cluster, owners, pair_list, out_ref,
    x_recv, a_send, a_recv, b_send, work, o_send, o_recv, t_send, t_recv, x_back,
    pick, pick_t, perm, perm_t, scores, peak, total, mixed,
    l_a_send, l_a_recv, l_b_send, l_b_recv, labels, mask_tile, mask_in, q_mask, k_mask,
    sem, label_sem, mask_sem, out_sem,
):
    nx, n_axis, per_pair, heads = dims
    rows = q_ref.shape[0]
    tokens = nx * rows
    width = heads * HEAD_DIM
    line = n_axis * CORES
    n_tok = n_axis * line
    slots = n_tok * per_pair
    a_rows = line * per_pair
    b_rows = n_axis * per_pair
    mine = heads // CORES
    sides = CORES + 2
    cl_dev, pairs = pair_list.shape
    invalid = sides * cl_dev
    my_x = lax.axis_index("head")
    tok = lax.axis_index("tok")
    z, y, core = tok // line, (tok // CORES) % n_axis, tok % CORES

    def place(par):
        return z + par * (y - z), y + par * (z - y)

    def device(a, b, c, par):
        return ((a + par * (b - a)) * line + (b + par * (a - b)) * CORES + c, my_x)

    def next_chip(step):
        a, b = place(core)
        chip = lax.rem(a * n_axis + b + n_axis * n_axis + step, n_axis * n_axis)
        return device(chip // n_axis, chip % n_axis, core, core)

    def copy_to(src, dst, send, recv, target):
        pltpu.make_async_remote_copy(
            src_ref=src, dst_ref=dst, send_sem=send, recv_sem=recv,
            device_id=target, device_id_type=MESH,
        ).start()

    def lanes(start, size):
        return pl.ds(pl.multiple_of(start, HEAD_DIM), size)

    def block(index, size):
        return pl.ds(pl.multiple_of(index * size, size), size)

    barrier = pltpu.get_barrier_semaphore()

    def greet(target):
        pl.semaphore_signal(barrier, inc=1, device_id=target, device_id_type=MESH)

    @pl.loop(1, nx)
    def _(d):
        greet((tok, lax.rem(my_x + d, nx)))

    @pl.loop(1, line)
    def _(d):
        greet((z * line + lax.rem(y * CORES + core + d, line), my_x))

    @pl.loop(1, n_axis)
    def _(d):
        for c in range(CORES):
            greet(((lax.rem(z + d, n_axis) * n_axis + y) * CORES + c, my_x))

    greet(next_chip(1))
    greet(next_chip(-1))
    @pl.when(y != z)
    def _():
        for c in range(CORES):
            greet(((y * n_axis + z) * CORES + c, my_x))

    @pl.when(y == z)
    def _():
        for c in range(CORES):
            greet((tok + 1 - 2 * core, my_x))

    greeted = (nx - 1) + (line - 1) + (n_axis - 1) * CORES + 2 + CORES

    def own_copy(ref, kind, h):
        return pltpu.make_async_copy(
            ref.at[:, lanes(my_x * width + h * HEAD_DIM, HEAD_DIM)],
            x_recv.at[h, block(my_x, rows), pl.ds(kind * HEAD_DIM, HEAD_DIM)],
            sem.at[X_OWN, h],
        )

    pl.semaphore_wait(barrier, greeted)

    def spread(h):
        @pl.loop(1, nx)
        def _(d):
            other = lax.rem(my_x + d, nx)
            for kind, ref in enumerate((q_ref, k_ref, v_ref)):
                copy_to(
                    ref.at[:, lanes(other * width + h * HEAD_DIM, HEAD_DIM)],
                    x_recv.at[h, block(my_x, rows), pl.ds(kind * HEAD_DIM, HEAD_DIM)],
                    sem.at[X_SEND, h],
                    sem.at[X_RECV, h],
                    (tok, other),
                )

        for kind, ref in enumerate((q_ref, k_ref, v_ref)):
            own_copy(ref, kind, h).start()

    @pl.loop(0, min(AHEAD, heads))
    def _(h):
        spread(h)

    clusters = owners.shape[1]
    cluster_hot = one_hot(iota((clusters, tokens), 0) == cluster[...])
    table = jnp.where(
        iota((TILE, clusters), 0) == 0, owners[...] // cl_dev, owners[...] % cl_dev
    )
    found = matmul(table.astype(F32).astype(BF16), cluster_hot).astype(jnp.int32)
    target, local_id = found[0:1], found[1:2]
    target_hot = one_hot(iota((n_tok, tokens), 0) == target)
    earlier = one_hot(iota((tokens, tokens), 0) < iota((tokens, tokens), 1))
    rank = jnp.sum(matmul(target_hot, earlier) * target_hot.astype(F32), axis=0, keepdims=True)
    rank = rank.astype(jnp.int32)
    send_row = target * per_pair + rank
    chunk = min(128, tokens)

    @pl.loop(0, slots // chunk)
    def _(i):
        pick[block(i, chunk)] = one_hot(iota((chunk, tokens), 0) + i * chunk == send_row)

    def first_hop(src, dst, send, recv, par, size):
        a, b = place(par)
        pltpu.make_async_copy(src.at[block(a, size)], dst.at[block(a, size)], recv).start()

        @pl.loop(1, n_axis)
        def _(d):
            other = lax.rem(a + d, n_axis)
            copy_to(
                src.at[block(other, size)], dst.at[block(a, size)], send, recv,
                device(other, b, core, par),
            )

    def second_hop(src_at, dst, send, near, recv, par):
        a, b = place(par)

        @pl.when(core == par)
        def _():
            pltpu.make_async_copy(src_at(b), dst, recv).start()

        @pl.when(core != par)
        def _():
            copy_to(src_at(b), dst, near, recv, device(a, b, par, par))

        @pl.loop(1, n_axis)
        def _(d):
            other = lax.rem(b + d, n_axis)
            copy_to(src_at(other), dst, send, recv, device(a, other, par, par))

    def source(par):
        _, b = place(par)
        return b * CORES + core

    others_a = pl.ds(0, slots - a_rows)
    others_b = pl.ds(0, b_rows * (n_axis - 1))
    label_others = pl.ds(0, n_tok - line)

    def pack(h):
        for kind, ref in enumerate((q_ref, k_ref, v_ref)):
            own_copy(ref, kind, h).wait()
        wait_bytes(x_recv.at[h, pl.ds(0, tokens - rows)], sem.at[X_RECV, h])

        @pl.when(h + AHEAD < heads)
        def _():
            spread(h + AHEAD)

        @pl.loop(0, 2)
        def _(i):
            part = block(i, slots // 2)
            a_send[h, part] = matmul(pick[part], x_recv[h]).astype(BF16)

        first_hop(a_send.at[h], a_recv.at[h], sem.at[A_SEND, h], sem.at[A_RECV, h], h % 2, a_rows)

    def turn(h):
        par = h % 2
        wait_bytes(a_recv.at[h], sem.at[A_RECV, h])

        @pl.loop(0, CORES)
        def _(i):
            b_send[h, i] = matmul(perm[i], a_recv[h]).astype(BF16)

        second_hop(
            lambda other: b_send.at[h, :, block(other, b_rows)],
            work.at[h // 2, pl.ds(1, CORES), block(source(par), b_rows)],
            sem.at[B_SEND, h], sem.at[B_NEAR, h], sem.at[B_RECV, h // 2], par,
        )

    def share(k):
        wait_bytes(work.at[k, pl.ds(1, CORES)], sem.at[B_RECV, k])
        for step, src, dst in ((-1, 1, CORES + 1), (1, CORES, 0)):
            copy_to(
                work.at[k, src, :, pl.ds(HEAD_DIM, 2 * HEAD_DIM)],
                work.at[k, dst, :, pl.ds(HEAD_DIM, 2 * HEAD_DIM)],
                sem.at[H_SEND, k], sem.at[H_RECV, k], next_chip(step),
            )

    two_sides = (pl.ds(0, 2), slice(None), pl.ds(HEAD_DIM, 2 * HEAD_DIM))
    tiles = slots // HEAD_DIM if slots >= HEAD_DIM else 1
    lane_step = min(slots, HEAD_DIM)

    def attend(k):
        peak[...] = jnp.full((CORES, slots, lane_step), -jnp.inf, F32)

        @pl.loop(0, 3 * CORES)
        def _(n):
            i = (n // 2) % 2 + n // 5
            part = 1 - i + n % 2 + (n // 4) * (2 * i - 1)

            @pl.when(n == 4)
            def _():
                wait_bytes(work.at[(k, *two_sides)], sem.at[H_RECV, k])

            query = jnp.concatenate([work[k, i + 1, :, 0:HEAD_DIM], q_mask[i]], axis=1)
            key = jnp.concatenate(
                [work[k, i + part, :, HEAD_DIM : 2 * HEAD_DIM], k_mask[i + part]], axis=1
            )
            found = matmul_t(query, key)
            scores[i, part] = found
            peak[i] = functools.reduce(
                jnp.maximum,
                [found[:, t * lane_step : (t + 1) * lane_step] for t in range(tiles)],
                peak[i],
            )

        @pl.loop(0, CORES)
        def _(i):
            row_max = jnp.max(peak[i], axis=1, keepdims=True)
            peak[i] = jnp.broadcast_to(row_max, (slots, lane_step))
            total[...] = jnp.zeros((slots, lane_step), F32)
            mixed[...] = jnp.zeros((slots, HEAD_DIM), F32)

            @pl.loop(0, 3)
            def _(part):
                row_max = peak[i]
                weights = [
                    jnp.exp2(
                        (scores[i, part, :, t * lane_step : (t + 1) * lane_step] - row_max)
                        * SCALE_LOG2
                    )
                    for t in range(tiles)
                ]
                total[...] += functools.reduce(jnp.add, weights)
                rounded = jnp.concatenate([w.astype(BF16) for w in weights], axis=1)
                mixed[...] += matmul(rounded, work[k, i + part, :, 2 * HEAD_DIM : 3 * HEAD_DIM])

            row_total = jnp.sum(total[...], axis=1, keepdims=True)
            o_send[k, i] = (mixed[...] / row_total).astype(BF16)

        h = CORES * k + core
        a, b = place(core)
        here = b * CORES + core
        dst = o_recv.at[h, :, block(b, b_rows)]

        def src(other):
            return o_send.at[k, :, block(other, b_rows)]

        pltpu.make_async_copy(src(here), dst, sem.at[RB_RECV, h]).start()

        @pl.loop(1, line)
        def _(d):
            other = lax.rem(here + d, line)
            copy_to(
                src(other), dst, sem.at[RB_SEND, k], sem.at[RB_RECV, h],
                device(a, other // CORES, other % CORES, core),
            )

    def turn_back(h):
        wait_bytes(o_recv.at[h], sem.at[RB_RECV, h])
        t_send[h] = matmul(perm_t[...], o_recv[h].reshape(slots, HEAD_DIM)).astype(BF16)
        first_hop(
            t_send.at[h], t_recv.at[h], sem.at[RA_SEND, h], sem.at[RA_RECV, h], h % 2, a_rows
        )

    def finish(h):
        wait_bytes(t_recv.at[h], sem.at[RA_RECV, h])
        x_back[h] = matmul(pick_t[...], t_recv[h]).astype(BF16)
        column = lanes(my_x * width + h * HEAD_DIM, HEAD_DIM)
        pltpu.make_async_copy(
            x_back.at[h, block(my_x, rows)], out_ref.at[:, column], sem.at[RX_OWN, h]
        ).start()

        @pl.loop(1, nx)
        def _(d):
            other = lax.rem(my_x + d, nx)
            copy_to(
                x_back.at[h, block(other, rows)], out_ref.at[:, column],
                sem.at[RX_SEND, h], out_sem, (tok, other),
            )

    keepers = [(z * n_axis + y) * CORES, (y * n_axis + z) * CORES + 1]

    def send_labels():
        pair_local = pair_list[...] - (tok - core - 1) * cl_dev
        lane = iota((cl_dev, HEAD_DIM), 1)
        allowed = lane > invalid
        for j in range(pairs):
            allowed = allowed | (pair_local[:, j : j + 1] == lane)
        mask_tile[...] = jnp.concatenate(
            [jnp.where(allowed, 0.0, MASKED), jnp.zeros((TILE - cl_dev, HEAD_DIM), F32)], axis=0
        ).astype(BF16)

        for end, keeper in enumerate(keepers):

            @pl.when(tok == keeper)
            def _():
                pltpu.make_async_copy(
                    mask_tile, mask_in.at[core], mask_sem.at[CORES + core]
                ).start()

            @pl.when(tok != keeper)
            def _():
                copy_to(
                    mask_tile, mask_in.at[core], mask_sem.at[end], mask_sem.at[CORES + core],
                    (keeper, my_x),
                )

        lane = iota((HEAD_DIM, tokens), 0) - rank * LANES
        filled = matmul_t(target_hot, one_hot((lane == local_id) | (lane == cl_dev)))
        lane = iota((n_tok, HEAD_DIM), 1)
        l_a_send[...] = jnp.where(lane % LANES == cl_dev, 1.0 - filled, filled).astype(BF16)

        for par in range(CORES):
            first_hop(
                l_a_send, l_a_recv.at[par], label_sem.at[0, par], label_sem.at[1, par], par, line
            )

    def make_perms():
        half = slots // CORES

        def source_of(row, i):
            r, a, b = row % per_pair, (row // per_pair) % n_axis, row // b_rows
            return a * a_rows + b * (CORES * per_pair) + i * per_pair + r

        for i in range(CORES):
            perm[i] = one_hot(source_of(iota((half, slots), 0), i) == iota((half, slots), 1))

        @pl.loop(0, slots // chunk)
        def _(part):
            row, column = iota((chunk, slots), 0) + part * chunk, iota((chunk, slots), 1)
            perm_t[block(part, chunk)] = one_hot(
                source_of(column % half, column // half) == row
            )

        same = one_hot(iota((tokens, tokens), 0) == iota((tokens, tokens), 1))
        pick_t[...] = matmul_t(same, pick[...]).astype(BF16)

    def turn_labels():
        row, column = iota((n_tok, n_tok), 0), iota((n_tok, n_tok), 1)
        start = (row // CORES) % n_axis * line + row // line * CORES + row % CORES
        turned = one_hot(start == column)
        for par in range(CORES):
            wait_bytes(l_a_recv.at[par], label_sem.at[1, par])
            l_b_send[par] = matmul(turned, l_a_recv[par]).astype(BF16)
            second_hop(
                lambda other: l_b_send.at[par, block(other, line)],
                l_b_recv.at[block(source(par), line)],
                label_sem.at[2, par], label_sem.at[3, par], label_sem.at[4, 0], par,
            )

    def share_labels():
        wait_bytes(l_b_recv, label_sem.at[4, 0])
        shape = (n_tok, line * line)
        row, column = iota(shape, 0), iota(shape, 1)
        start = row // n_axis * line + row % n_axis * CORES
        for i in range(CORES):
            labels[i + 1] = matmul(one_hot(start + i == column), l_b_recv[...]).astype(BF16)
        for step, src, dst in ((-1, 1, CORES + 1), (1, CORES, 0)):
            copy_to(
                labels.at[src], labels.at[dst], label_sem.at[5, 0], label_sem.at[5, 1],
                next_chip(step),
            )

    def make_masks():
        wait_bytes(labels.at[pl.ds(0, 2)], label_sem.at[5, 1])
        for c in range(CORES):
            wait_bytes(mask_in.at[c], mask_sem.at[CORES + c])
        row, column = iota((HEAD_DIM, HEAD_DIM), 0), iota((HEAD_DIM, HEAD_DIM), 1)
        fold = one_hot((row % LANES == column) & (row < per_pair * LANES))
        owner_row = one_hot(iota((slots, n_tok), 0) // per_pair == iota((slots, n_tok), 1))
        shape = (slots, HEAD_DIM)
        own_lanes = iota(shape, 1) // LANES == iota(shape, 0) % per_pair
        rest = jnp.zeros((HEAD_DIM - TILE, HEAD_DIM), BF16)

        @pl.loop(0, sides)
        def _(side):
            spaced = jnp.where(own_lanes, matmul(owner_row, labels[side]), 0.0).astype(BF16)
            label = matmul(spaced, fold).astype(BF16)
            shift = one_hot(
                ((row < cl_dev) & (column == row + cl_dev * side))
                | ((row == cl_dev) & (column == invalid))
            )
            k_mask[side] = matmul(label, shift).astype(BF16)

            @pl.when((side >= 1) & (side <= CORES))
            def _():
                mask = jnp.concatenate([mask_in[side - 1], rest], axis=0)
                q_mask[side - 1] = matmul(label, mask).astype(BF16)

    def both(stage):
        def pair(k):
            @pl.loop(CORES * k, CORES * k + CORES)
            def _(h):
                stage(h)

        return pair

    stages = [(0, both(pack)), (1, both(turn)), (2, share), (4, both(turn_back))]
    stages += [(5, both(finish)), (3, attend)]

    @pl.loop(0, mine + 5)
    def _(step):
        for number, (lag, stage) in enumerate(stages):

            @pl.when((step >= lag) & (step < mine + lag))
            def _():
                stage(step - lag)

            if number == 0:

                @pl.when(step == 0)
                def _():
                    send_labels()
                    make_perms()
                    turn_labels()

        @pl.when(step == 1)
        def _():
            share_labels()

        @pl.when(step == 2)
        def _():
            make_masks()

    wait_bytes(out_ref.at[:, pl.ds(0, (nx - 1) * width)], out_sem)

    @pl.loop(0, heads)
    def _(h):
        wait_bytes(x_recv.at[h, pl.ds(0, tokens - rows)], sem.at[X_SEND, h])
        wait_bytes(a_send.at[h, others_a], sem.at[A_SEND, h])
        wait_bytes(b_send.at[h, :, others_b], sem.at[B_SEND, h])
        wait_bytes(t_send.at[h, others_a], sem.at[RA_SEND, h])
        wait_bytes(x_back.at[h, pl.ds(0, tokens - rows)], sem.at[RX_SEND, h])
        wait_bytes(x_back.at[h, pl.ds(0, rows)], sem.at[RX_OWN, h])

        @pl.when(core != h % 2)
        def _():
            wait_bytes(b_send.at[h, :, pl.ds(0, b_rows)], sem.at[B_NEAR, h])

    @pl.loop(0, mine)
    def _(k):
        wait_bytes(work.at[(k, *two_sides)], sem.at[H_SEND, k])
        wait_bytes(o_send.at[k, :, pl.ds(0, (line - 1) * b_rows)], sem.at[RB_SEND, k])

    for par in range(CORES):
        wait_bytes(l_a_send.at[label_others], label_sem.at[0, par])
        wait_bytes(l_b_send.at[par, label_others], label_sem.at[2, par])

        @pl.when(core != par)
        def _():
            wait_bytes(l_b_send.at[par, pl.ds(0, line)], label_sem.at[3, par])

        @pl.when(tok != keepers[par])
        def _():
            wait_bytes(mask_tile, mask_sem.at[par])

    wait_bytes(labels.at[pl.ds(0, 2)], label_sem.at[5, 0])


def per_device(queries, key_rows, values, cluster, owners, pair_list):
    nx, n_tok = lax.axis_size("head"), lax.axis_size("tok")
    n_axis = math.isqrt(n_tok // CORES)
    cl_dev = pair_list.shape[0]
    per_pair = CAP * cl_dev // n_tok
    rows, features = queries.shape
    heads = features // nx // HEAD_DIM
    tokens = rows * nx
    slots, line = n_tok * per_pair, n_axis * CORES
    mine, sides, half = heads // CORES, CORES + 2, slots // CORES
    wide, thin = 3 * HEAD_DIM, HEAD_DIM
    lane_step = min(slots, HEAD_DIM)

    def vmem(*shape, dtype=BF16):
        return pltpu.VMEM(shape, dtype)

    return pl.pallas_call(
        functools.partial(kernel, (nx, n_axis, per_pair, heads)),
        out_shape=jax.ShapeDtypeStruct((rows, features), BF16),
        in_specs=[pl.BlockSpec(memory_space=pltpu.HBM)] * 3
        + [pl.BlockSpec(memory_space=pltpu.VMEM)] * 3,
        out_specs=pl.BlockSpec(memory_space=pltpu.HBM),
        scratch_shapes=[
            vmem(heads, tokens, wide),
            vmem(heads, slots, wide),
            vmem(heads, slots, wide),
            vmem(heads, CORES, half, wide),
            vmem(mine, sides, slots, wide),
            vmem(mine, CORES, slots, thin),
            vmem(heads, CORES, half, thin),
            vmem(heads, slots, thin),
            vmem(heads, slots, thin),
            vmem(heads, tokens, thin),
            vmem(slots, tokens),
            vmem(tokens, slots),
            vmem(CORES, half, slots),
            vmem(slots, slots),
            vmem(CORES, 3, slots, slots, dtype=F32),
            vmem(CORES, slots, lane_step, dtype=F32),
            vmem(slots, lane_step, dtype=F32),
            vmem(slots, thin, dtype=F32),
            vmem(n_tok, thin),
            vmem(CORES, n_tok, thin),
            vmem(CORES, n_tok, thin),
            vmem(line * line, thin),
            vmem(sides, n_tok, thin),
            vmem(TILE, thin),
            vmem(CORES, TILE, thin),
            vmem(CORES, slots, thin),
            vmem(sides, slots, thin),
            pltpu.SemaphoreType.DMA((STAGES, heads)),
            pltpu.SemaphoreType.DMA((6, 2)),
            pltpu.SemaphoreType.DMA((2 * CORES,)),
            pltpu.SemaphoreType.DMA,
        ],
        compiler_params=pltpu.CompilerParams(
            collective_id=0, has_side_effects=True, vmem_limit_bytes=60 * 2**20
        ),
    )(queries, key_rows, values, cluster[None, :], owners[None, :], pair_list)


def solution(mesh):
    return jax.shard_map(
        per_device,
        mesh=mesh,
        in_specs=(
            P(("tok", "head"), None),
            P(("tok", "head"), None),
            P(("tok", "head"), None),
            P("tok"),
            P(),
            P("tok", None),
        ),
        out_specs=P(("tok", "head"), None),
        check_vma=False,
    )
```

```python
import functools
import math

import jax
import jax.numpy as jnp
from jax import lax
from jax.experimental import pallas as pl
from jax.experimental.pallas import tpu as pltpu
from jax.sharding import PartitionSpec as P

HEAD_DIM = 128
CAP = 128
CORES = 2
TILE = 16
LANES = 8
AHEAD = 2
STEP = 1
MASKED = -(2.0**100)
SCALE_LOG2 = math.log2(math.e) / math.sqrt(HEAD_DIM)
MESH = pl.DeviceIdType.MESH
F32 = jnp.float32
BF16 = jnp.bfloat16

X_OWN, X_SEND, X_RECV, A_SEND, A_RECV, B_SEND, B_NEAR, B_RECV, H_SEND, H_RECV = range(10)
RB_SEND, RB_RECV, RA_SEND, RA_RECV, RX_SEND, RX_OWN = range(10, 16)
STAGES = 16


def matmul(left, right):
    return jnp.dot(left, right, preferred_element_type=F32)


def matmul_t(left, right):
    return lax.dot_general(left, right, (((1,), (1,)), ((), ())), preferred_element_type=F32)


def iota(shape, dim):
    return lax.broadcasted_iota(jnp.int32, shape, dim)


def one_hot(condition):
    return jnp.where(condition, 1.0, 0.0).astype(BF16)


def wait_bytes(ref, sem):
    pltpu.make_async_copy(ref, ref, sem).wait()


def kernel(
    dims, q_ref, k_ref, v_ref, cluster, owners, pair_list, out_ref,
    x_recv, a_send, a_recv, b_send, work, o_send, o_recv, t_send, t_recv, x_back,
    pick, pick_t, perm, perm_t, scores, peak, total, mixed,
    l_a_send, l_a_recv, l_b_send, l_b_recv, labels, mask_tile, mask_in, q_mask, k_mask,
    sem, label_sem, mask_sem, out_sem,
):
    nx, n_axis, per_pair, heads = dims
    rows = q_ref.shape[0]
    tokens = nx * rows
    width = heads * HEAD_DIM
    line = n_axis * CORES
    n_tok = n_axis * line
    slots = n_tok * per_pair
    a_rows = line * per_pair
    b_rows = n_axis * per_pair
    mine = heads // CORES
    sides = CORES + 2
    cl_dev, pairs = pair_list.shape
    invalid = sides * cl_dev
    my_x = lax.axis_index("head")
    tok = lax.axis_index("tok")
    z, y, core = tok // line, (tok // CORES) % n_axis, tok % CORES

    def place(par):
        return z + par * (y - z), y + par * (z - y)

    def device(a, b, c, par):
        return ((a + par * (b - a)) * line + (b + par * (a - b)) * CORES + c, my_x)

    def next_chip(step):
        a, b = place(core)
        chip = lax.rem(a * n_axis + b + n_axis * n_axis + step, n_axis * n_axis)
        return device(chip // n_axis, chip % n_axis, core, core)

    def copy_to(src, dst, send, recv, target):
        pltpu.make_async_remote_copy(
            src_ref=src, dst_ref=dst, send_sem=send, recv_sem=recv,
            device_id=target, device_id_type=MESH,
        ).start()

    def lanes(start, size):
        return pl.ds(pl.multiple_of(start, HEAD_DIM), size)

    def block(index, size):
        return pl.ds(pl.multiple_of(index * size, size), size)

    barrier = pltpu.get_barrier_semaphore()

    def greet(target):
        pl.semaphore_signal(barrier, inc=1, device_id=target, device_id_type=MESH)

    @pl.loop(1, nx)
    def _(d):
        greet((tok, lax.rem(my_x + d, nx)))

    @pl.loop(1, line)
    def _(d):
        greet((z * line + lax.rem(y * CORES + core + d, line), my_x))

    @pl.loop(1, n_axis)
    def _(d):
        for c in range(CORES):
            greet(((lax.rem(z + d, n_axis) * n_axis + y) * CORES + c, my_x))

    greet(next_chip(1))
    greet(next_chip(-1))
    @pl.when(y != z)
    def _():
        for c in range(CORES):
            greet(((y * n_axis + z) * CORES + c, my_x))

    @pl.when(y == z)
    def _():
        for c in range(CORES):
            greet((tok + 1 - 2 * core, my_x))

    greeted = (nx - 1) + (line - 1) + (n_axis - 1) * CORES + 2 + CORES

    def own_copy(ref, kind, h):
        return pltpu.make_async_copy(
            ref.at[:, lanes(my_x * width + h * HEAD_DIM, HEAD_DIM)],
            x_recv.at[h, block(my_x, rows), pl.ds(kind * HEAD_DIM, HEAD_DIM)],
            sem.at[X_OWN, h],
        )

    pl.semaphore_wait(barrier, greeted)

    def spread(h):
        @pl.loop(1, nx)
        def _(d):
            other = lax.rem(my_x + d, nx)
            for kind, ref in enumerate((q_ref, k_ref, v_ref)):
                copy_to(
                    ref.at[:, lanes(other * width + h * HEAD_DIM, HEAD_DIM)],
                    x_recv.at[h, block(my_x, rows), pl.ds(kind * HEAD_DIM, HEAD_DIM)],
                    sem.at[X_SEND, h],
                    sem.at[X_RECV, h],
                    (tok, other),
                )

        for kind, ref in enumerate((q_ref, k_ref, v_ref)):
            own_copy(ref, kind, h).start()

    @pl.loop(0, min(AHEAD, heads))
    def _(h):
        spread(h)

    clusters = owners.shape[1]
    cluster_hot = one_hot(iota((clusters, tokens), 0) == cluster[...])
    table = jnp.where(
        iota((TILE, clusters), 0) == 0, owners[...] // cl_dev, owners[...] % cl_dev
    )
    found = matmul(table.astype(F32).astype(BF16), cluster_hot).astype(jnp.int32)
    target, local_id = found[0:1], found[1:2]
    target_hot = one_hot(iota((n_tok, tokens), 0) == target)
    earlier = one_hot(iota((tokens, tokens), 0) < iota((tokens, tokens), 1))
    rank = jnp.sum(matmul(target_hot, earlier) * target_hot.astype(F32), axis=0, keepdims=True)
    rank = rank.astype(jnp.int32)
    send_row = target * per_pair + rank
    chunk = min(128, tokens)

    @pl.loop(0, slots // chunk)
    def _(i):
        pick[block(i, chunk)] = one_hot(iota((chunk, tokens), 0) + i * chunk == send_row)

    lane = iota((HEAD_DIM, tokens), 0) - rank * LANES
    filled = matmul_t(target_hot, one_hot((lane == local_id) | (lane == cl_dev)))
    lane = iota((n_tok, HEAD_DIM), 1)
    l_a_send[...] = jnp.where(lane % LANES == cl_dev, 1.0 - filled, filled).astype(BF16)

    half_ring = n_axis // 2

    def round_ring(here, step):
        return lax.rem(here + n_axis + step, n_axis)

    def interleave(puts):
        @pl.loop(1, half_ring)
        def _(d):
            for step in (d, -d):
                for put, here in puts:
                    put(round_ring(here, step))

        for put, here in puts:
            put(round_ring(here, half_ring))

    def first_hops(hops, size):
        def start(par, src, dst, send, recv):
            a, b = place(par)
            pltpu.make_async_copy(src.at[block(a, size)], dst.at[block(a, size)], recv).start()

            def put(other):
                copy_to(
                    src.at[block(other, size)], dst.at[block(a, size)], send, recv,
                    device(other, b, core, par),
                )

            return put, a

        interleave([start(par, *hop) for par, hop in enumerate(hops)])

    def second_hops(hops):
        def start(par, src_at, dst, send, near, recv):
            a, b = place(par)

            @pl.when(core == par)
            def _():
                pltpu.make_async_copy(src_at(b), dst, recv).start()

            @pl.when(core != par)
            def _():
                copy_to(src_at(b), dst, near, recv, device(a, b, par, par))

            def put(other):
                copy_to(src_at(other), dst, send, recv, device(a, other, par, par))

            return put, b

        interleave([start(par, *hop) for par, hop in enumerate(hops)])

    def source(par):
        _, b = place(par)
        return b * CORES + core

    others_a = pl.ds(0, slots - a_rows)
    others_b = pl.ds(0, b_rows * (n_axis - 1))
    label_others = pl.ds(0, n_tok - line)

    both = range(CORES)
    first_hops(
        [
            (l_a_send, l_a_recv.at[par], label_sem.at[0, par], label_sem.at[1, par])
            for par in both
        ],
        line,
    )

    def pack(h):
        for kind, ref in enumerate((q_ref, k_ref, v_ref)):
            own_copy(ref, kind, h).wait()
        wait_bytes(x_recv.at[h, pl.ds(0, tokens - rows)], sem.at[X_RECV, h])

        @pl.when(h + AHEAD < heads)
        def _():
            spread(h + AHEAD)

        @pl.loop(0, 2)
        def _(i):
            part = block(i, slots // 2)
            a_send[h, part] = matmul(pick[part], x_recv[h]).astype(BF16)

    def turn(h):
        wait_bytes(a_recv.at[h], sem.at[A_RECV, h])

        @pl.loop(0, CORES)
        def _(i):
            b_send[h, i] = matmul(perm[i], a_recv[h]).astype(BF16)

    def way_of(src, dst, send, recv):
        def stage(k):
            first_hops(
                [
                    (src.at[h], dst.at[h], sem.at[send, h], sem.at[recv, h])
                    for h in (CORES * k + par for par in both)
                ],
                a_rows,
            )

        return stage

    send_a = way_of(a_send, a_recv, A_SEND, A_RECV)
    send_ra = way_of(t_send, t_recv, RA_SEND, RA_RECV)

    def send_b(k):
        def hop(par):
            h = CORES * k + par
            return (
                lambda other: b_send.at[h, :, block(other, b_rows)],
                work.at[k, pl.ds(1, CORES), block(source(par), b_rows)],
                sem.at[B_SEND, h], sem.at[B_NEAR, h], sem.at[B_RECV, k],
            )

        second_hops([hop(par) for par in both])

    def share(k):
        wait_bytes(work.at[k, pl.ds(1, CORES)], sem.at[B_RECV, k])
        for step, src, dst in ((-1, 1, CORES + 1), (1, CORES, 0)):
            copy_to(
                work.at[k, src, :, pl.ds(HEAD_DIM, 2 * HEAD_DIM)],
                work.at[k, dst, :, pl.ds(HEAD_DIM, 2 * HEAD_DIM)],
                sem.at[H_SEND, k], sem.at[H_RECV, k], next_chip(step),
            )

    two_sides = (pl.ds(0, 2), slice(None), pl.ds(HEAD_DIM, 2 * HEAD_DIM))
    tiles = slots // HEAD_DIM if slots >= HEAD_DIM else 1
    lane_step = min(slots, HEAD_DIM)

    def attend(k):
        peak[...] = jnp.full((CORES, slots, lane_step), -jnp.inf, F32)

        @pl.loop(0, 3 * CORES)
        def _(n):
            i = (n // 2) % 2 + n // 5
            part = 1 - i + n % 2 + (n // 4) * (2 * i - 1)

            @pl.when(n == 4)
            def _():
                wait_bytes(work.at[(k, *two_sides)], sem.at[H_RECV, k])

            query = jnp.concatenate([work[k, i + 1, :, 0:HEAD_DIM], q_mask[i]], axis=1)
            key = jnp.concatenate(
                [work[k, i + part, :, HEAD_DIM : 2 * HEAD_DIM], k_mask[i + part]], axis=1
            )
            found = matmul_t(query, key)
            scores[i, part] = found
            peak[i] = functools.reduce(
                jnp.maximum,
                [found[:, t * lane_step : (t + 1) * lane_step] for t in range(tiles)],
                peak[i],
            )

        @pl.loop(0, CORES)
        def _(i):
            row_max = jnp.max(peak[i], axis=1, keepdims=True)
            peak[i] = jnp.broadcast_to(row_max, (slots, lane_step))
            total[...] = jnp.zeros((slots, lane_step), F32)
            mixed[...] = jnp.zeros((slots, HEAD_DIM), F32)

            @pl.loop(0, 3)
            def _(part):
                row_max = peak[i]
                weights = [
                    jnp.exp2(
                        (scores[i, part, :, t * lane_step : (t + 1) * lane_step] - row_max)
                        * SCALE_LOG2
                    )
                    for t in range(tiles)
                ]
                total[...] += functools.reduce(jnp.add, weights)
                rounded = jnp.concatenate([w.astype(BF16) for w in weights], axis=1)
                mixed[...] += matmul(rounded, work[k, i + part, :, 2 * HEAD_DIM : 3 * HEAD_DIM])

            row_total = jnp.sum(total[...], axis=1, keepdims=True)
            o_send[k, i] = (mixed[...] / row_total).astype(BF16)

        h = CORES * k + core
        a, b = place(core)
        here = b * CORES + core
        dst = o_recv.at[h, :, block(b, b_rows)]

        def src(other):
            return o_send.at[k, :, block(other, b_rows)]

        pltpu.make_async_copy(src(here), dst, sem.at[RB_RECV, h]).start()

        @pl.loop(1, line)
        def _(d):
            other = lax.rem(here + d, line)
            copy_to(
                src(other), dst, sem.at[RB_SEND, k], sem.at[RB_RECV, h],
                device(a, other // CORES, other % CORES, core),
            )

    def turn_back(h):
        wait_bytes(o_recv.at[h], sem.at[RB_RECV, h])
        t_send[h] = matmul(perm_t[...], o_recv[h].reshape(slots, HEAD_DIM)).astype(BF16)

    def finish(h):
        wait_bytes(t_recv.at[h], sem.at[RA_RECV, h])
        x_back[h] = matmul(pick_t[...], t_recv[h]).astype(BF16)
        column = lanes(my_x * width + h * HEAD_DIM, HEAD_DIM)
        pltpu.make_async_copy(
            x_back.at[h, block(my_x, rows)], out_ref.at[:, column], sem.at[RX_OWN, h]
        ).start()

        @pl.loop(1, nx)
        def _(d):
            other = lax.rem(my_x + d, nx)
            copy_to(
                x_back.at[h, block(other, rows)], out_ref.at[:, column],
                sem.at[RX_SEND, h], out_sem, (tok, other),
            )

    keepers = [(z * n_axis + y) * CORES, (y * n_axis + z) * CORES + 1]

    def send_masks():
        pair_local = pair_list[...] - (tok - core - 1) * cl_dev
        lane = iota((cl_dev, HEAD_DIM), 1)
        allowed = lane > invalid
        for j in range(pairs):
            allowed = allowed | (pair_local[:, j : j + 1] == lane)
        mask_tile[...] = jnp.concatenate(
            [jnp.where(allowed, 0.0, MASKED), jnp.zeros((TILE - cl_dev, HEAD_DIM), F32)], axis=0
        ).astype(BF16)

        for end, keeper in enumerate(keepers):

            @pl.when(tok == keeper)
            def _():
                pltpu.make_async_copy(
                    mask_tile, mask_in.at[core], mask_sem.at[CORES + core]
                ).start()

            @pl.when(tok != keeper)
            def _():
                copy_to(
                    mask_tile, mask_in.at[core], mask_sem.at[end], mask_sem.at[CORES + core],
                    (keeper, my_x),
                )

    def make_perms():
        half = slots // CORES

        def source_of(row, i):
            r, a, b = row % per_pair, (row // per_pair) % n_axis, row // b_rows
            return a * a_rows + b * (CORES * per_pair) + i * per_pair + r

        for i in range(CORES):
            perm[i] = one_hot(source_of(iota((half, slots), 0), i) == iota((half, slots), 1))

        @pl.loop(0, slots // chunk)
        def _(part):
            row, column = iota((chunk, slots), 0) + part * chunk, iota((chunk, slots), 1)
            perm_t[block(part, chunk)] = one_hot(
                source_of(column % half, column // half) == row
            )

        same = one_hot(iota((tokens, tokens), 0) == iota((tokens, tokens), 1))
        pick_t[...] = matmul_t(same, pick[...]).astype(BF16)

    def turn_labels():
        row, column = iota((n_tok, n_tok), 0), iota((n_tok, n_tok), 1)
        start = (row // CORES) % n_axis * line + row // line * CORES + row % CORES
        turned = one_hot(start == column)
        for par in both:
            wait_bytes(l_a_recv.at[par], label_sem.at[1, par])
            l_b_send[par] = matmul(turned, l_a_recv[par]).astype(BF16)

        def hop(par):
            return (
                lambda other: l_b_send.at[par, block(other, line)],
                l_b_recv.at[block(source(par), line)],
                label_sem.at[2, par], label_sem.at[3, par], label_sem.at[4, 0],
            )

        second_hops([hop(par) for par in both])

    def share_labels():
        wait_bytes(l_b_recv, label_sem.at[4, 0])
        shape = (n_tok, line * line)
        row, column = iota(shape, 0), iota(shape, 1)
        start = row // n_axis * line + row % n_axis * CORES
        for i in range(CORES):
            labels[i + 1] = matmul(one_hot(start + i == column), l_b_recv[...]).astype(BF16)
        for step, src, dst in ((-1, 1, CORES + 1), (1, CORES, 0)):
            copy_to(
                labels.at[src], labels.at[dst], label_sem.at[5, 0], label_sem.at[5, 1],
                next_chip(step),
            )

    def make_masks():
        wait_bytes(labels.at[pl.ds(0, 2)], label_sem.at[5, 1])
        for c in range(CORES):
            wait_bytes(mask_in.at[c], mask_sem.at[CORES + c])
        row, column = iota((HEAD_DIM, HEAD_DIM), 0), iota((HEAD_DIM, HEAD_DIM), 1)
        fold = one_hot((row % LANES == column) & (row < per_pair * LANES))
        owner_row = one_hot(iota((slots, n_tok), 0) // per_pair == iota((slots, n_tok), 1))
        shape = (slots, HEAD_DIM)
        own_lanes = iota(shape, 1) // LANES == iota(shape, 0) % per_pair
        rest = jnp.zeros((HEAD_DIM - TILE, HEAD_DIM), BF16)

        @pl.loop(0, sides)
        def _(side):
            spaced = jnp.where(own_lanes, matmul(owner_row, labels[side]), 0.0).astype(BF16)
            label = matmul(spaced, fold).astype(BF16)
            shift = one_hot(
                ((row < cl_dev) & (column == row + cl_dev * side))
                | ((row == cl_dev) & (column == invalid))
            )
            k_mask[side] = matmul(label, shift).astype(BF16)

            @pl.when((side >= 1) & (side <= CORES))
            def _():
                mask = jnp.concatenate([mask_in[side - 1], rest], axis=0)
                q_mask[side - 1] = matmul(label, mask).astype(BF16)

    def pair(stage, send=None):
        def stage_of_pair(k):
            @pl.loop(CORES * k, CORES * k + CORES)
            def _(h):
                stage(h)

            if send is not None:
                send(k)

        return stage_of_pair

    stages = (
        pair(pack, send_a), pair(turn, send_b), share, attend,
        pair(turn_back, send_ra), pair(finish),
    )

    @pl.loop(0, mine + STEP * (len(stages) - 1))
    def _(step):
        for number, stage in enumerate(stages):
            lag = STEP * number

            @pl.when((step >= lag) & (step < mine + lag))
            def _():
                stage(step - lag)

            if number == 0:

                @pl.when(step == 0)
                def _():
                    make_perms()
                    turn_labels()
                    send_masks()

        @pl.when(step == 1)
        def _():
            share_labels()

        @pl.when(step == 2)
        def _():
            make_masks()

    wait_bytes(out_ref.at[:, pl.ds(0, (nx - 1) * width)], out_sem)

    @pl.loop(0, heads)
    def _(h):
        wait_bytes(x_recv.at[h, pl.ds(0, tokens - rows)], sem.at[X_SEND, h])
        wait_bytes(a_send.at[h, others_a], sem.at[A_SEND, h])
        wait_bytes(b_send.at[h, :, others_b], sem.at[B_SEND, h])
        wait_bytes(t_send.at[h, others_a], sem.at[RA_SEND, h])
        wait_bytes(x_back.at[h, pl.ds(0, tokens - rows)], sem.at[RX_SEND, h])
        wait_bytes(x_back.at[h, pl.ds(0, rows)], sem.at[RX_OWN, h])

        @pl.when(core != h % 2)
        def _():
            wait_bytes(b_send.at[h, :, pl.ds(0, b_rows)], sem.at[B_NEAR, h])

    @pl.loop(0, mine)
    def _(k):
        wait_bytes(work.at[(k, *two_sides)], sem.at[H_SEND, k])
        wait_bytes(o_send.at[k, :, pl.ds(0, (line - 1) * b_rows)], sem.at[RB_SEND, k])

    for par in range(CORES):
        wait_bytes(l_a_send.at[label_others], label_sem.at[0, par])
        wait_bytes(l_b_send.at[par, label_others], label_sem.at[2, par])

        @pl.when(core != par)
        def _():
            wait_bytes(l_b_send.at[par, pl.ds(0, line)], label_sem.at[3, par])

        @pl.when(tok != keepers[par])
        def _():
            wait_bytes(mask_tile, mask_sem.at[par])

    wait_bytes(labels.at[pl.ds(0, 2)], label_sem.at[5, 0])


def per_device(queries, key_rows, values, cluster, owners, pair_list):
    nx, n_tok = lax.axis_size("head"), lax.axis_size("tok")
    n_axis = math.isqrt(n_tok // CORES)
    cl_dev = pair_list.shape[0]
    per_pair = CAP * cl_dev // n_tok
    rows, features = queries.shape
    heads = features // nx // HEAD_DIM
    tokens = rows * nx
    slots, line = n_tok * per_pair, n_axis * CORES
    mine, sides, half = heads // CORES, CORES + 2, slots // CORES
    wide, thin = 3 * HEAD_DIM, HEAD_DIM
    lane_step = min(slots, HEAD_DIM)

    def vmem(*shape, dtype=BF16):
        return pltpu.VMEM(shape, dtype)

    return pl.pallas_call(
        functools.partial(kernel, (nx, n_axis, per_pair, heads)),
        out_shape=jax.ShapeDtypeStruct((rows, features), BF16),
        in_specs=[pl.BlockSpec(memory_space=pltpu.HBM)] * 3
        + [pl.BlockSpec(memory_space=pltpu.VMEM)] * 3,
        out_specs=pl.BlockSpec(memory_space=pltpu.HBM),
        scratch_shapes=[
            vmem(heads, tokens, wide),
            vmem(heads, slots, wide),
            vmem(heads, slots, wide),
            vmem(heads, CORES, half, wide),
            vmem(mine, sides, slots, wide),
            vmem(mine, CORES, slots, thin),
            vmem(heads, CORES, half, thin),
            vmem(heads, slots, thin),
            vmem(heads, slots, thin),
            vmem(heads, tokens, thin),
            vmem(slots, tokens),
            vmem(tokens, slots),
            vmem(CORES, half, slots),
            vmem(slots, slots),
            vmem(CORES, 3, slots, slots, dtype=F32),
            vmem(CORES, slots, lane_step, dtype=F32),
            vmem(slots, lane_step, dtype=F32),
            vmem(slots, thin, dtype=F32),
            vmem(n_tok, thin),
            vmem(CORES, n_tok, thin),
            vmem(CORES, n_tok, thin),
            vmem(line * line, thin),
            vmem(sides, n_tok, thin),
            vmem(TILE, thin),
            vmem(CORES, TILE, thin),
            vmem(CORES, slots, thin),
            vmem(sides, slots, thin),
            pltpu.SemaphoreType.DMA((STAGES, heads)),
            pltpu.SemaphoreType.DMA((6, 2)),
            pltpu.SemaphoreType.DMA((2 * CORES,)),
            pltpu.SemaphoreType.DMA,
        ],
        compiler_params=pltpu.CompilerParams(
            collective_id=0, has_side_effects=True, vmem_limit_bytes=60 * 2**20
        ),
    )(queries, key_rows, values, cluster[None, :], owners[None, :], pair_list)


def solution(mesh):
    return jax.shard_map(
        per_device,
        mesh=mesh,
        in_specs=(
            P(("tok", "head"), None),
            P(("tok", "head"), None),
            P(("tok", "head"), None),
            P("tok"),
            P(),
            P("tok", None),
        ),
        out_specs=P(("tok", "head"), None),
        check_vma=False,
    )
```

```python
import functools
import math

import jax
import jax.numpy as jnp
from jax import lax
from jax.experimental import pallas as pl
from jax.experimental.pallas import tpu as pltpu
from jax.sharding import PartitionSpec as P

HEAD_DIM = 128
CAP = 128
CORES = 2
TILE = 16
LANES = 8
AHEAD = 2
STEP = 1
MASKED = -(2.0**100)
SCALE_LOG2 = math.log2(math.e) / math.sqrt(HEAD_DIM)
MESH = pl.DeviceIdType.MESH
F32 = jnp.float32
BF16 = jnp.bfloat16

X_OWN, X_SEND, X_RECV, A_SEND, A_RECV, B_SEND, B_NEAR, B_RECV, H_SEND, H_RECV = range(10)
RB_SEND, RB_RECV, RA_SEND, RA_RECV, RX_SEND, RX_OWN = range(10, 16)
STAGES = 16


def matmul(left, right):
    return jnp.dot(left, right, preferred_element_type=F32)


def matmul_t(left, right):
    return lax.dot_general(left, right, (((1,), (1,)), ((), ())), preferred_element_type=F32)


def iota(shape, dim):
    return lax.broadcasted_iota(jnp.int32, shape, dim)


def one_hot(condition):
    return jnp.where(condition, 1.0, 0.0).astype(BF16)


def wait_bytes(ref, sem):
    pltpu.make_async_copy(ref, ref, sem).wait()


def kernel(
    dims, q_ref, k_ref, v_ref, cluster, owners, pair_list, out_ref,
    x_recv, a_send, a_recv, b_send, work, o_send, o_recv, t_send, t_recv, x_back,
    pick, pick_t, perm, perm_t, scores, peak, total, mixed,
    l_a_send, l_a_recv, l_b_send, l_b_recv, labels, mask_tile, mask_in, q_mask, k_mask,
    sem, label_sem, mask_sem, out_sem,
):
    nx, n_axis, per_pair, heads = dims
    rows = q_ref.shape[0]
    tokens = nx * rows
    width = heads * HEAD_DIM
    line = n_axis * CORES
    n_tok = n_axis * line
    slots = n_tok * per_pair
    a_rows = line * per_pair
    b_rows = n_axis * per_pair
    mine = heads // CORES
    sides = CORES + 2
    cl_dev, pairs = pair_list.shape
    invalid = sides * cl_dev
    my_x = lax.axis_index("head")
    tok = lax.axis_index("tok")
    z, y, core = tok // line, (tok // CORES) % n_axis, tok % CORES

    def place(par):
        return z + par * (y - z), y + par * (z - y)

    def device(a, b, c, par):
        return ((a + par * (b - a)) * line + (b + par * (a - b)) * CORES + c, my_x)

    def next_chip(step):
        a, b = place(core)
        chip = lax.rem(a * n_axis + b + n_axis * n_axis + step, n_axis * n_axis)
        return device(chip // n_axis, chip % n_axis, core, core)

    def copy_to(src, dst, send, recv, target):
        pltpu.make_async_remote_copy(
            src_ref=src, dst_ref=dst, send_sem=send, recv_sem=recv,
            device_id=target, device_id_type=MESH,
        ).start()

    def lanes(start, size):
        return pl.ds(pl.multiple_of(start, HEAD_DIM), size)

    def block(index, size):
        return pl.ds(pl.multiple_of(index * size, size), size)

    barrier = pltpu.get_barrier_semaphore()

    def greet(target):
        pl.semaphore_signal(barrier, inc=1, device_id=target, device_id_type=MESH)

    @pl.loop(1, nx)
    def _(d):
        greet((tok, lax.rem(my_x + d, nx)))

    @pl.loop(1, line)
    def _(d):
        greet((z * line + lax.rem(y * CORES + core + d, line), my_x))

    @pl.loop(1, n_axis)
    def _(d):
        for c in range(CORES):
            greet(((lax.rem(z + d, n_axis) * n_axis + y) * CORES + c, my_x))

    greet(next_chip(1))
    greet(next_chip(-1))
    @pl.when(y != z)
    def _():
        for c in range(CORES):
            greet(((y * n_axis + z) * CORES + c, my_x))

    @pl.when(y == z)
    def _():
        for c in range(CORES):
            greet((tok + 1 - 2 * core, my_x))

    greeted = (nx - 1) + (line - 1) + (n_axis - 1) * CORES + 2 + CORES

    def own_copy(ref, kind, h):
        return pltpu.make_async_copy(
            ref.at[:, lanes(my_x * width + h * HEAD_DIM, HEAD_DIM)],
            x_recv.at[h, block(my_x, rows), pl.ds(kind * HEAD_DIM, HEAD_DIM)],
            sem.at[X_OWN, h],
        )

    pl.semaphore_wait(barrier, greeted)

    def spread(h):
        @pl.loop(1, nx)
        def _(d):
            other = lax.rem(my_x + d, nx)
            for kind, ref in enumerate((q_ref, k_ref, v_ref)):
                copy_to(
                    ref.at[:, lanes(other * width + h * HEAD_DIM, HEAD_DIM)],
                    x_recv.at[h, block(my_x, rows), pl.ds(kind * HEAD_DIM, HEAD_DIM)],
                    sem.at[X_SEND, h],
                    sem.at[X_RECV, h],
                    (tok, other),
                )

    @pl.loop(0, min(AHEAD, heads))
    def _(h):
        spread(h)

    @pl.loop(0, heads)
    def _(h):
        for kind, ref in enumerate((q_ref, k_ref, v_ref)):
            own_copy(ref, kind, h).start()

    pair_local = pair_list[...] - (tok - core - 1) * cl_dev
    lane = iota((cl_dev, HEAD_DIM), 1)
    allowed = lane > invalid
    for j in range(pairs):
        allowed = allowed | (pair_local[:, j : j + 1] == lane)
    mask_tile[...] = jnp.concatenate(
        [jnp.where(allowed, 0.0, MASKED), jnp.zeros((TILE - cl_dev, HEAD_DIM), F32)], axis=0
    ).astype(BF16)

    keepers = [(z * n_axis + y) * CORES, (y * n_axis + z) * CORES + 1]
    for end, keeper in enumerate(keepers):

        @pl.when(tok == keeper)
        def _():
            pltpu.make_async_copy(
                mask_tile, mask_in.at[core], mask_sem.at[CORES + core]
            ).start()

        @pl.when(tok != keeper)
        def _():
            copy_to(
                mask_tile, mask_in.at[core], mask_sem.at[end], mask_sem.at[CORES + core],
                (keeper, my_x),
            )

    clusters = owners.shape[1]
    cluster_hot = one_hot(iota((clusters, tokens), 0) == cluster[...])
    table = jnp.where(
        iota((TILE, clusters), 0) == 0, owners[...] // cl_dev, owners[...] % cl_dev
    )
    found = matmul(table.astype(F32).astype(BF16), cluster_hot).astype(jnp.int32)
    target, local_id = found[0:1], found[1:2]
    target_hot = one_hot(iota((n_tok, tokens), 0) == target)
    earlier = one_hot(iota((tokens, tokens), 0) < iota((tokens, tokens), 1))
    rank = jnp.sum(matmul(target_hot, earlier) * target_hot.astype(F32), axis=0, keepdims=True)
    rank = rank.astype(jnp.int32)
    send_row = target * per_pair + rank
    chunk = min(128, tokens)

    @pl.loop(0, slots // chunk)
    def _(i):
        pick[block(i, chunk)] = one_hot(iota((chunk, tokens), 0) + i * chunk == send_row)

    lane = iota((HEAD_DIM, tokens), 0) - rank * LANES
    filled = matmul_t(target_hot, one_hot((lane == local_id) | (lane == cl_dev)))
    lane = iota((n_tok, HEAD_DIM), 1)
    l_a_send[...] = jnp.where(lane % LANES == cl_dev, 1.0 - filled, filled).astype(BF16)

    def first_hop(src, dst, send, recv, par, size):
        a, b = place(par)
        pltpu.make_async_copy(src.at[block(a, size)], dst.at[block(a, size)], recv).start()

        @pl.loop(1, n_axis)
        def _(d):
            other = lax.rem(a + d, n_axis)
            copy_to(
                src.at[block(other, size)], dst.at[block(a, size)], send, recv,
                device(other, b, core, par),
            )

    def second_hop(src_at, dst, send, near, recv, par):
        a, b = place(par)

        @pl.when(core == par)
        def _():
            pltpu.make_async_copy(src_at(b), dst, recv).start()

        @pl.when(core != par)
        def _():
            copy_to(src_at(b), dst, near, recv, device(a, b, par, par))

        @pl.loop(1, n_axis)
        def _(d):
            other = lax.rem(b + d, n_axis)
            copy_to(src_at(other), dst, send, recv, device(a, other, par, par))

    def source(par):
        _, b = place(par)
        return b * CORES + core

    others_a = pl.ds(0, slots - a_rows)
    others_b = pl.ds(0, b_rows * (n_axis - 1))
    label_others = pl.ds(0, n_tok - line)

    for par in range(CORES):
        first_hop(
            l_a_send, l_a_recv.at[par], label_sem.at[0, par], label_sem.at[1, par], par, line
        )

    def pack(h):
        for kind, ref in enumerate((q_ref, k_ref, v_ref)):
            own_copy(ref, kind, h).wait()
        wait_bytes(x_recv.at[h, pl.ds(0, tokens - rows)], sem.at[X_RECV, h])

        @pl.when(h + AHEAD < heads)
        def _():
            spread(h + AHEAD)

        @pl.loop(0, 2)
        def _(i):
            part = block(i, slots // 2)
            a_send[h, part] = matmul(pick[part], x_recv[h]).astype(BF16)

        first_hop(a_send.at[h], a_recv.at[h], sem.at[A_SEND, h], sem.at[A_RECV, h], h % 2, a_rows)

    def turn(h):
        par = h % 2
        wait_bytes(a_recv.at[h], sem.at[A_RECV, h])

        @pl.loop(0, CORES)
        def _(i):
            b_send[h, i] = matmul(perm[i], a_recv[h]).astype(BF16)

        second_hop(
            lambda other: b_send.at[h, :, block(other, b_rows)],
            work.at[h // 2, pl.ds(1, CORES), block(source(par), b_rows)],
            sem.at[B_SEND, h], sem.at[B_NEAR, h], sem.at[B_RECV, h // 2], par,
        )

    def share(k):
        wait_bytes(work.at[k, pl.ds(1, CORES)], sem.at[B_RECV, k])
        for step, src, dst in ((-1, 1, CORES + 1), (1, CORES, 0)):
            copy_to(
                work.at[k, src, :, pl.ds(HEAD_DIM, 2 * HEAD_DIM)],
                work.at[k, dst, :, pl.ds(HEAD_DIM, 2 * HEAD_DIM)],
                sem.at[H_SEND, k], sem.at[H_RECV, k], next_chip(step),
            )

    two_sides = (pl.ds(0, 2), slice(None), pl.ds(HEAD_DIM, 2 * HEAD_DIM))
    tiles = slots // HEAD_DIM if slots >= HEAD_DIM else 1
    lane_step = min(slots, HEAD_DIM)

    def attend(k):
        peak[...] = jnp.full((CORES, slots, lane_step), -jnp.inf, F32)

        @pl.loop(0, 3 * CORES)
        def _(n):
            i = (n // 2) % 2 + n // 5
            part = 1 - i + n % 2 + (n // 4) * (2 * i - 1)

            @pl.when(n == 4)
            def _():
                wait_bytes(work.at[(k, *two_sides)], sem.at[H_RECV, k])

            query = jnp.concatenate([work[k, i + 1, :, 0:HEAD_DIM], q_mask[i]], axis=1)
            key = jnp.concatenate(
                [work[k, i + part, :, HEAD_DIM : 2 * HEAD_DIM], k_mask[i + part]], axis=1
            )
            found = matmul_t(query, key)
            scores[i, part] = found
            peak[i] = functools.reduce(
                jnp.maximum,
                [found[:, t * lane_step : (t + 1) * lane_step] for t in range(tiles)],
                peak[i],
            )

        @pl.loop(0, CORES)
        def _(i):
            row_max = jnp.max(peak[i], axis=1, keepdims=True)
            peak[i] = jnp.broadcast_to(row_max, (slots, lane_step))
            total[...] = jnp.zeros((slots, lane_step), F32)
            mixed[...] = jnp.zeros((slots, HEAD_DIM), F32)

            @pl.loop(0, 3)
            def _(part):
                row_max = peak[i]
                weights = [
                    jnp.exp2(
                        (scores[i, part, :, t * lane_step : (t + 1) * lane_step] - row_max)
                        * SCALE_LOG2
                    )
                    for t in range(tiles)
                ]
                total[...] += functools.reduce(jnp.add, weights)
                rounded = jnp.concatenate([w.astype(BF16) for w in weights], axis=1)
                mixed[...] += matmul(rounded, work[k, i + part, :, 2 * HEAD_DIM : 3 * HEAD_DIM])

            row_total = jnp.sum(total[...], axis=1, keepdims=True)
            o_send[k, i] = (mixed[...] / row_total).astype(BF16)

        h = CORES * k + core
        a, b = place(core)
        here = b * CORES + core
        dst = o_recv.at[h, :, block(b, b_rows)]

        def src(other):
            return o_send.at[k, :, block(other, b_rows)]

        pltpu.make_async_copy(src(here), dst, sem.at[RB_RECV, h]).start()

        @pl.loop(1, line)
        def _(d):
            other = lax.rem(here + d, line)
            copy_to(
                src(other), dst, sem.at[RB_SEND, k], sem.at[RB_RECV, h],
                device(a, other // CORES, other % CORES, core),
            )

    def turn_back(h):
        wait_bytes(o_recv.at[h], sem.at[RB_RECV, h])

        @pl.loop(0, 2)
        def _(i):
            part = block(i, slots // 2)
            returned = o_recv[h].reshape(slots, HEAD_DIM)
            t_send[h, part] = matmul(perm_t[part], returned).astype(BF16)

        first_hop(
            t_send.at[h], t_recv.at[h], sem.at[RA_SEND, h], sem.at[RA_RECV, h], h % 2, a_rows
        )

    def finish(h):
        wait_bytes(t_recv.at[h], sem.at[RA_RECV, h])
        x_back[h] = matmul(pick_t[...], t_recv[h]).astype(BF16)
        column = lanes(my_x * width + h * HEAD_DIM, HEAD_DIM)
        pltpu.make_async_copy(
            x_back.at[h, block(my_x, rows)], out_ref.at[:, column], sem.at[RX_OWN, h]
        ).start()

        @pl.loop(1, nx)
        def _(d):
            other = lax.rem(my_x + d, nx)
            copy_to(
                x_back.at[h, block(other, rows)], out_ref.at[:, column],
                sem.at[RX_SEND, h], out_sem, (tok, other),
            )

    def make_perms():
        half = slots // CORES

        def source_of(row, i):
            r, a, b = row % per_pair, (row // per_pair) % n_axis, row // b_rows
            return a * a_rows + b * (CORES * per_pair) + i * per_pair + r

        piece = min(chunk, half)

        @pl.loop(0, slots // piece)
        def _(part):
            row, column = iota((piece, slots), 0) + part * piece, iota((piece, slots), 1)
            i, start = part * piece // half, part * piece % half
            rows_here = pl.ds(pl.multiple_of(start, piece), piece)
            perm[i, rows_here] = one_hot(source_of(row % half, i) == column)
            perm_t[block(part, piece)] = one_hot(
                source_of(column % half, column // half) == row
            )

        same = one_hot(iota((tokens, tokens), 0) == iota((tokens, tokens), 1))
        pick_t[...] = matmul_t(same, pick[...]).astype(BF16)

    def turn_labels():
        row, column = iota((n_tok, n_tok), 0), iota((n_tok, n_tok), 1)
        start = (row // CORES) % n_axis * line + row // line * CORES + row % CORES
        turned = one_hot(start == column)
        for par in range(CORES):
            wait_bytes(l_a_recv.at[par], label_sem.at[1, par])
            l_b_send[par] = matmul(turned, l_a_recv[par]).astype(BF16)
            second_hop(
                lambda other: l_b_send.at[par, block(other, line)],
                l_b_recv.at[block(source(par), line)],
                label_sem.at[2, par], label_sem.at[3, par], label_sem.at[4, 0], par,
            )

    def share_labels():
        wait_bytes(l_b_recv, label_sem.at[4, 0])
        shape = (n_tok, line * line)
        row, column = iota(shape, 0), iota(shape, 1)
        start = row // n_axis * line + row % n_axis * CORES
        for i in range(CORES):
            labels[i + 1] = matmul(one_hot(start + i == column), l_b_recv[...]).astype(BF16)
        for step, src, dst in ((-1, 1, CORES + 1), (1, CORES, 0)):
            copy_to(
                labels.at[src], labels.at[dst], label_sem.at[5, 0], label_sem.at[5, 1],
                next_chip(step),
            )

    def make_masks():
        wait_bytes(labels.at[pl.ds(0, 2)], label_sem.at[5, 1])
        for c in range(CORES):
            wait_bytes(mask_in.at[c], mask_sem.at[CORES + c])
        row, column = iota((HEAD_DIM, HEAD_DIM), 0), iota((HEAD_DIM, HEAD_DIM), 1)
        fold = one_hot((row % LANES == column) & (row < per_pair * LANES))
        rest = jnp.zeros((HEAD_DIM - TILE, HEAD_DIM), BF16)
        piece = min(chunk, slots)

        @pl.loop(0, sides * (slots // piece))
        def _(n):
            side, start = n // (slots // piece), n % (slots // piece) * piece
            here = pl.ds(pl.multiple_of(start, piece), piece)
            owner = (iota((piece, n_tok), 0) + start) // per_pair
            owner_row = one_hot(owner == iota((piece, n_tok), 1))
            shape = (piece, HEAD_DIM)
            own_lanes = iota(shape, 1) // LANES == iota(shape, 0) % per_pair
            spaced = jnp.where(own_lanes, matmul(owner_row, labels[side]), 0.0).astype(BF16)
            label = matmul(spaced, fold).astype(BF16)
            shift = one_hot(
                ((row < cl_dev) & (column == row + cl_dev * side))
                | ((row == cl_dev) & (column == invalid))
            )
            k_mask[side, here] = matmul(label, shift).astype(BF16)

            @pl.when((side >= 1) & (side <= CORES))
            def _():
                mask = jnp.concatenate([mask_in[side - 1], rest], axis=0)
                q_mask[side - 1, here] = matmul(label, mask).astype(BF16)

    def both(stage):
        def pair(k):
            @pl.loop(CORES * k, CORES * k + CORES)
            def _(h):
                stage(h)

        return pair

    stages = (both(pack), both(turn), share, attend, both(turn_back), both(finish))

    @pl.loop(0, mine + STEP * (len(stages) - 1))
    def _(step):
        for number, stage in enumerate(stages):
            lag = STEP * number

            @pl.when((step >= lag) & (step < mine + lag))
            def _():
                stage(step - lag)

            if number == 0:

                @pl.when(step == 0)
                def _():
                    make_perms()
                    turn_labels()

        @pl.when(step == 1)
        def _():
            share_labels()

        @pl.when(step == 2)
        def _():
            make_masks()

    wait_bytes(out_ref.at[:, pl.ds(0, (nx - 1) * width)], out_sem)

    @pl.loop(0, heads)
    def _(h):
        wait_bytes(x_recv.at[h, pl.ds(0, tokens - rows)], sem.at[X_SEND, h])
        wait_bytes(a_send.at[h, others_a], sem.at[A_SEND, h])
        wait_bytes(b_send.at[h, :, others_b], sem.at[B_SEND, h])
        wait_bytes(t_send.at[h, others_a], sem.at[RA_SEND, h])
        wait_bytes(x_back.at[h, pl.ds(0, tokens - rows)], sem.at[RX_SEND, h])
        wait_bytes(x_back.at[h, pl.ds(0, rows)], sem.at[RX_OWN, h])

        @pl.when(core != h % 2)
        def _():
            wait_bytes(b_send.at[h, :, pl.ds(0, b_rows)], sem.at[B_NEAR, h])

    @pl.loop(0, mine)
    def _(k):
        wait_bytes(work.at[(k, *two_sides)], sem.at[H_SEND, k])
        wait_bytes(o_send.at[k, :, pl.ds(0, (line - 1) * b_rows)], sem.at[RB_SEND, k])

    for par in range(CORES):
        wait_bytes(l_a_send.at[label_others], label_sem.at[0, par])
        wait_bytes(l_b_send.at[par, label_others], label_sem.at[2, par])

        @pl.when(core != par)
        def _():
            wait_bytes(l_b_send.at[par, pl.ds(0, line)], label_sem.at[3, par])

        @pl.when(tok != keepers[par])
        def _():
            wait_bytes(mask_tile, mask_sem.at[par])

    wait_bytes(labels.at[pl.ds(0, 2)], label_sem.at[5, 0])


def per_device(queries, key_rows, values, cluster, owners, pair_list):
    nx, n_tok = lax.axis_size("head"), lax.axis_size("tok")
    n_axis = math.isqrt(n_tok // CORES)
    cl_dev = pair_list.shape[0]
    per_pair = CAP * cl_dev // n_tok
    rows, features = queries.shape
    heads = features // nx // HEAD_DIM
    tokens = rows * nx
    slots, line = n_tok * per_pair, n_axis * CORES
    mine, sides, half = heads // CORES, CORES + 2, slots // CORES
    wide, thin = 3 * HEAD_DIM, HEAD_DIM
    lane_step = min(slots, HEAD_DIM)

    def vmem(*shape, dtype=BF16):
        return pltpu.VMEM(shape, dtype)

    return pl.pallas_call(
        functools.partial(kernel, (nx, n_axis, per_pair, heads)),
        out_shape=jax.ShapeDtypeStruct((rows, features), BF16),
        in_specs=[pl.BlockSpec(memory_space=pltpu.HBM)] * 3
        + [pl.BlockSpec(memory_space=pltpu.VMEM)] * 3,
        out_specs=pl.BlockSpec(memory_space=pltpu.HBM),
        scratch_shapes=[
            vmem(heads, tokens, wide),
            vmem(heads, slots, wide),
            vmem(heads, slots, wide),
            vmem(heads, CORES, half, wide),
            vmem(mine, sides, slots, wide),
            vmem(mine, CORES, slots, thin),
            vmem(heads, CORES, half, thin),
            vmem(heads, slots, thin),
            vmem(heads, slots, thin),
            vmem(heads, tokens, thin),
            vmem(slots, tokens),
            vmem(tokens, slots),
            vmem(CORES, half, slots),
            vmem(slots, slots),
            vmem(CORES, 3, slots, slots, dtype=F32),
            vmem(CORES, slots, lane_step, dtype=F32),
            vmem(slots, lane_step, dtype=F32),
            vmem(slots, thin, dtype=F32),
            vmem(n_tok, thin),
            vmem(CORES, n_tok, thin),
            vmem(CORES, n_tok, thin),
            vmem(line * line, thin),
            vmem(sides, n_tok, thin),
            vmem(TILE, thin),
            vmem(CORES, TILE, thin),
            vmem(CORES, slots, thin),
            vmem(sides, slots, thin),
            pltpu.SemaphoreType.DMA((STAGES, heads)),
            pltpu.SemaphoreType.DMA((6, 2)),
            pltpu.SemaphoreType.DMA((2 * CORES,)),
            pltpu.SemaphoreType.DMA,
        ],
        compiler_params=pltpu.CompilerParams(
            collective_id=0, has_side_effects=True, vmem_limit_bytes=int(53.3 * 2**20)
        ),
    )(queries, key_rows, values, cluster[None, :], owners[None, :], pair_list)


def solution(mesh):
    return jax.shard_map(
        per_device,
        mesh=mesh,
        in_specs=(
            P(("tok", "head"), None),
            P(("tok", "head"), None),
            P(("tok", "head"), None),
            P("tok"),
            P(),
            P("tok", None),
        ),
        out_specs=P(("tok", "head"), None),
        check_vma=False,
    )
```

```python
import functools
import math

import jax
import jax.numpy as jnp
from jax import lax
from jax.experimental import pallas as pl
from jax.experimental.pallas import tpu as pltpu
from jax.sharding import PartitionSpec as P

HEAD_DIM = 128
CAP = 128
CORES = 2
TILE = 16
LANES = 8
AHEAD = 2
STEP = 1
MASKED = -(2.0**100)
SCALE_LOG2 = math.log2(math.e) / math.sqrt(HEAD_DIM)
MESH = pl.DeviceIdType.MESH
F32 = jnp.float32
BF16 = jnp.bfloat16

X_OWN, X_SEND, X_RECV, A_SEND, A_RECV, B_SEND, B_NEAR, B_RECV, H_SEND, H_RECV = range(10)
RB_SEND, RB_RECV, RA_SEND, RA_RECV, RX_SEND, RX_OWN = range(10, 16)
STAGES = 16


def matmul(left, right):
    return jnp.dot(left, right, preferred_element_type=F32)


def matmul_t(left, right):
    return lax.dot_general(left, right, (((1,), (1,)), ((), ())), preferred_element_type=F32)


def iota(shape, dim):
    return lax.broadcasted_iota(jnp.int32, shape, dim)


def one_hot(condition):
    return jnp.where(condition, 1.0, 0.0).astype(BF16)


def wait_bytes(ref, sem):
    pltpu.make_async_copy(ref, ref, sem).wait()


def kernel(
    dims, q_ref, k_ref, v_ref, cluster, owners, pair_list, out_ref,
    x_recv, a_send, a_recv, b_send, work, o_send, o_recv, t_send, t_recv, x_back,
    pick, pick_t, perm, perm_t, scores, peak, total, mixed,
    l_a_send, l_a_recv, l_b_send, l_b_recv, labels, mask_tile, mask_in, q_mask, k_mask,
    sem, label_sem, mask_sem, out_sem,
):
    nx, n_axis, per_pair, heads = dims
    rows = q_ref.shape[0]
    tokens = nx * rows
    width = heads * HEAD_DIM
    line = n_axis * CORES
    n_tok = n_axis * line
    slots = n_tok * per_pair
    a_rows = line * per_pair
    b_rows = n_axis * per_pair
    mine = heads // CORES
    sides = CORES + 2
    cl_dev, pairs = pair_list.shape
    invalid = sides * cl_dev
    my_x = lax.axis_index("head")
    tok = lax.axis_index("tok")
    z, y, core = tok // line, (tok // CORES) % n_axis, tok % CORES

    def place(par):
        return z + par * (y - z), y + par * (z - y)

    def device(a, b, c, par):
        return ((a + par * (b - a)) * line + (b + par * (a - b)) * CORES + c, my_x)

    def next_chip(step):
        a, b = place(core)
        chip = lax.rem(a * n_axis + b + n_axis * n_axis + step, n_axis * n_axis)
        return device(chip // n_axis, chip % n_axis, core, core)

    def copy_to(src, dst, send, recv, target):
        pltpu.make_async_remote_copy(
            src_ref=src, dst_ref=dst, send_sem=send, recv_sem=recv,
            device_id=target, device_id_type=MESH,
        ).start()

    def lanes(start, size):
        return pl.ds(pl.multiple_of(start, HEAD_DIM), size)

    def block(index, size):
        return pl.ds(pl.multiple_of(index * size, size), size)

    barrier = pltpu.get_barrier_semaphore()

    def greet(target):
        pl.semaphore_signal(barrier, inc=1, device_id=target, device_id_type=MESH)

    @pl.loop(1, nx)
    def _(d):
        greet((tok, lax.rem(my_x + d, nx)))

    @pl.loop(1, line)
    def _(d):
        greet((z * line + lax.rem(y * CORES + core + d, line), my_x))

    @pl.loop(1, n_axis)
    def _(d):
        for c in range(CORES):
            greet(((lax.rem(z + d, n_axis) * n_axis + y) * CORES + c, my_x))

    greet(next_chip(1))
    greet(next_chip(-1))
    @pl.when(y != z)
    def _():
        for c in range(CORES):
            greet(((y * n_axis + z) * CORES + c, my_x))

    @pl.when(y == z)
    def _():
        for c in range(CORES):
            greet((tok + 1 - 2 * core, my_x))

    greeted = (nx - 1) + (line - 1) + (n_axis - 1) * CORES + 2 + CORES

    def own_copy(ref, kind, h):
        return pltpu.make_async_copy(
            ref.at[:, lanes(my_x * width + h * HEAD_DIM, HEAD_DIM)],
            x_recv.at[h, block(my_x, rows), pl.ds(kind * HEAD_DIM, HEAD_DIM)],
            sem.at[X_OWN, h],
        )

    pl.semaphore_wait(barrier, greeted)

    def spread(h):
        @pl.loop(1, nx)
        def _(d):
            other = lax.rem(my_x + d, nx)
            for kind, ref in enumerate((q_ref, k_ref, v_ref)):
                copy_to(
                    ref.at[:, lanes(other * width + h * HEAD_DIM, HEAD_DIM)],
                    x_recv.at[h, block(my_x, rows), pl.ds(kind * HEAD_DIM, HEAD_DIM)],
                    sem.at[X_SEND, h],
                    sem.at[X_RECV, h],
                    (tok, other),
                )

    @pl.loop(0, min(AHEAD, heads))
    def _(h):
        spread(h)

    @pl.loop(0, heads)
    def _(h):
        for kind, ref in enumerate((q_ref, k_ref, v_ref)):
            own_copy(ref, kind, h).start()

    pair_local = pair_list[...] - (tok - core - 1) * cl_dev
    lane = iota((cl_dev, HEAD_DIM), 1)
    allowed = lane > invalid
    for j in range(pairs):
        allowed = allowed | (pair_local[:, j : j + 1] == lane)
    mask_tile[...] = jnp.concatenate(
        [jnp.where(allowed, 0.0, MASKED), jnp.zeros((TILE - cl_dev, HEAD_DIM), F32)], axis=0
    ).astype(BF16)

    keepers = [(z * n_axis + y) * CORES, (y * n_axis + z) * CORES + 1]
    for end, keeper in enumerate(keepers):

        @pl.when(tok == keeper)
        def _():
            pltpu.make_async_copy(
                mask_tile, mask_in.at[core], mask_sem.at[CORES + core]
            ).start()

        @pl.when(tok != keeper)
        def _():
            copy_to(
                mask_tile, mask_in.at[core], mask_sem.at[end], mask_sem.at[CORES + core],
                (keeper, my_x),
            )

    clusters = owners.shape[1]
    cluster_hot = one_hot(iota((clusters, tokens), 0) == cluster[...])
    table = jnp.where(
        iota((TILE, clusters), 0) == 0, owners[...] // cl_dev, owners[...] % cl_dev
    )
    found = matmul(table.astype(F32).astype(BF16), cluster_hot).astype(jnp.int32)
    target, local_id = found[0:1], found[1:2]
    target_hot = one_hot(iota((n_tok, tokens), 0) == target)
    earlier = one_hot(iota((tokens, tokens), 0) < iota((tokens, tokens), 1))
    rank = jnp.sum(matmul(target_hot, earlier) * target_hot.astype(F32), axis=0, keepdims=True)
    rank = rank.astype(jnp.int32)
    send_row = target * per_pair + rank
    chunk = min(128, tokens)

    @pl.loop(0, slots // chunk)
    def _(i):
        pick[block(i, chunk)] = one_hot(iota((chunk, tokens), 0) + i * chunk == send_row)

    lane = iota((HEAD_DIM, tokens), 0) - rank * LANES
    filled = matmul_t(target_hot, one_hot((lane == local_id) | (lane == cl_dev)))
    lane = iota((n_tok, HEAD_DIM), 1)
    l_a_send[...] = jnp.where(lane % LANES == cl_dev, 1.0 - filled, filled).astype(BF16)

    def first_hop(src, dst, send, recv, par, size):
        a, b = place(par)
        pltpu.make_async_copy(src.at[block(a, size)], dst.at[block(a, size)], recv).start()

        @pl.loop(1, n_axis)
        def _(d):
            other = lax.rem(a + d, n_axis)
            copy_to(
                src.at[block(other, size)], dst.at[block(a, size)], send, recv,
                device(other, b, core, par),
            )

    def second_hop(src_at, dst, send, near, recv, par):
        a, b = place(par)

        @pl.when(core == par)
        def _():
            pltpu.make_async_copy(src_at(b), dst, recv).start()

        @pl.when(core != par)
        def _():
            copy_to(src_at(b), dst, near, recv, device(a, b, par, par))

        @pl.loop(1, n_axis)
        def _(d):
            other = lax.rem(b + d, n_axis)
            copy_to(src_at(other), dst, send, recv, device(a, other, par, par))

    def source(par):
        _, b = place(par)
        return b * CORES + core

    others_a = pl.ds(0, slots - a_rows)
    others_b = pl.ds(0, b_rows * (n_axis - 1))
    label_others = pl.ds(0, n_tok - line)

    for par in range(CORES):
        first_hop(
            l_a_send, l_a_recv.at[par], label_sem.at[0, par], label_sem.at[1, par], par, line
        )

    def pack(h):
        for kind, ref in enumerate((q_ref, k_ref, v_ref)):
            own_copy(ref, kind, h).wait()
        wait_bytes(x_recv.at[h, pl.ds(0, tokens - rows)], sem.at[X_RECV, h])

        @pl.when(h + AHEAD < heads)
        def _():
            spread(h + AHEAD)

        @pl.loop(0, 2)
        def _(i):
            part = block(i, slots // 2)
            a_send[h, part] = matmul(pick[part], x_recv[h]).astype(BF16)

        first_hop(a_send.at[h], a_recv.at[h], sem.at[A_SEND, h], sem.at[A_RECV, h], h % 2, a_rows)

    def turn(h):
        par = h % 2
        wait_bytes(a_recv.at[h], sem.at[A_RECV, h])

        @pl.loop(0, CORES)
        def _(i):
            b_send[h, i] = matmul(perm[i], a_recv[h]).astype(BF16)

        second_hop(
            lambda other: b_send.at[h, :, block(other, b_rows)],
            work.at[h // 2, pl.ds(1, CORES), block(source(par), b_rows)],
            sem.at[B_SEND, h], sem.at[B_NEAR, h], sem.at[B_RECV, h // 2], par,
        )

    def share(k):
        wait_bytes(work.at[k, pl.ds(1, CORES)], sem.at[B_RECV, k])
        for step, src, dst in ((-1, 1, CORES + 1), (1, CORES, 0)):
            copy_to(
                work.at[k, src, :, pl.ds(HEAD_DIM, 2 * HEAD_DIM)],
                work.at[k, dst, :, pl.ds(HEAD_DIM, 2 * HEAD_DIM)],
                sem.at[H_SEND, k], sem.at[H_RECV, k], next_chip(step),
            )

    two_sides = (pl.ds(0, 2), slice(None), pl.ds(HEAD_DIM, 2 * HEAD_DIM))
    tiles = slots // HEAD_DIM if slots >= HEAD_DIM else 1
    lane_step = min(slots, HEAD_DIM)

    def attend(k):
        peak[...] = jnp.full((CORES, slots, lane_step), -jnp.inf, F32)

        @pl.loop(0, 3 * CORES)
        def _(n):
            i = (n // 2) % 2 + n // 5
            part = 1 - i + n % 2 + (n // 4) * (2 * i - 1)

            @pl.when(n == 4)
            def _():
                wait_bytes(work.at[(k, *two_sides)], sem.at[H_RECV, k])

            query = jnp.concatenate([work[k, i + 1, :, 0:HEAD_DIM], q_mask[i]], axis=1)
            key = jnp.concatenate(
                [work[k, i + part, :, HEAD_DIM : 2 * HEAD_DIM], k_mask[i + part]], axis=1
            )
            found = matmul_t(query, key)
            scores[i, part] = found
            peak[i] = functools.reduce(
                jnp.maximum,
                [found[:, t * lane_step : (t + 1) * lane_step] for t in range(tiles)],
                peak[i],
            )

        @pl.loop(0, CORES)
        def _(i):
            row_max = jnp.max(peak[i], axis=1, keepdims=True)
            peak[i] = jnp.broadcast_to(row_max, (slots, lane_step))
            total[...] = jnp.zeros((slots, lane_step), F32)
            mixed[...] = jnp.zeros((slots, HEAD_DIM), F32)

            @pl.loop(0, 3)
            def _(part):
                row_max = peak[i]
                weights = [
                    jnp.exp2(
                        (scores[i, part, :, t * lane_step : (t + 1) * lane_step] - row_max)
                        * SCALE_LOG2
                    )
                    for t in range(tiles)
                ]
                total[...] += functools.reduce(jnp.add, weights)
                rounded = jnp.concatenate([w.astype(BF16) for w in weights], axis=1)
                mixed[...] += matmul(rounded, work[k, i + part, :, 2 * HEAD_DIM : 3 * HEAD_DIM])

            row_total = jnp.sum(total[...], axis=1, keepdims=True)
            o_send[k, i] = (mixed[...] / row_total).astype(BF16)

        h = CORES * k + core
        a, b = place(core)
        here = b * CORES + core
        dst = o_recv.at[h, :, block(b, b_rows)]

        def src(other):
            return o_send.at[k, :, block(other, b_rows)]

        pltpu.make_async_copy(src(here), dst, sem.at[RB_RECV, h]).start()

        @pl.loop(1, line)
        def _(d):
            other = lax.rem(here + d, line)
            copy_to(
                src(other), dst, sem.at[RB_SEND, k], sem.at[RB_RECV, h],
                device(a, other // CORES, other % CORES, core),
            )

    def turn_back(h):
        wait_bytes(o_recv.at[h], sem.at[RB_RECV, h])

        @pl.loop(0, 2)
        def _(i):
            part = block(i, slots // 2)
            returned = o_recv[h].reshape(slots, HEAD_DIM)
            t_send[h, part] = matmul(perm_t[part], returned).astype(BF16)

        first_hop(
            t_send.at[h], t_recv.at[h], sem.at[RA_SEND, h], sem.at[RA_RECV, h], h % 2, a_rows
        )

    def finish(h):
        wait_bytes(t_recv.at[h], sem.at[RA_RECV, h])
        x_back[h] = matmul(pick_t[...], t_recv[h]).astype(BF16)
        column = lanes(my_x * width + h * HEAD_DIM, HEAD_DIM)
        pltpu.make_async_copy(
            x_back.at[h, block(my_x, rows)], out_ref.at[:, column], sem.at[RX_OWN, h]
        ).start()

        @pl.loop(1, nx)
        def _(d):
            other = lax.rem(my_x + d, nx)
            copy_to(
                x_back.at[h, block(other, rows)], out_ref.at[:, column],
                sem.at[RX_SEND, h], out_sem, (tok, other),
            )

    def make_perms():
        half = slots // CORES

        def source_of(row, i):
            r, a, b = row % per_pair, (row // per_pair) % n_axis, row // b_rows
            return a * a_rows + b * (CORES * per_pair) + i * per_pair + r

        piece = min(chunk, half)

        @pl.loop(0, slots // piece)
        def _(part):
            row, column = iota((piece, slots), 0) + part * piece, iota((piece, slots), 1)
            i, start = part * piece // half, part * piece % half
            rows_here = pl.ds(pl.multiple_of(start, piece), piece)
            perm[i, rows_here] = one_hot(source_of(row % half, i) == column)
            perm_t[block(part, piece)] = one_hot(
                source_of(column % half, column // half) == row
            )

        same = one_hot(iota((tokens, tokens), 0) == iota((tokens, tokens), 1))
        pick_t[...] = matmul_t(same, pick[...]).astype(BF16)

    def turn_labels():
        row, column = iota((n_tok, n_tok), 0), iota((n_tok, n_tok), 1)
        start = (row // CORES) % n_axis * line + row // line * CORES + row % CORES
        turned = one_hot(start == column)
        for par in range(CORES):
            wait_bytes(l_a_recv.at[par], label_sem.at[1, par])
            l_b_send[par] = matmul(turned, l_a_recv[par]).astype(BF16)
            second_hop(
                lambda other: l_b_send.at[par, block(other, line)],
                l_b_recv.at[block(source(par), line)],
                label_sem.at[2, par], label_sem.at[3, par], label_sem.at[4, 0], par,
            )

    def share_labels():
        wait_bytes(l_b_recv, label_sem.at[4, 0])
        shape = (n_tok, line * line)
        row, column = iota(shape, 0), iota(shape, 1)
        start = row // n_axis * line + row % n_axis * CORES
        for i in range(CORES):
            labels[i + 1] = matmul(one_hot(start + i == column), l_b_recv[...]).astype(BF16)
        for step, src, dst in ((-1, 1, CORES + 1), (1, CORES, 0)):
            copy_to(
                labels.at[src], labels.at[dst], label_sem.at[5, 0], label_sem.at[5, 1],
                next_chip(step),
            )

    def make_masks():
        wait_bytes(labels.at[pl.ds(0, 2)], label_sem.at[5, 1])
        for c in range(CORES):
            wait_bytes(mask_in.at[c], mask_sem.at[CORES + c])
        row, column = iota((HEAD_DIM, HEAD_DIM), 0), iota((HEAD_DIM, HEAD_DIM), 1)
        fold = one_hot((row % LANES == column) & (row < per_pair * LANES))
        rest = jnp.zeros((HEAD_DIM - TILE, HEAD_DIM), BF16)
        piece = min(chunk, slots)

        @pl.loop(0, sides * (slots // piece))
        def _(n):
            side, start = n // (slots // piece), n % (slots // piece) * piece
            here = pl.ds(pl.multiple_of(start, piece), piece)
            owner = (iota((piece, n_tok), 0) + start) // per_pair
            owner_row = one_hot(owner == iota((piece, n_tok), 1))
            shape = (piece, HEAD_DIM)
            own_lanes = iota(shape, 1) // LANES == iota(shape, 0) % per_pair
            spaced = jnp.where(own_lanes, matmul(owner_row, labels[side]), 0.0).astype(BF16)
            label = matmul(spaced, fold).astype(BF16)
            shift = one_hot(
                ((row < cl_dev) & (column == row + cl_dev * side))
                | ((row == cl_dev) & (column == invalid))
            )
            k_mask[side, here] = matmul(label, shift).astype(BF16)

            @pl.when((side >= 1) & (side <= CORES))
            def _():
                mask = jnp.concatenate([mask_in[side - 1], rest], axis=0)
                q_mask[side - 1, here] = matmul(label, mask).astype(BF16)

    def both(stage):
        def pair(k):
            @pl.loop(CORES * k, CORES * k + CORES)
            def _(h):
                stage(h)

        return pair

    stages = (both(pack), both(turn), share, attend, both(turn_back), both(finish))

    @pl.loop(0, mine + STEP * (len(stages) - 1))
    def _(step):
        for number, stage in enumerate(stages):
            lag = STEP * number

            @pl.when((step >= lag) & (step < mine + lag))
            def _():
                stage(step - lag)

            if number == 0:

                @pl.when(step == 0)
                def _():
                    make_perms()
                    turn_labels()

        @pl.when(step == 1)
        def _():
            share_labels()

        @pl.when(step == 2)
        def _():
            make_masks()

    wait_bytes(out_ref.at[:, pl.ds(0, (nx - 1) * width)], out_sem)

    @pl.loop(0, heads)
    def _(h):
        wait_bytes(x_recv.at[h, pl.ds(0, tokens - rows)], sem.at[X_SEND, h])
        wait_bytes(a_send.at[h, others_a], sem.at[A_SEND, h])
        wait_bytes(b_send.at[h, :, others_b], sem.at[B_SEND, h])
        wait_bytes(t_send.at[h, others_a], sem.at[RA_SEND, h])
        wait_bytes(x_back.at[h, pl.ds(0, tokens - rows)], sem.at[RX_SEND, h])
        wait_bytes(x_back.at[h, pl.ds(0, rows)], sem.at[RX_OWN, h])

        @pl.when(core != h % 2)
        def _():
            wait_bytes(b_send.at[h, :, pl.ds(0, b_rows)], sem.at[B_NEAR, h])

    @pl.loop(0, mine)
    def _(k):
        wait_bytes(work.at[(k, *two_sides)], sem.at[H_SEND, k])
        wait_bytes(o_send.at[k, :, pl.ds(0, (line - 1) * b_rows)], sem.at[RB_SEND, k])

    for par in range(CORES):
        wait_bytes(l_a_send.at[label_others], label_sem.at[0, par])
        wait_bytes(l_b_send.at[par, label_others], label_sem.at[2, par])

        @pl.when(core != par)
        def _():
            wait_bytes(l_b_send.at[par, pl.ds(0, line)], label_sem.at[3, par])

        @pl.when(tok != keepers[par])
        def _():
            wait_bytes(mask_tile, mask_sem.at[par])

    wait_bytes(labels.at[pl.ds(0, 2)], label_sem.at[5, 0])


def per_device(queries, key_rows, values, cluster, owners, pair_list):
    nx, n_tok = lax.axis_size("head"), lax.axis_size("tok")
    n_axis = math.isqrt(n_tok // CORES)
    cl_dev = pair_list.shape[0]
    per_pair = CAP * cl_dev // n_tok
    rows, features = queries.shape
    heads = features // nx // HEAD_DIM
    tokens = rows * nx
    slots, line = n_tok * per_pair, n_axis * CORES
    mine, sides, half = heads // CORES, CORES + 2, slots // CORES
    wide, thin = 3 * HEAD_DIM, HEAD_DIM
    lane_step = min(slots, HEAD_DIM)

    def vmem(*shape, dtype=BF16):
        return pltpu.VMEM(shape, dtype)

    return pl.pallas_call(
        functools.partial(kernel, (nx, n_axis, per_pair, heads)),
        out_shape=jax.ShapeDtypeStruct((rows, features), BF16),
        in_specs=[pl.BlockSpec(memory_space=pltpu.HBM)] * 3
        + [pl.BlockSpec(memory_space=pltpu.VMEM)] * 3,
        out_specs=pl.BlockSpec(memory_space=pltpu.HBM),
        scratch_shapes=[
            vmem(heads, tokens, wide),
            vmem(heads, slots, wide),
            vmem(heads, slots, wide),
            vmem(heads, CORES, half, wide),
            vmem(mine, sides, slots, wide),
            vmem(mine, CORES, slots, thin),
            vmem(heads, CORES, half, thin),
            vmem(heads, slots, thin),
            vmem(heads, slots, thin),
            vmem(heads, tokens, thin),
            vmem(slots, tokens),
            vmem(tokens, slots),
            vmem(CORES, half, slots),
            vmem(slots, slots),
            vmem(CORES, 3, slots, slots, dtype=F32),
            vmem(CORES, slots, lane_step, dtype=F32),
            vmem(slots, lane_step, dtype=F32),
            vmem(slots, thin, dtype=F32),
            vmem(n_tok, thin),
            vmem(CORES, n_tok, thin),
            vmem(CORES, n_tok, thin),
            vmem(line * line, thin),
            vmem(sides, n_tok, thin),
            vmem(TILE, thin),
            vmem(CORES, TILE, thin),
            vmem(CORES, slots, thin),
            vmem(sides, slots, thin),
            pltpu.SemaphoreType.DMA((STAGES, heads)),
            pltpu.SemaphoreType.DMA((6, 2)),
            pltpu.SemaphoreType.DMA((2 * CORES,)),
            pltpu.SemaphoreType.DMA,
        ],
        compiler_params=pltpu.CompilerParams(
            collective_id=0, has_side_effects=True, vmem_limit_bytes=60 * 2**20
        ),
    )(queries, key_rows, values, cluster[None, :], owners[None, :], pair_list)


def solution(mesh):
    return jax.shard_map(
        per_device,
        mesh=mesh,
        in_specs=(
            P(("tok", "head"), None),
            P(("tok", "head"), None),
            P(("tok", "head"), None),
            P("tok"),
            P(),
            P("tok", None),
        ),
        out_specs=P(("tok", "head"), None),
        check_vma=False,
    )
```
